128 devices in a mesh: gx: 8 (over z_hi, x), gy: 16 (over y, z_lo, core).
Axes of the slice: x: 4, y: 4, z: 4 (z_hi: 2, z_lo: 2; z = z_hi * 2 + z_lo), core: 2. Of those that a mesh axis runs over, the one named last changes fastest.
Arguments:
- orbitals: bfloat16 [8, 16, 2, 64, 4096], P('gx', 'gy'), may hold values from -6 to 6
- anchors: int32 [256, 3], replicated, may hold values from 0 to 727, as said below
- pair_list: int32 [8, 16, 12, 2], P('gx', 'gy'), may hold values from 0 to 255, as said below
- pair_count: int32 [8, 16], P('gx', 'gy'), may hold values from 1 to 12, as said below
- core_density: float32 [384, 768, 128], P('gx', 'gy'), may hold values from 0.05 to 2
Outputs:
- action: float32 [8, 16, 2, 64, 4096], P('gx', 'gy')
- potential: float32 [384, 768, 128], P('gx', 'gy')
The draws below stay inside these ranges and needn't reach their ends.
Inputs may be any that keep to these rules, and one draw needn't show every extreme that they name: Orbital n = (a 16 + b) * 2 + k is held by device (a, b) of (gx, gy); anchors[n] has its first coordinate in a 48 to a 55, its second in b * 48 to b * 48 + 7, its third in 0 to 64. `pair_list`: every slot of device (a, b) names two different orbitals: the first held by (a, b), the second by (a + s, b + t) with s and t in -1, 0, 1, taken modulo 8 and 16. `pair_count`: some device has 12 live slots.
All inputs are finite; a program needn't handle non-finite values.
Results may differ from the reference program's by a relative error of at most 0.0012.
Values may be sent and summed in bfloat16 or wider, within the bound.
A program may use at most 128 MiB of HBM per device.

```python
import math
import jax
import jax.numpy as jnp
from jax import lax

B = 64
ORB = 2
PSLOT = 12
SWEEPS = 4
GZ = 128
C = 48
OFF = 8
GX = 384
GY = 768
NORB = 256
N_GX = 8
N_GY = 16


def draw_anchors(key, part):
    orbit_ids = jnp.arange(NORB, dtype=jnp.int32)
    holder = orbit_ids // ORB
    offset_x = jax.random.randint(jax.random.fold_in(key, 11), (NORB,), 0, OFF, dtype=jnp.int32)
    offset_y = jax.random.randint(jax.random.fold_in(key, 12), (NORB,), 0, OFF, dtype=jnp.int32)
    grid_depth = jax.random.randint(jax.random.fold_in(key, 13), (NORB,), 0, GZ - B + 1, dtype=jnp.int32)
    return jnp.stack([holder // N_GY * C + offset_x, holder % N_GY * C + offset_y, grid_depth], axis=1)


def draw_pair_list(key, part):
    shape_all = (N_GX, N_GY, PSLOT)
    first_slot = jax.random.randint(jax.random.fold_in(key, 21), shape_all, 0, ORB, dtype=jnp.int32)
    second_slot = jax.random.randint(jax.random.fold_in(key, 22), shape_all, 0, ORB, dtype=jnp.int32)
    step_x = jax.random.randint(jax.random.fold_in(key, 23), shape_all, -1, 2, dtype=jnp.int32)
    step_y = jax.random.randint(jax.random.fold_in(key, 24), shape_all, -1, 2, dtype=jnp.int32)
    same_box = (step_x == 0) & (step_y == 0) & (second_slot == first_slot)
    second_slot = jnp.where(same_box, (first_slot + 1) % ORB, second_slot)
    holder_x = lax.broadcasted_iota(jnp.int32, shape_all, 0)
    holder_y = lax.broadcasted_iota(jnp.int32, shape_all, 1)
    first_orbit = (holder_x * N_GY + holder_y) * ORB + first_slot
    second_orbit = ((holder_x + step_x) % N_GX * N_GY + (holder_y + step_y) % N_GY) * ORB + second_slot
    return jnp.stack([first_orbit, second_orbit], axis=-1)


def draw_pair_count(key, part):
    base_count = jax.random.randint(jax.random.fold_in(key, 31), (N_GX, N_GY), 1, PSLOT // 2 + 1, dtype=jnp.int32)
    busiest = jax.random.randint(jax.random.fold_in(key, 32), (), 0, N_GX * N_GY, dtype=jnp.int32)
    flat_index = lax.broadcasted_iota(jnp.int32, (N_GX, N_GY), 0) * N_GY + lax.broadcasted_iota(jnp.int32, (N_GX, N_GY), 1)
    return jnp.where(flat_index == busiest, PSLOT, base_count)


def block_scale(rng, extent, cuts, low, high):
    level = 1.0
    for position, parts in cuts:
        steps = jax.random.uniform(jax.random.fold_in(jax.random.fold_in(rng, 6), position), (parts,), jnp.float32, low / len(cuts), high / len(cuts))
        level = level * jnp.repeat(jnp.exp(steps), extent[position] // parts).reshape((-1,) + (1,) * (len(extent) - 1 - position))
    return level


def scatter_about(own_key, shape, scale, bound, pieces=(), held_as=jnp.bfloat16):
    loudness = block_scale(own_key, shape, pieces, -0.22, 0.18) if pieces else 1.0
    entries = jax.random.normal(own_key, shape, jnp.float32) * scale * loudness
    return jnp.minimum(jnp.maximum(entries, -bound), bound).astype(held_as)


def setup_inputs(seed: int = 0) -> dict:
    seeds = jax.random.split(jax.random.key(seed), 6)
    return {
        "orbitals": scatter_about(seeds[0], (N_GX, N_GY, ORB, B, B * B), 1.0, 6.0, ((0, 8), (1, 16))),
        "anchors": draw_anchors(jax.random.fold_in(seeds[5], 71), 0),
        "pair_list": draw_pair_list(jax.random.fold_in(seeds[5], 71), 0),
        "pair_count": draw_pair_count(jax.random.fold_in(seeds[5], 71), 0),
        "core_density": jnp.clip(jnp.exp(math.log(2.0) - 3.6888794 * jax.random.uniform(seeds[4], (GX, GY, GZ), jnp.float32) ** block_scale(seeds[4], (GX, GY, GZ), ((0, 8), (1, 16)), -0.2, 0.2)), 0.05, 2.0),
    }


screen_mass = 0.25
coupling = 2.0 * math.pi
exx_share = 0.25
xc_factor = (3.0 / math.pi) ** (1.0 / 3.0)


def sweep_weights(sweep_count):
    return [1.0 / (1.0 + 0.7 * math.cos(math.pi * (2 * order + 1) / (2 * sweep_count))) for order in range(sweep_count)]


def column_parts(box_side):
    column_index = lax.broadcasted_iota(jnp.int32, (1, box_side * box_side), 1)
    return column_index // box_side, column_index % box_side


def neighbour_sum(values):
    box_side = values.shape[0]
    depth_index = column_parts(box_side)[1]
    zero_row = jnp.zeros((1, values.shape[1]), values.dtype)
    summed = jnp.concatenate([values[1:], zero_row], 0) + jnp.concatenate([zero_row, values[:-1]], 0)
    zero_band = jnp.zeros((box_side, box_side), values.dtype)
    summed = summed + jnp.concatenate([values[:, box_side:], zero_band], 1) + jnp.concatenate([zero_band, values[:, :-box_side]], 1)
    zero_cell = jnp.zeros((box_side, 1), values.dtype)
    upward = jnp.concatenate([values[:, 1:], zero_cell], 1)
    downward = jnp.concatenate([zero_cell, values[:, :-1]], 1)
    summed = summed + jnp.where(depth_index < box_side - 1, upward, 0.0) + jnp.where(depth_index > 0, downward, 0.0)
    return summed


def screened_solve(source):
    diagonal = 6.0 + screen_mass
    solved = jnp.zeros_like(source)
    for weight in sweep_weights(SWEEPS):
        residual = source - (diagonal * solved - neighbour_sum(solved))
        solved = solved + (weight / diagonal) * residual
    return solved


def move_box(values, shift_x, shift_y, shift_z):
    box_side = values.shape[0]
    row_index = lax.broadcasted_iota(jnp.int32, (box_side, 1), 0)
    across, depth_index = column_parts(box_side)
    rolled = jnp.roll(values, shift_x, axis=0)
    rolled = jnp.roll(rolled, shift_y * box_side + shift_z, axis=1)
    inside = (row_index >= shift_x) & (row_index < box_side + shift_x)
    inside = inside & (across >= shift_y) & (across < box_side + shift_y)
    inside = inside & (depth_index >= shift_z) & (depth_index < box_side + shift_z)
    return jnp.where(inside, rolled, 0.0)


def relative(first_anchor, second_anchor, span_x, span_y):
    delta = second_anchor - first_anchor
    delta_x = (delta[0] + span_x // 2) % span_x - span_x // 2
    delta_y = (delta[1] + span_y // 2) % span_y - span_y // 2
    return delta_x, delta_y, delta[2]


def box_indices(anchor, box_side, span_x, span_y):
    steps_along = jnp.arange(box_side, dtype=jnp.int32)
    index_x = (anchor[0] + steps_along) % span_x
    index_y = (anchor[1] + steps_along) % span_y
    index_z = anchor[2] + steps_along
    return index_x[:, None, None], index_y[None, :, None], index_z[None, None, :]


def reference(orbitals, anchors, pair_list, pair_count, core_density):
    box_side = orbitals.shape[3]
    flat_side = box_side * box_side
    box_list = orbitals.reshape(NORB, box_side, flat_side)
    span_x = core_density.shape[0]
    span_y = core_density.shape[1]
    pair_rows = pair_list.reshape(N_GX * N_GY * PSLOT, 2)
    slot_index = lax.broadcasted_iota(jnp.int32, (N_GX * N_GY, PSLOT), 1)
    live_flag = (slot_index < pair_count.reshape(N_GX * N_GY, 1)).reshape(N_GX * N_GY * PSLOT)

    def pair_step(exchange, carried):
        pair_ids, live_one = carried
        first_box = box_list[pair_ids[0]].astype(jnp.float32)
        second_box = box_list[pair_ids[1]].astype(jnp.float32)
        delta_x, delta_y, delta_z = relative(anchors[pair_ids[0]], anchors[pair_ids[1]], span_x, span_y)
        moved = move_box(second_box, delta_x, delta_y, delta_z)
        solved = screened_solve(coupling * first_box * moved)
        weight_live = jnp.where(live_one, 1.0, 0.0).astype(jnp.float32)
        exchange = exchange.at[pair_ids[0]].add(weight_live * (solved * moved))
        exchange = exchange.at[pair_ids[1]].add(weight_live * move_box(solved * first_box, -delta_x, -delta_y, -delta_z))
        return exchange, None

    exchange, _ = lax.scan(pair_step, jnp.zeros((NORB, box_side, flat_side), jnp.float32), (pair_rows, live_flag))

    def deposit(grid_sum, carried):
        orbital_box, anchor = carried
        squared = jnp.square(orbital_box.astype(jnp.float32)).reshape(box_side, box_side, box_side)
        index_x, index_y, index_z = box_indices(anchor, box_side, span_x, span_y)
        return grid_sum.at[index_x, index_y, index_z].add(squared), None

    density, _ = lax.scan(deposit, jnp.zeros(core_density.shape, jnp.float32), (box_list, anchors))
    potential = -xc_factor * jnp.cbrt(density + core_density)

    def apply_box(carried):
        orbital_box, anchor, exchange_box = carried
        index_x, index_y, index_z = box_indices(anchor, box_side, span_x, span_y)
        sampled = potential[index_x, index_y, index_z].reshape(box_side, flat_side)
        return sampled * orbital_box.astype(jnp.float32) - exx_share * exchange_box

    action = lax.map(apply_box, (box_list, anchors, exchange))
    return action.reshape(N_GX, N_GY, ORB, box_side, flat_side), potential
```

```python
import functools
import math

import jax
import jax.numpy as jnp
from jax import lax
from jax.experimental import pallas as pl
from jax.experimental.pallas import tpu as pltpu
from jax.sharding import PartitionSpec as P

SWEEPS = 4
SIDE = 64
HALF = SIDE // 2
FLAT = SIDE * SIDE
RIM = 24
LOW = SIDE - RIM
RIM_LEADS = RIM // 2
LOW_LEADS = LOW // 2
LANES = 128
PAD = 1024

screen_mass = 0.25
coupling = 2.0 * math.pi
exx_share = 0.25
xc_factor = (3.0 / math.pi) ** (1.0 / 3.0)

BASE_X = 2 * HALF * SIDE
BASE_Y = BASE_X + 4 * HALF * RIM
BASE_C = BASE_Y + 4 * RIM_LEADS * SIDE
WINDOW_ROWS = BASE_C + 8 * RIM_LEADS * RIM
STEPS = [(0, 0), (-1, 0), (1, 0), (0, -1), (0, 1), (-1, -1), (-1, 1), (1, -1), (1, 1)]


def place_of(step_x, step_y):
    rows = SIDE if step_x == 0 else RIM
    leads = HALF if step_y == 0 else RIM_LEADS
    if step_x == 0 and step_y == 0:
        base = 0
    elif step_y == 0:
        base = BASE_X + (2 * HALF * RIM if step_x > 0 else 0)
    elif step_x == 0:
        base = BASE_Y + (2 * RIM_LEADS * SIDE if step_y > 0 else 0)
    else:
        base = BASE_C + ((2 if step_x > 0 else 0) + (1 if step_y > 0 else 0)) * 2 * RIM_LEADS * RIM
    return base, rows, leads


def sweep_weights(sweep_count):
    return [
        1.0 / (1.0 + 0.7 * math.cos(math.pi * (2 * order + 1) / (2 * sweep_count)))
        for order in range(sweep_count)
    ]


def lane_index(rows):
    return lax.broadcasted_iota(jnp.int32, (rows, LANES), 1)


def for_leads(count, step):
    lax.fori_loop(0, count, lambda index, _: (step(index), 0)[1], 0)


def pair_kernel(mesh_x, mesh_y, anchors, pairs, count, *refs):
    pieces = refs[:9]
    outs = refs[9:18]
    window, first_sum, second_sum, moved3, source3, even3, moved8, source8, even8, odd3, odd8 = refs[18:]
    here_x = lax.axis_index("gx")
    here_y = lax.axis_index("gy")
    span_x = mesh_x * (SIDE - 16)
    span_y = mesh_y * (SIDE - 16)

    for (step_x, step_y), piece in zip(STEPS, pieces):
        base, rows, leads = place_of(step_x, step_y)

        def widen(lead, base=base, rows=rows, leads=leads, piece=piece):
            lanes = pl.ds(pl.multiple_of(lead * LANES, LANES), LANES)
            for k in range(2):
                start = pl.multiple_of(PAD + base + k * leads * rows + lead * rows, 8)
                window[pl.ds(start, rows), :] = piece[k, :, lanes].astype(jnp.float32)

        for_leads(leads, widen)

    zeros64 = jnp.zeros((SIDE, LANES), jnp.float32)

    def clear_first(lead):
        first_sum[pl.ds(pl.multiple_of(lead * SIDE, SIDE), SIDE), :] = zeros64

    for_leads(2 * HALF, clear_first)

    def clear_second(lead):
        second_sum[pl.ds(pl.multiple_of(lead * SIDE, SIDE), SIDE), :] = zeros64

    for_leads((WINDOW_ROWS + 2 * PAD) // SIDE, clear_second)

    for field in (source3, even3, odd3, source8, even8, odd8):
        rows = field.shape[1]

        def clear_field(lead, field=field, rows=rows):
            field[lead] = jnp.zeros((rows, LANES), jnp.float32)

        for_leads(HALF + 2, clear_field)

    weights = sweep_weights(SWEEPS)
    diagonal = 6.0 + screen_mass
    scale = [weight / diagonal for weight in weights]
    keep = [(1.0 - weight) / part for weight, part in zip(weights, scale)]
    total_scale = coupling * scale[0] * scale[1] * scale[2] * scale[3]

    def pair_step(slot, carry):
        first = pairs[2 * slot]
        second = pairs[2 * slot + 1]
        first_k = lax.rem(first, 2)
        second_k = lax.rem(second, 2)
        holder = lax.div(second, 2)
        step_x = lax.rem(lax.div(holder, mesh_y) - here_x + 1 + mesh_x, mesh_x) - 1
        step_y = lax.rem(lax.rem(holder, mesh_y) - here_y + 1 + mesh_y, mesh_y) - 1
        shift_x = anchors[3 * second] - anchors[3 * first]
        shift_y = anchors[3 * second + 1] - anchors[3 * first + 1]
        shift_z = anchors[3 * second + 2] - anchors[3 * first + 2]
        shift_x = shift_x + jnp.where(shift_x < -(span_x // 2), span_x, 0) - jnp.where(
            shift_x >= span_x // 2, span_x, 0
        )
        shift_y = shift_y + jnp.where(shift_y < -(span_y // 2), span_y, 0) - jnp.where(
            shift_y >= span_y // 2, span_y, 0
        )
        half_y = lax.shift_right_arithmetic(shift_y, 1)
        odd_y = shift_y - 2 * half_y
        side_x = step_x != 0
        side_y = step_y != 0
        stride = jnp.where(side_x, RIM, SIDE)
        leads = jnp.where(side_y, RIM_LEADS, HALF)
        plus_x = jnp.where(step_x > 0, 1, 0)
        plus_y = jnp.where(step_y > 0, 1, 0)
        base = jnp.where(
            side_x,
            jnp.where(
                side_y,
                BASE_C + (2 * plus_x + plus_y) * (2 * RIM_LEADS * RIM),
                BASE_X + plus_x * (2 * HALF * RIM),
            ),
            jnp.where(side_y, BASE_Y + plus_y * (2 * RIM_LEADS * SIDE), 0),
        )
        base = base + second_k * leads * stride
        start_x = plus_x * LOW
        start_lead = plus_y * LOW_LEADS
        origin_x = jnp.where(step_x < 0, LOW, 0)
        origin_lead = jnp.where(step_y < 0, LOW_LEADS, 0)
        far_start = PAD + base + (start_lead - half_y - origin_lead) * stride + start_x - shift_x - origin_x
        own_start = first_k * (HALF * SIDE) + start_lead * SIDE + start_x
        lane_turn = lax.rem(SIDE * odd_y + shift_z + LANES, LANES)
        lane_back = lax.rem(LANES - lane_turn, LANES)

        def run(tiles, chunk, moved, source, even, odd):
            rows = tiles * 8
            inner = pl.ds(8, rows)
            lane = lane_index(rows)
            depth = lax.rem(lane, SIDE)
            upper = lane >= SIDE
            row = lax.broadcasted_iota(jnp.int32, (rows, LANES), 0) + start_x
            column_part = jnp.where(upper, 1, 0) - shift_y
            same_lead = (lane < SIDE) | (odd_y == 0)
            inside_xz = (
                (row >= shift_x)
                & (row < SIDE + shift_x)
                & (depth >= shift_z)
                & (depth < SIDE + shift_z)
            )
            not_top = depth < SIDE - 1
            not_bottom = depth > 0

            def inside(lead):
                column = column_part + 2 * lead
                return inside_xz & (column >= 0) & (column < SIDE)

            def far_rows(lead):
                return pl.ds(far_start + lead * stride, rows)

            def own_rows(lead):
                return pl.ds(pl.multiple_of(own_start + lead * SIDE, 8), rows)

            def phi_rows(lead):
                return pl.ds(pl.multiple_of(PAD + own_start + lead * SIDE, 8), rows)

            def build(index):
                lead = index * chunk
                loads = [window[far_rows(lead + j), :] for j in range(-1, chunk)]
                for j in range(chunk):
                    picked = jnp.where(same_lead, loads[j + 1], loads[j])
                    turned = pltpu.roll(picked, lane_turn, 1)
                    piece = jnp.where(inside(start_lead + lead + j), turned, 0.0)
                    moved[lead + j] = piece
                    source[lead + j + 1, inner, :] = piece * window[phi_rows(lead + j), :]

            def neighbours(field, lead):
                here = field[lead + 1, inner, :]
                before = field[lead, inner, :]
                after = field[lead + 2, inner, :]
                across = pltpu.roll(here + jnp.where(upper, before, after), SIDE, 1)
                up = jnp.where(not_top, pltpu.roll(here, LANES - 1, 1), 0.0)
                down = jnp.where(not_bottom, pltpu.roll(here, 1, 1), 0.0)
                beside = field[lead + 1, pl.ds(7, rows), :] + field[lead + 1, pl.ds(9, rows), :]
                return here, (across + beside) + (up + down)

            def sweep(old, new, own_part, source_part):
                def body(index):
                    lead = index * chunk
                    for j in range(chunk):
                        here, near = neighbours(old, lead + j)
                        value = own_part * here + near
                        if source_part is not None:
                            value = value + source_part * source[lead + j + 1, inner, :]
                        new[lead + j + 1, inner, :] = value

                return body

            def finish(index):
                lead = index * chunk
                turned = []
                for j in range(chunk):
                    here, near = neighbours(odd, lead + j)
                    value = keep[3] * here + near
                    value = value + (1.0 / (scale[0] * scale[1] * scale[2])) * source[lead + j + 1, inner, :]
                    value = value * total_scale
                    first_sum[own_rows(lead + j), :] = (
                        first_sum[own_rows(lead + j), :] + value * moved[lead + j]
                    )
                    back = jnp.where(
                        inside(start_lead + lead + j), value * window[phi_rows(lead + j), :], 0.0
                    )
                    turned.append(pltpu.roll(back, lane_back, 1))
                targets = [second_sum[far_rows(lead + j), :] for j in range(-1, chunk)]
                for j in range(-1, chunk):
                    here = turned[j] if j >= 0 else 0.0
                    after = turned[j + 1] if j + 1 < chunk else 0.0
                    targets[j + 1] = targets[j + 1] + jnp.where(same_lead, here, after)
                for j in range(-1, chunk):
                    second_sum[far_rows(lead + j), :] = targets[j + 1]

            edge = jnp.zeros((rows, LANES), jnp.float32)
            for field in (source, even, odd):
                field[leads + 1, inner, :] = edge
            chunks = lax.div(leads, chunk)
            for_leads(chunks, build)
            for_leads(chunks, sweep(source, even, keep[1] + 1.0 / scale[0], None))
            for_leads(chunks, sweep(even, odd, keep[2], 1.0 / (scale[0] * scale[1])))
            for_leads(chunks, finish)

        @pl.when(side_x)
        def _():
            run(RIM // 8, 4, moved3, source3, even3, odd3)

        @pl.when(jnp.logical_not(side_x))
        def _():
            run(SIDE // 8, 4, moved8, source8, even8, odd8)

        return carry

    lax.fori_loop(0, count[0], pair_step, 0)

    for (step_x, step_y), out in zip(STEPS, outs):
        base, rows, leads = place_of(step_x, step_y)

        def narrow(lead, base=base, rows=rows, leads=leads, out=out, own=(step_x == 0 and step_y == 0)):
            lanes = pl.ds(pl.multiple_of(lead * LANES, LANES), LANES)
            for k in range(2):
                start = base + k * leads * rows + lead * rows
                value = second_sum[pl.ds(pl.multiple_of(PAD + start, 8), rows), :]
                if own:
                    value = value + first_sum[pl.ds(pl.multiple_of(start, 8), rows), :]
                out[k, :, lanes] = value.astype(out.dtype)

        for_leads(leads, narrow)


GRID_PAD = 8
GRID_ROWS = 88


def cube_root(value):
    inverse = jnp.exp(jnp.log(value) * (-1.0 / 3.0))
    inverse = inverse * (4.0 - value * inverse * inverse * inverse) * (1.0 / 3.0)
    return value * inverse * inverse


def grid_kernel(mesh_x, mesh_y, anchors, *refs):
    pieces = refs[:9]
    core, core_x, core_y, core_xy, applied, potential, grid = refs[9:]
    here_x = lax.axis_index("gx")
    here_y = lax.axis_index("gy")
    slab = core.shape[0]

    def clear(lead):
        grid[pl.ds(pl.multiple_of(lead * GRID_ROWS, 8), GRID_ROWS), :] = jnp.zeros(
            (GRID_ROWS, LANES), jnp.float32
        )

    for_leads(GRID_ROWS, clear)

    def offsets(step_x, step_y, k):
        holder_x = lax.rem(here_x + step_x + mesh_x, mesh_x)
        holder_y = lax.rem(here_y + step_y + mesh_y, mesh_y)
        orbit = (holder_x * mesh_y + holder_y) * 2 + k
        at_x = anchors[3 * orbit] - holder_x * slab
        at_y = anchors[3 * orbit + 1] - holder_y * slab
        return at_x, at_y, anchors[3 * orbit + 2]

    for (step_x, step_y), piece in zip(STEPS, pieces):
        base, rows, leads = place_of(step_x, step_y)
        chunk = 2 if rows == SIDE else 4
        lane = lane_index(rows)
        for k in range(2):
            at_x, at_y, at_z = offsets(step_x, step_y, k)
            row = at_x + step_x * slab + GRID_PAD + (LOW if step_x < 0 else 0)
            column = at_y + step_y * slab + GRID_PAD + (LOW if step_y < 0 else 0)
            start = column * GRID_ROWS + row
            mask = (lane >= at_z) & (lane < at_z + SIDE)
            turn_low = at_z
            turn_high = lax.rem(at_z + SIDE, LANES)

            def deposit(index):
                lead = index * chunk
                added = []
                for j in range(chunk):
                    lanes = pl.ds(pl.multiple_of((lead + j) * LANES, LANES), LANES)
                    value = piece[k, :, lanes].astype(jnp.float32)
                    value = value * value
                    added.append(jnp.where(mask, pltpu.roll(value, turn_low, 1), 0.0))
                    added.append(jnp.where(mask, pltpu.roll(value, turn_high, 1), 0.0))
                where_at = [
                    pl.ds(start + (2 * lead + j) * GRID_ROWS, rows) for j in range(2 * chunk)
                ]
                held = [grid[at, :] for at in where_at]
                for at, old, new in zip(where_at, held, added):
                    grid[at, :] = old + new

            for_leads(leads // chunk, deposit)

    def finish_at(row, column, core_part):
        at = pl.ds((column + GRID_PAD) * GRID_ROWS + GRID_PAD + row, 8, stride=GRID_ROWS)
        value = -xc_factor * cube_root(grid[at, :] + core_part)
        grid[at, :] = value
        return value

    def own_rows(row):
        for column in range(0, slab, 8):
            value = finish_at(row, column, core[row, pl.ds(column, 8), :])
            potential[row, pl.ds(column, 8), :] = value
        above = core_y[row].astype(jnp.float32)
        for column in range(0, RIM, 8):
            finish_at(row, slab + column, above[column : column + 8])

    for_leads(slab, own_rows)

    def rim_rows(row):
        beside = core_x[row].astype(jnp.float32)
        for column in range(0, slab, 8):
            finish_at(slab + row, column, beside[column : column + 8])
        above = core_xy[row].astype(jnp.float32)
        for column in range(0, RIM, 8):
            finish_at(slab + row, slab + column, above[column : column + 8])

    for_leads(RIM, rim_rows)

    lane = lane_index(SIDE)
    for k in range(2):
        at_x, at_y, at_z = offsets(0, 0, k)
        start = (at_y + GRID_PAD) * GRID_ROWS + at_x + GRID_PAD
        turn_low = lax.rem(LANES - at_z, LANES)
        turn_high = lax.rem(LANES + SIDE - at_z, LANES)

        def sample(index):
            for j in range(2):
                lead = index * 2 + j
                lanes = pl.ds(pl.multiple_of(lead * LANES, LANES), LANES)
                low = grid[pl.ds(start + 2 * lead * GRID_ROWS, SIDE), :]
                high = grid[pl.ds(start + (2 * lead + 1) * GRID_ROWS, SIDE), :]
                value = jnp.where(
                    lane < SIDE, pltpu.roll(low, turn_low, 1), pltpu.roll(high, turn_high, 1)
                )
                applied[k, :, lanes] = value * pieces[0][k, :, lanes].astype(jnp.float32)

        for_leads(HALF // 2, sample)


def from_behind(block, axis, distance):
    size = lax.axis_size(axis)
    return lax.ppermute(block, axis, [((i - distance) % size, i) for i in range(size)])


def local(orbitals, anchors, pair_list, pair_count, core_density):
    mesh_x = lax.axis_size("gx")
    mesh_y = lax.axis_size("gy")
    own = orbitals[0, 0]
    flat_anchors = anchors.reshape(-1)
    flat_pairs = pair_list.reshape(-1)
    flat_count = pair_count.reshape(-1)
    low_cut = LOW * SIDE
    rim_cut = RIM * SIDE

    from_left = from_behind(own[:, LOW:], "gx", 1)
    from_right = from_behind(own[:, :RIM], "gx", -1)
    from_below = from_behind(own[..., low_cut:], "gy", 1)
    from_above = from_behind(own[..., :rim_cut], "gy", -1)
    sides = jnp.stack([from_left, from_right])
    below_sides = from_behind(sides[..., low_cut:], "gy", 1)
    above_sides = from_behind(sides[..., :rim_cut], "gy", -1)
    narrow_core = core_density.astype(jnp.bfloat16)
    core_x = from_behind(narrow_core[:RIM], "gx", -1)
    core_y = from_behind(narrow_core[:, :RIM], "gy", -1)
    core_xy = from_behind(core_x[:, :RIM], "gy", -1)
    pieces = [
        own,
        from_left,
        from_right,
        from_below,
        from_above,
        below_sides[0],
        above_sides[0],
        below_sides[1],
        above_sides[1],
    ]
    smem = pl.BlockSpec(memory_space=pltpu.SMEM)
    vmem = pl.BlockSpec(memory_space=pltpu.VMEM)
    term_shapes = [jax.ShapeDtypeStruct(own.shape, jnp.float32)] + [
        jax.ShapeDtypeStruct(piece.shape, jnp.bfloat16) for piece in pieces[1:]
    ]

    def field(rows):
        return pltpu.VMEM((HALF + 2, rows, LANES), jnp.float32)

    terms = pl.pallas_call(
        functools.partial(pair_kernel, mesh_x, mesh_y),
        out_shape=term_shapes,
        in_specs=[smem] * 3 + [vmem] * 9,
        out_specs=[vmem] * 9,
        scratch_shapes=[
            pltpu.VMEM((WINDOW_ROWS + 2 * PAD, LANES), jnp.float32),
            pltpu.VMEM((2 * HALF * SIDE, LANES), jnp.float32),
            pltpu.VMEM((WINDOW_ROWS + 2 * PAD, LANES), jnp.float32),
            pltpu.VMEM((HALF, RIM, LANES), jnp.float32),
            field(RIM + 16),
            field(RIM + 16),
            pltpu.VMEM((HALF, SIDE, LANES), jnp.float32),
            field(SIDE + 16),
            field(SIDE + 16),
            field(RIM + 16),
            field(SIDE + 16),
        ],
        compiler_params=pltpu.CompilerParams(vmem_limit_bytes=56 * 1024 * 1024),
        cost_estimate=pl.CostEstimate(flops=40_000_000, bytes_accessed=8_000_000, transcendentals=0),
        name="pair_terms",
    )(flat_anchors, flat_pairs, flat_count, *pieces)

    applied, potential = pl.pallas_call(
        functools.partial(grid_kernel, mesh_x, mesh_y),
        out_shape=[
            jax.ShapeDtypeStruct(own.shape, jnp.float32),
            jax.ShapeDtypeStruct(core_density.shape, jnp.float32),
        ],
        in_specs=[smem] + [vmem] * 13,
        out_specs=[vmem] * 2,
        scratch_shapes=[pltpu.VMEM((GRID_ROWS * GRID_ROWS, LANES), jnp.float32)],
        compiler_params=pltpu.CompilerParams(vmem_limit_bytes=56 * 1024 * 1024),
        cost_estimate=pl.CostEstimate(flops=20_000_000, bytes_accessed=8_000_000, transcendentals=0),
        name="grid_terms",
    )(flat_anchors, *pieces, core_density, core_x, core_y, core_xy)

    below_left, above_left, below_right, above_right = terms[5:]
    back_below = from_behind(terms[3], "gy", -1)
    back_above = from_behind(terms[4], "gy", 1)
    back_below_sides = from_behind(jnp.stack([below_left, below_right]), "gy", -1).astype(jnp.float32)
    back_above_sides = from_behind(jnp.stack([above_left, above_right]), "gy", 1).astype(jnp.float32)
    side_terms = jnp.stack([terms[1], terms[2]]).astype(jnp.float32)
    side_terms = side_terms.at[..., low_cut:].add(back_below_sides)
    side_terms = side_terms.at[..., :rim_cut].add(back_above_sides).astype(jnp.bfloat16)
    back_left = from_behind(side_terms[0], "gx", -1)
    back_right = from_behind(side_terms[1], "gx", 1)
    exchange = terms[0]
    exchange = exchange.at[..., low_cut:].add(back_below.astype(jnp.float32))
    exchange = exchange.at[..., :rim_cut].add(back_above.astype(jnp.float32))
    exchange = exchange.at[:, LOW:].add(back_left.astype(jnp.float32))
    exchange = exchange.at[:, :RIM].add(back_right.astype(jnp.float32))
    action = applied - exx_share * exchange
    return (action.reshape(orbitals.shape), potential)


def solution(mesh):
    placed = (
        P("gx", "gy", None, None, None),
        P(),
        P("gx", "gy", None, None),
        P("gx", "gy"),
        P("gx", "gy", None),
    )
    return jax.shard_map(
        local,
        mesh=mesh,
        in_specs=placed,
        out_specs=(P("gx", "gy", None, None, None), P("gx", "gy", None)),
        check_vma=False,
    )
```

```python
import functools
import math

import jax
import jax.numpy as jnp
from jax import lax
from jax.experimental import pallas as pl
from jax.experimental.pallas import tpu as pltpu
from jax.sharding import PartitionSpec as P

SWEEPS = 4
SIDE = 64
HALF = SIDE // 2
FLAT = SIDE * SIDE
RIM = 24
LOW = SIDE - RIM
RIM_LEADS = RIM // 2
LOW_LEADS = LOW // 2
LANES = 128
PAD = 512
CHUNKS = [(False, False, 32), (True, False, 32), (False, True, 12), (True, True, 12)]

screen_mass = 0.25
coupling = 2.0 * math.pi
exx_share = 0.25
xc_factor = (3.0 / math.pi) ** (1.0 / 3.0)

BASE_X = 2 * HALF * SIDE
BASE_Y = BASE_X + 4 * HALF * RIM
BASE_C = BASE_Y + 4 * RIM_LEADS * SIDE
WINDOW_ROWS = BASE_C + 8 * RIM_LEADS * RIM
STEPS = [(0, 0), (-1, 0), (1, 0), (0, -1), (0, 1), (-1, -1), (-1, 1), (1, -1), (1, 1)]


def place_of(step_x, step_y):
    rows = SIDE if step_x == 0 else RIM
    leads = HALF if step_y == 0 else RIM_LEADS
    if step_x == 0 and step_y == 0:
        base = 0
    elif step_y == 0:
        base = BASE_X + (2 * HALF * RIM if step_x > 0 else 0)
    elif step_x == 0:
        base = BASE_Y + (2 * RIM_LEADS * SIDE if step_y > 0 else 0)
    else:
        base = BASE_C + ((2 if step_x > 0 else 0) + (1 if step_y > 0 else 0)) * 2 * RIM_LEADS * RIM
    return base, rows, leads


def sweep_weights(sweep_count):
    return [
        1.0 / (1.0 + 0.7 * math.cos(math.pi * (2 * order + 1) / (2 * sweep_count)))
        for order in range(sweep_count)
    ]


def lane_index(rows):
    return lax.broadcasted_iota(jnp.int32, (rows, LANES), 1)


def one_where(condition):
    return jnp.where(condition, 1.0, 0.0).astype(jnp.bfloat16)


def halves(value):
    upper = value.astype(jnp.bfloat16)
    lower = (value - upper.astype(jnp.float32)).astype(jnp.bfloat16)
    return jnp.concatenate([upper, lower], 1)


def for_leads(count, step):
    lax.fori_loop(0, count, lambda index, _: (step(index), 0)[1], 0)


def pair_kernel(mesh_x, mesh_y, anchors, pairs, count, *refs):
    pieces = refs[:9]
    outs = refs[9:18]
    (
        window,
        sums,
        near,
        turn_in,
        turn_out,
        moved3,
        source3,
        even3,
        odd3,
        moved8,
        source8,
        even8,
        odd8,
    ) = refs[18:]
    here_x = lax.axis_index("gx")
    here_y = lax.axis_index("gy")
    span_x = mesh_x * (SIDE - 16)
    span_y = mesh_y * (SIDE - 16)

    for (step_x, step_y), piece in zip(STEPS, pieces):
        base, rows, leads = place_of(step_x, step_y)

        def widen(lead, base=base, rows=rows, leads=leads, piece=piece):
            lanes = pl.ds(pl.multiple_of(lead * LANES, LANES), LANES)
            for k in range(2):
                start = pl.multiple_of(PAD + base + k * leads * rows + lead * rows, 8)
                window[pl.ds(start, rows), :] = piece[k, :, lanes].astype(jnp.float32)

        for_leads(leads, widen)

    zeros64 = jnp.zeros((SIDE, LANES), jnp.float32)

    def clear_sums(lead):
        sums[pl.ds(pl.multiple_of(lead * SIDE, SIDE), SIDE), :] = zeros64

    for_leads((WINDOW_ROWS + 2 * PAD) // SIDE, clear_sums)

    def clear_ends(lead):
        for start in (0, PAD + WINDOW_ROWS):
            window[pl.ds(pl.multiple_of(start + lead * SIDE, SIDE), SIDE), :] = zeros64

    for_leads(PAD // SIDE, clear_ends)

    for field in (source3, even3, odd3, source8, even8, odd8):
        rows = field.shape[1]
        field[0] = jnp.zeros((rows, LANES), jnp.float32)

        def clear_edge(lead, field=field, rows=rows):
            edge = jnp.zeros((8, LANES), jnp.float32)
            field[lead, pl.ds(0, 8), :] = edge
            field[lead, pl.ds(rows - 8, 8), :] = edge

        for_leads(HALF + 2, clear_edge)

    from_lane = lax.broadcasted_iota(jnp.int32, (LANES, LANES), 0)
    to_lane = lax.broadcasted_iota(jnp.int32, (LANES, LANES), 1)
    swap = jnp.abs(to_lane - from_lane) == SIDE
    step = (jnp.abs(to_lane - from_lane) == 1) & ((to_lane < SIDE) == (from_lane < SIDE))
    for start in (0, LANES):
        near[start : start + LANES, :LANES] = one_where(step | swap)
        near[start : start + LANES, LANES:] = one_where(swap)

    weights = sweep_weights(SWEEPS)
    diagonal = 6.0 + screen_mass
    scale = [weight / diagonal for weight in weights]
    keep = [(1.0 - weight) / part for weight, part in zip(weights, scale)]
    total_scale = coupling * scale[0] * scale[1] * scale[2] * scale[3]

    def pair_step(slot, carry):
        first = pairs[2 * slot]
        second = pairs[2 * slot + 1]
        first_k = lax.rem(first, 2)
        second_k = lax.rem(second, 2)
        holder = lax.div(second, 2)
        step_x = lax.rem(lax.div(holder, mesh_y) - here_x + 1 + mesh_x, mesh_x) - 1
        step_y = lax.rem(lax.rem(holder, mesh_y) - here_y + 1 + mesh_y, mesh_y) - 1
        shift_x = anchors[3 * second] - anchors[3 * first]
        shift_y = anchors[3 * second + 1] - anchors[3 * first + 1]
        shift_z = anchors[3 * second + 2] - anchors[3 * first + 2]
        shift_x = shift_x + jnp.where(shift_x < -(span_x // 2), span_x, 0) - jnp.where(
            shift_x >= span_x // 2, span_x, 0
        )
        shift_y = shift_y + jnp.where(shift_y < -(span_y // 2), span_y, 0) - jnp.where(
            shift_y >= span_y // 2, span_y, 0
        )
        half_y = lax.shift_right_arithmetic(shift_y, 1)
        odd_y = shift_y - 2 * half_y
        side_x = step_x != 0
        side_y = step_y != 0
        stride = jnp.where(side_x, RIM, SIDE)
        leads = jnp.where(side_y, RIM_LEADS, HALF)
        plus_x = jnp.where(step_x > 0, 1, 0)
        plus_y = jnp.where(step_y > 0, 1, 0)
        base = jnp.where(
            side_x,
            jnp.where(
                side_y,
                BASE_C + (2 * plus_x + plus_y) * (2 * RIM_LEADS * RIM),
                BASE_X + plus_x * (2 * HALF * RIM),
            ),
            jnp.where(side_y, BASE_Y + plus_y * (2 * RIM_LEADS * SIDE), 0),
        )
        base = base + second_k * leads * stride
        start_x = plus_x * LOW
        start_lead = plus_y * LOW_LEADS
        origin_x = jnp.where(step_x < 0, LOW, 0)
        origin_lead = jnp.where(step_y < 0, LOW_LEADS, 0)
        far_start = PAD + base + (start_lead - half_y - origin_lead) * stride + start_x - shift_x - origin_x
        own_start = first_k * (HALF * SIDE) + start_lead * SIDE + start_x
        from_lane = lax.broadcasted_iota(jnp.int32, (LANES, LANES), 0)
        to_lane = lax.broadcasted_iota(jnp.int32, (LANES, LANES), 1)
        apart = to_lane - from_lane - shift_z
        depth = lax.rem(to_lane, SIDE) - shift_z
        valid = (depth >= 0) & (depth < SIDE)
        same = valid & (apart == SIDE * odd_y)
        other = valid & (apart == -SIDE) & (odd_y == 1)
        turn_in[:LANES] = one_where(same)
        turn_in[LANES:] = one_where(other)
        from_lane, to_lane = to_lane, from_lane
        apart = to_lane - from_lane - shift_z
        depth = lax.rem(to_lane, SIDE) - shift_z
        valid = (depth >= 0) & (depth < SIDE)
        same = one_where(valid & (apart == SIDE * odd_y))
        other = one_where(valid & (apart == -SIDE) & (odd_y == 1))
        turn_out[:LANES, :LANES] = same
        turn_out[LANES:, :LANES] = same
        turn_out[:LANES, LANES:] = other
        turn_out[LANES:, LANES:] = other

        def run(tiles, leads, chunk, moved, source, even, odd):
            rows = tiles * 8
            inner = pl.ds(8, rows)
            lane = lane_index(rows)
            upper = lane >= SIDE
            row = lax.broadcasted_iota(jnp.int32, (rows, LANES), 0) + start_x
            column_part = jnp.where(upper, 1, 0) - shift_y
            inside_x = (row >= shift_x) & (row < SIDE + shift_x)

            def inside(lead):
                column = column_part + 2 * lead
                return inside_x & (column >= 0) & (column < SIDE)

            def far_rows(lead):
                return pl.ds(far_start + lead * stride, rows)

            def own_rows(lead):
                return pl.ds(pl.multiple_of(PAD + own_start + lead * SIDE, 8), rows)

            def part(value, index):
                return value[index * rows : (index + 1) * rows]

            def build(index):
                lead = index * chunk
                loads = [window[far_rows(lead + j), :] for j in range(-1, chunk)]
                now = jnp.concatenate(loads[1:], 0).astype(jnp.bfloat16)
                before = jnp.concatenate(loads[:-1], 0).astype(jnp.bfloat16)
                turned = jnp.dot(
                    jnp.concatenate([now, before], 1), turn_in[...], preferred_element_type=jnp.float32
                )
                for j in range(chunk):
                    piece = jnp.where(inside(start_lead + lead + j), part(turned, j), 0.0)
                    moved[lead + j] = piece
                    source[lead + j + 1, inner, :] = piece * window[own_rows(lead + j), :]

            def near_fields(field, lead):
                values = [field[lead + j, inner, :] for j in range(chunk + 2)]
                product = jnp.dot(
                    halves(jnp.concatenate(values, 0)), near[...], preferred_element_type=jnp.float32
                )
                for j in range(chunk):
                    across = jnp.where(
                        upper, part(product, j + 2)[:, LANES:], part(product, j)[:, LANES:]
                    )
                    beside = field[lead + j + 1, pl.ds(7, rows), :] + field[lead + j + 1, pl.ds(9, rows), :]
                    yield values[j + 1], (part(product, j + 1)[:, :LANES] + across) + beside

            def sweep(old, new, own_part, source_part):
                def body(index):
                    lead = index * chunk
                    for j, (here, near_sum) in enumerate(near_fields(old, lead)):
                        value = own_part * here + near_sum
                        if source_part is not None:
                            value = value + source_part * source[lead + j + 1, inner, :]
                        new[lead + j + 1, inner, :] = value

                return body

            def finish(index):
                lead = index * chunk
                back = []
                for j, (here, near_sum) in enumerate(near_fields(odd, lead)):
                    value = keep[3] * here + near_sum
                    value = value + (1.0 / (scale[0] * scale[1] * scale[2])) * source[lead + j + 1, inner, :]
                    value = value * total_scale
                    sums[own_rows(lead + j), :] = sums[own_rows(lead + j), :] + value * moved[lead + j]
                    back.append(
                        jnp.where(inside(start_lead + lead + j), value * window[own_rows(lead + j), :], 0.0)
                    )
                turned = jnp.dot(
                    halves(jnp.concatenate(back, 0)), turn_out[...], preferred_element_type=jnp.float32
                )
                targets = [sums[far_rows(lead + j), :] for j in range(-1, chunk)]
                for j in range(-1, chunk):
                    total = targets[j + 1]
                    if j >= 0:
                        total = total + part(turned, j)[:, :LANES]
                    if j + 1 < chunk:
                        total = total + part(turned, j + 1)[:, LANES:]
                    targets[j + 1] = total
                for j in range(-1, chunk):
                    sums[far_rows(lead + j), :] = targets[j + 1]

            edge = jnp.zeros((rows, LANES), jnp.float32)
            for field in (source, even, odd):
                field[leads + 1, inner, :] = edge
            chunks = leads // chunk
            for_leads(chunks, build)
            for_leads(chunks, sweep(source, even, keep[1] + 1.0 / scale[0], None))
            for_leads(chunks, sweep(even, odd, keep[2], 1.0 / (scale[0] * scale[1])))
            for_leads(chunks, finish)

        for has_x, has_y, chunk in CHUNKS:
            narrow = side_x if has_x else jnp.logical_not(side_x)
            narrow = narrow & (side_y if has_y else jnp.logical_not(side_y))
            fields = (moved3, source3, even3, odd3) if has_x else (moved8, source8, even8, odd8)

            @pl.when(narrow)
            def _(has_x=has_x, has_y=has_y, chunk=chunk, fields=fields):
                run(
                    (RIM if has_x else SIDE) // 8,
                    RIM_LEADS if has_y else HALF,
                    chunk,
                    *fields,
                )

        return carry

    lax.fori_loop(0, count[0], pair_step, 0)

    for (step_x, step_y), out in zip(STEPS, outs):
        base, rows, leads = place_of(step_x, step_y)

        def narrow(lead, base=base, rows=rows, leads=leads, out=out):
            lanes = pl.ds(pl.multiple_of(lead * LANES, LANES), LANES)
            for k in range(2):
                start = pl.multiple_of(PAD + base + k * leads * rows + lead * rows, 8)
                out[k, :, lanes] = sums[pl.ds(start, rows), :].astype(out.dtype)

        for_leads(leads, narrow)


smem = pl.BlockSpec(memory_space=pltpu.SMEM)
vmem = pl.BlockSpec(memory_space=pltpu.VMEM)


def pairs_call(mesh_x, mesh_y, flat_anchors, flat_pairs, flat_count, pieces):
    term_shapes = [jax.ShapeDtypeStruct(pieces[0].shape, jnp.float32)] + [
        jax.ShapeDtypeStruct(piece.shape, jnp.bfloat16) for piece in pieces[1:]
    ]

    def field(rows):
        return pltpu.VMEM((HALF + 2, rows, LANES), jnp.float32)

    return pl.pallas_call(
        functools.partial(pair_kernel, mesh_x, mesh_y),
        out_shape=term_shapes,
        in_specs=[smem] * 3 + [vmem] * 9,
        out_specs=[vmem] * 9,
        scratch_shapes=[
            pltpu.VMEM((WINDOW_ROWS + 2 * PAD, LANES), jnp.float32),
            pltpu.VMEM((WINDOW_ROWS + 2 * PAD, LANES), jnp.float32),
            pltpu.VMEM((2 * LANES, 2 * LANES), jnp.bfloat16),
            pltpu.VMEM((2 * LANES, LANES), jnp.bfloat16),
            pltpu.VMEM((2 * LANES, 2 * LANES), jnp.bfloat16),
            pltpu.VMEM((HALF, RIM, LANES), jnp.float32),
            field(RIM + 16),
            field(RIM + 16),
            field(RIM + 16),
            pltpu.VMEM((HALF, SIDE, LANES), jnp.float32),
            field(SIDE + 16),
            field(SIDE + 16),
            field(SIDE + 16),
        ],
        compiler_params=pltpu.CompilerParams(vmem_limit_bytes=56 * 1024 * 1024),
        cost_estimate=pl.CostEstimate(flops=40_000_000, bytes_accessed=8_000_000, transcendentals=0),
        name="pair_terms",
    )(flat_anchors, flat_pairs, flat_count, *pieces)


GRID_PAD = 8
GRID_ROWS = 88


def cube_root(value):
    inverse = jnp.exp(jnp.log(value) * (-1.0 / 3.0))
    inverse = inverse * (4.0 - value * inverse * inverse * inverse) * (1.0 / 3.0)
    return value * inverse * inverse


def grid_kernel(mesh_x, mesh_y, anchors, *refs):
    pieces = refs[:9]
    core, core_x, core_y, core_xy, applied, potential, grid = refs[9:]
    here_x = lax.axis_index("gx")
    here_y = lax.axis_index("gy")
    slab = core.shape[0]

    def clear(lead):
        grid[pl.ds(pl.multiple_of(lead * GRID_ROWS, 8), GRID_ROWS), :] = jnp.zeros(
            (GRID_ROWS, LANES), jnp.float32
        )

    for_leads(GRID_ROWS, clear)

    def offsets(step_x, step_y, k):
        holder_x = lax.rem(here_x + step_x + mesh_x, mesh_x)
        holder_y = lax.rem(here_y + step_y + mesh_y, mesh_y)
        orbit = (holder_x * mesh_y + holder_y) * 2 + k
        at_x = anchors[3 * orbit] - holder_x * slab
        at_y = anchors[3 * orbit + 1] - holder_y * slab
        return at_x, at_y, anchors[3 * orbit + 2]

    for (step_x, step_y), piece in zip(STEPS, pieces):
        base, rows, leads = place_of(step_x, step_y)
        chunk = 2 if rows == SIDE else 4
        lane = lane_index(rows)
        for k in range(2):
            at_x, at_y, at_z = offsets(step_x, step_y, k)
            row = at_x + step_x * slab + GRID_PAD + (LOW if step_x < 0 else 0)
            column = at_y + step_y * slab + GRID_PAD + (LOW if step_y < 0 else 0)
            start = column * GRID_ROWS + row
            mask = (lane >= at_z) & (lane < at_z + SIDE)
            turn_low = at_z
            turn_high = lax.rem(at_z + SIDE, LANES)

            def deposit(index):
                lead = index * chunk
                added = []
                for j in range(chunk):
                    lanes = pl.ds(pl.multiple_of((lead + j) * LANES, LANES), LANES)
                    value = piece[k, :, lanes].astype(jnp.float32)
                    value = value * value
                    added.append(jnp.where(mask, pltpu.roll(value, turn_low, 1), 0.0))
                    added.append(jnp.where(mask, pltpu.roll(value, turn_high, 1), 0.0))
                where_at = [
                    pl.ds(start + (2 * lead + j) * GRID_ROWS, rows) for j in range(2 * chunk)
                ]
                held = [grid[at, :] for at in where_at]
                for at, old, new in zip(where_at, held, added):
                    grid[at, :] = old + new

            for_leads(leads // chunk, deposit)

    def finish_at(row, column, core_part):
        at = pl.ds((column + GRID_PAD) * GRID_ROWS + GRID_PAD + row, 8, stride=GRID_ROWS)
        value = -xc_factor * cube_root(grid[at, :] + core_part)
        grid[at, :] = value
        return value

    def own_rows(row):
        for column in range(0, slab, 8):
            value = finish_at(row, column, core[row, pl.ds(column, 8), :])
            potential[row, pl.ds(column, 8), :] = value
        above = core_y[row].astype(jnp.float32)
        for column in range(0, RIM, 8):
            finish_at(row, slab + column, above[column : column + 8])

    for_leads(slab, own_rows)

    def rim_rows(row):
        beside = core_x[row].astype(jnp.float32)
        for column in range(0, slab, 8):
            finish_at(slab + row, column, beside[column : column + 8])
        above = core_xy[row].astype(jnp.float32)
        for column in range(0, RIM, 8):
            finish_at(slab + row, slab + column, above[column : column + 8])

    for_leads(RIM, rim_rows)

    lane = lane_index(SIDE)
    for k in range(2):
        at_x, at_y, at_z = offsets(0, 0, k)
        start = (at_y + GRID_PAD) * GRID_ROWS + at_x + GRID_PAD
        turn_low = lax.rem(LANES - at_z, LANES)
        turn_high = lax.rem(LANES + SIDE - at_z, LANES)

        def sample(index):
            for j in range(2):
                lead = index * 2 + j
                lanes = pl.ds(pl.multiple_of(lead * LANES, LANES), LANES)
                low = grid[pl.ds(start + 2 * lead * GRID_ROWS, SIDE), :]
                high = grid[pl.ds(start + (2 * lead + 1) * GRID_ROWS, SIDE), :]
                value = jnp.where(
                    lane < SIDE, pltpu.roll(low, turn_low, 1), pltpu.roll(high, turn_high, 1)
                )
                applied[k, :, lanes] = value * pieces[0][k, :, lanes].astype(jnp.float32)

        for_leads(HALF // 2, sample)


def from_behind(block, axis, distance):
    size = lax.axis_size(axis)
    return lax.ppermute(block, axis, [((i - distance) % size, i) for i in range(size)])


def local(orbitals, anchors, pair_list, pair_count, core_density):
    mesh_x = lax.axis_size("gx")
    mesh_y = lax.axis_size("gy")
    own = orbitals[0, 0]
    flat_anchors = anchors.reshape(-1)
    flat_pairs = pair_list.reshape(-1)
    flat_count = pair_count.reshape(-1)
    low_cut = LOW * SIDE
    rim_cut = RIM * SIDE

    from_left = from_behind(own[:, LOW:], "gx", 1)
    from_right = from_behind(own[:, :RIM], "gx", -1)
    from_below = from_behind(own[..., low_cut:], "gy", 1)
    from_above = from_behind(own[..., :rim_cut], "gy", -1)
    sides = jnp.stack([from_left, from_right])
    below_sides = from_behind(sides[..., low_cut:], "gy", 1)
    above_sides = from_behind(sides[..., :rim_cut], "gy", -1)
    narrow_core = core_density.astype(jnp.bfloat16)
    core_x = from_behind(narrow_core[:RIM], "gx", -1)
    core_y = from_behind(narrow_core[:, :RIM], "gy", -1)
    core_xy = from_behind(core_x[:, :RIM], "gy", -1)
    pieces = [
        own,
        from_left,
        from_right,
        from_below,
        from_above,
        below_sides[0],
        above_sides[0],
        below_sides[1],
        above_sides[1],
    ]
    terms = pairs_call(mesh_x, mesh_y, flat_anchors, flat_pairs, flat_count, pieces)

    applied, potential = pl.pallas_call(
        functools.partial(grid_kernel, mesh_x, mesh_y),
        out_shape=[
            jax.ShapeDtypeStruct(own.shape, jnp.float32),
            jax.ShapeDtypeStruct(core_density.shape, jnp.float32),
        ],
        in_specs=[smem] + [vmem] * 13,
        out_specs=[vmem] * 2,
        scratch_shapes=[pltpu.VMEM((GRID_ROWS * GRID_ROWS, LANES), jnp.float32)],
        compiler_params=pltpu.CompilerParams(vmem_limit_bytes=56 * 1024 * 1024),
        cost_estimate=pl.CostEstimate(flops=20_000_000, bytes_accessed=8_000_000, transcendentals=0),
        name="grid_terms",
    )(flat_anchors, *pieces, core_density, core_x, core_y, core_xy)

    below_left, above_left, below_right, above_right = terms[5:]
    back_below = from_behind(terms[3], "gy", -1)
    back_above = from_behind(terms[4], "gy", 1)
    back_below_sides = from_behind(jnp.stack([below_left, below_right]), "gy", -1).astype(jnp.float32)
    back_above_sides = from_behind(jnp.stack([above_left, above_right]), "gy", 1).astype(jnp.float32)
    side_terms = jnp.stack([terms[1], terms[2]]).astype(jnp.float32)
    side_terms = side_terms.at[..., low_cut:].add(back_below_sides)
    side_terms = side_terms.at[..., :rim_cut].add(back_above_sides).astype(jnp.bfloat16)
    back_left = from_behind(side_terms[0], "gx", -1)
    back_right = from_behind(side_terms[1], "gx", 1)
    exchange = terms[0]
    exchange = exchange.at[..., low_cut:].add(back_below.astype(jnp.float32))
    exchange = exchange.at[..., :rim_cut].add(back_above.astype(jnp.float32))
    exchange = exchange.at[:, LOW:].add(back_left.astype(jnp.float32))
    exchange = exchange.at[:, :RIM].add(back_right.astype(jnp.float32))
    action = applied - exx_share * exchange
    return (action.reshape(orbitals.shape), potential)


def solution(mesh):
    placed = (
        P("gx", "gy", None, None, None),
        P(),
        P("gx", "gy", None, None),
        P("gx", "gy"),
        P("gx", "gy", None),
    )
    return jax.shard_map(
        local,
        mesh=mesh,
        in_specs=placed,
        out_specs=(P("gx", "gy", None, None, None), P("gx", "gy", None)),
        check_vma=False,
    )
```

```python
import functools
import math

import jax
import jax.numpy as jnp
from jax import lax
from jax.experimental import pallas as pl
from jax.experimental.pallas import tpu as pltpu
from jax.sharding import PartitionSpec as P

SWEEPS = 4
SIDE = 64
HALF = SIDE // 2
FLAT = SIDE * SIDE
RIM = 24
LOW = SIDE - RIM
RIM_LEADS = RIM // 2
LOW_LEADS = LOW // 2
LANES = 128
PAD = 512
CHUNKS = [(False, False, 32), (True, False, 32), (False, True, 12), (True, True, 12)]

screen_mass = 0.25
coupling = 2.0 * math.pi
exx_share = 0.25
xc_factor = (3.0 / math.pi) ** (1.0 / 3.0)

BASE_X = 2 * HALF * SIDE
BASE_Y = BASE_X + 4 * HALF * RIM
BASE_C = BASE_Y + 4 * RIM_LEADS * SIDE
WINDOW_ROWS = BASE_C + 8 * RIM_LEADS * RIM
STEPS = [(0, 0), (-1, 0), (1, 0), (0, -1), (0, 1), (-1, -1), (-1, 1), (1, -1), (1, 1)]


def place_of(step_x, step_y):
    rows = SIDE if step_x == 0 else RIM
    leads = HALF if step_y == 0 else RIM_LEADS
    if step_x == 0 and step_y == 0:
        base = 0
    elif step_y == 0:
        base = BASE_X + (2 * HALF * RIM if step_x > 0 else 0)
    elif step_x == 0:
        base = BASE_Y + (2 * RIM_LEADS * SIDE if step_y > 0 else 0)
    else:
        base = BASE_C + ((2 if step_x > 0 else 0) + (1 if step_y > 0 else 0)) * 2 * RIM_LEADS * RIM
    return base, rows, leads


def sweep_weights(sweep_count):
    return [
        1.0 / (1.0 + 0.7 * math.cos(math.pi * (2 * order + 1) / (2 * sweep_count)))
        for order in range(sweep_count)
    ]


def lane_index(rows):
    return lax.broadcasted_iota(jnp.int32, (rows, LANES), 1)


def one_where(condition):
    return jnp.where(condition, 1.0, 0.0).astype(jnp.bfloat16)


def halves(value):
    upper = value.astype(jnp.bfloat16)
    lower = (value - upper.astype(jnp.float32)).astype(jnp.bfloat16)
    return jnp.concatenate([upper, lower], 1)


def for_leads(count, step):
    lax.fori_loop(0, count, lambda index, _: (step(index), 0)[1], 0)


def pair_kernel(mesh_x, mesh_y, anchors, pairs, count, *refs):
    pieces = refs[:9]
    own_out, grid_out = refs[9:11]
    outs = refs[11:19]
    (
        window,
        sums,
        near,
        turn_in,
        turn_out,
        moved3,
        source3,
        even3,
        odd3,
        moved8,
        source8,
        even8,
        odd8,
        grid,
        place,
        copies,
    ) = refs[19:]
    here_x = lax.axis_index("gx")
    here_y = lax.axis_index("gy")
    span_x = mesh_x * (SIDE - 16)
    span_y = mesh_y * (SIDE - 16)

    for (step_x, step_y), piece in zip(STEPS, pieces):
        base, rows, leads = place_of(step_x, step_y)

        def widen(lead, base=base, rows=rows, leads=leads, piece=piece):
            lanes = pl.ds(pl.multiple_of(lead * LANES, LANES), LANES)
            if rows == RIM:
                both = piece[:, lanes].astype(jnp.float32)
            for k in range(2):
                start = pl.multiple_of(PAD + base + k * leads * rows + lead * rows, 8)
                if rows == RIM:
                    value = both[k * RIM : (k + 1) * RIM]
                else:
                    value = piece[k, :, lanes].astype(jnp.float32)
                window[pl.ds(start, rows), :] = value

        for_leads(leads, widen)

    zeros64 = jnp.zeros((SIDE, LANES), jnp.float32)

    def clear_sums(lead):
        sums[pl.ds(pl.multiple_of(lead * SIDE, SIDE), SIDE), :] = zeros64

    for_leads((WINDOW_ROWS + 2 * PAD) // SIDE, clear_sums)

    def clear_ends(lead):
        for start in (0, PAD + WINDOW_ROWS):
            window[pl.ds(pl.multiple_of(start + lead * SIDE, SIDE), SIDE), :] = zeros64

    for_leads(PAD // SIDE, clear_ends)

    for field in (source3, even3, odd3, source8, even8, odd8):
        rows = field.shape[1]
        field[0] = jnp.zeros((rows, LANES), jnp.float32)

        def clear_edge(lead, field=field, rows=rows):
            edge = jnp.zeros((8, LANES), jnp.float32)
            field[lead, pl.ds(0, 8), :] = edge
            field[lead, pl.ds(rows - 8, 8), :] = edge

        for_leads(HALF + 2, clear_edge)

    from_lane = lax.broadcasted_iota(jnp.int32, (LANES, LANES), 0)
    to_lane = lax.broadcasted_iota(jnp.int32, (LANES, LANES), 1)
    swap = jnp.abs(to_lane - from_lane) == SIDE
    step = (jnp.abs(to_lane - from_lane) == 1) & ((to_lane < SIDE) == (from_lane < SIDE))
    for start in (0, LANES):
        near[start : start + LANES, :LANES] = one_where(step | swap)
        near[start : start + LANES, LANES:] = one_where(swap)

    weights = sweep_weights(SWEEPS)
    diagonal = 6.0 + screen_mass
    scale = [weight / diagonal for weight in weights]
    keep = [(1.0 - weight) / part for weight, part in zip(weights, scale)]
    total_scale = coupling * scale[0] * scale[1] * scale[2] * scale[3]

    def pair_step(slot, carry):
        first = pairs[2 * slot]
        second = pairs[2 * slot + 1]
        first_k = lax.rem(first, 2)
        second_k = lax.rem(second, 2)
        holder = lax.div(second, 2)
        step_x = lax.rem(lax.div(holder, mesh_y) - here_x + 1 + mesh_x, mesh_x) - 1
        step_y = lax.rem(lax.rem(holder, mesh_y) - here_y + 1 + mesh_y, mesh_y) - 1
        shift_x = anchors[3 * second] - anchors[3 * first]
        shift_y = anchors[3 * second + 1] - anchors[3 * first + 1]
        shift_z = anchors[3 * second + 2] - anchors[3 * first + 2]
        shift_x = shift_x + jnp.where(shift_x < -(span_x // 2), span_x, 0) - jnp.where(
            shift_x >= span_x // 2, span_x, 0
        )
        shift_y = shift_y + jnp.where(shift_y < -(span_y // 2), span_y, 0) - jnp.where(
            shift_y >= span_y // 2, span_y, 0
        )
        half_y = lax.shift_right_arithmetic(shift_y, 1)
        odd_y = shift_y - 2 * half_y
        side_x = step_x != 0
        side_y = step_y != 0
        stride = jnp.where(side_x, RIM, SIDE)
        leads = jnp.where(side_y, RIM_LEADS, HALF)
        plus_x = jnp.where(step_x > 0, 1, 0)
        plus_y = jnp.where(step_y > 0, 1, 0)
        base = jnp.where(
            side_x,
            jnp.where(
                side_y,
                BASE_C + (2 * plus_x + plus_y) * (2 * RIM_LEADS * RIM),
                BASE_X + plus_x * (2 * HALF * RIM),
            ),
            jnp.where(side_y, BASE_Y + plus_y * (2 * RIM_LEADS * SIDE), 0),
        )
        base = base + second_k * leads * stride
        start_x = plus_x * LOW
        start_lead = plus_y * LOW_LEADS
        origin_x = jnp.where(step_x < 0, LOW, 0)
        origin_lead = jnp.where(step_y < 0, LOW_LEADS, 0)
        far_start = PAD + base + (start_lead - half_y - origin_lead) * stride + start_x - shift_x - origin_x
        own_start = first_k * (HALF * SIDE) + start_lead * SIDE + start_x
        from_lane = lax.broadcasted_iota(jnp.int32, (LANES, LANES), 0)
        to_lane = lax.broadcasted_iota(jnp.int32, (LANES, LANES), 1)
        apart = to_lane - from_lane - shift_z
        depth = lax.rem(to_lane, SIDE) - shift_z
        valid = (depth >= 0) & (depth < SIDE)
        same = valid & (apart == SIDE * odd_y)
        other = valid & (apart == -SIDE) & (odd_y == 1)
        turn_in[:LANES] = one_where(same)
        turn_in[LANES:] = one_where(other)
        from_lane, to_lane = to_lane, from_lane
        apart = to_lane - from_lane - shift_z
        depth = lax.rem(to_lane, SIDE) - shift_z
        valid = (depth >= 0) & (depth < SIDE)
        same = one_where(valid & (apart == SIDE * odd_y))
        other = one_where(valid & (apart == -SIDE) & (odd_y == 1))
        turn_out[:LANES, :LANES] = same
        turn_out[LANES:, :LANES] = same
        turn_out[:LANES, LANES:] = other
        turn_out[LANES:, LANES:] = other

        def run(tiles, leads, chunk, moved, source, even, odd):
            rows = tiles * 8
            inner = pl.ds(8, rows)
            lane = lane_index(rows)
            upper = lane >= SIDE
            row = lax.broadcasted_iota(jnp.int32, (rows, LANES), 0) + start_x
            column_part = jnp.where(upper, 1, 0) - shift_y
            inside_x = (row >= shift_x) & (row < SIDE + shift_x)

            def inside(lead):
                column = column_part + 2 * lead
                return inside_x & (column >= 0) & (column < SIDE)

            def far_rows(lead):
                return pl.ds(far_start + lead * stride, rows)

            def own_rows(lead):
                return pl.ds(pl.multiple_of(PAD + own_start + lead * SIDE, 8), rows)

            def part(value, index):
                return value[index * rows : (index + 1) * rows]

            def build(index):
                lead = index * chunk
                loads = [window[far_rows(lead + j), :] for j in range(-1, chunk)]
                now = jnp.concatenate(loads[1:], 0).astype(jnp.bfloat16)
                before = jnp.concatenate(loads[:-1], 0).astype(jnp.bfloat16)
                turned = jnp.dot(
                    jnp.concatenate([now, before], 1), turn_in[...], preferred_element_type=jnp.float32
                )
                for j in range(chunk):
                    piece = jnp.where(inside(start_lead + lead + j), part(turned, j), 0.0)
                    moved[lead + j] = piece
                    source[lead + j + 1, inner, :] = piece * window[own_rows(lead + j), :]

            def near_fields(field, lead):
                values = [field[lead + j, inner, :] for j in range(chunk + 2)]
                product = jnp.dot(
                    halves(jnp.concatenate(values, 0)), near[...], preferred_element_type=jnp.float32
                )
                for j in range(chunk):
                    across = jnp.where(
                        upper, part(product, j + 2)[:, LANES:], part(product, j)[:, LANES:]
                    )
                    beside = field[lead + j + 1, pl.ds(7, rows), :] + field[lead + j + 1, pl.ds(9, rows), :]
                    yield values[j + 1], (part(product, j + 1)[:, :LANES] + across) + beside

            def sweep(old, new, own_part, source_part):
                def body(index):
                    lead = index * chunk
                    for j, (here, near_sum) in enumerate(near_fields(old, lead)):
                        value = own_part * here + near_sum
                        if source_part is not None:
                            value = value + source_part * source[lead + j + 1, inner, :]
                        new[lead + j + 1, inner, :] = value

                return body

            def finish(index):
                lead = index * chunk
                back = []
                for j, (here, near_sum) in enumerate(near_fields(odd, lead)):
                    value = keep[3] * here + near_sum
                    value = value + (1.0 / (scale[0] * scale[1] * scale[2])) * source[lead + j + 1, inner, :]
                    value = value * total_scale
                    sums[own_rows(lead + j), :] = sums[own_rows(lead + j), :] + value * moved[lead + j]
                    back.append(
                        jnp.where(inside(start_lead + lead + j), value * window[own_rows(lead + j), :], 0.0)
                    )
                turned = jnp.dot(
                    halves(jnp.concatenate(back, 0)), turn_out[...], preferred_element_type=jnp.float32
                )
                targets = [sums[far_rows(lead + j), :] for j in range(-1, chunk)]
                for j in range(-1, chunk):
                    total = targets[j + 1]
                    if j >= 0:
                        total = total + part(turned, j)[:, :LANES]
                    if j + 1 < chunk:
                        total = total + part(turned, j + 1)[:, LANES:]
                    targets[j + 1] = total
                for j in range(-1, chunk):
                    sums[far_rows(lead + j), :] = targets[j + 1]

            edge = jnp.zeros((rows, LANES), jnp.float32)
            for field in (source, even, odd):
                field[leads + 1, inner, :] = edge
            chunks = leads // chunk
            for_leads(chunks, build)
            for_leads(chunks, sweep(source, even, keep[1] + 1.0 / scale[0], None))
            for_leads(chunks, sweep(even, odd, keep[2], 1.0 / (scale[0] * scale[1])))
            for_leads(chunks, finish)

        for has_x, has_y, chunk in CHUNKS:
            narrow = side_x if has_x else jnp.logical_not(side_x)
            narrow = narrow & (side_y if has_y else jnp.logical_not(side_y))
            fields = (moved3, source3, even3, odd3) if has_x else (moved8, source8, even8, odd8)

            @pl.when(narrow)
            def _(has_x=has_x, has_y=has_y, chunk=chunk, fields=fields):
                run(
                    (RIM if has_x else SIDE) // 8,
                    RIM_LEADS if has_y else HALF,
                    chunk,
                    *fields,
                )

        return carry

    lax.fori_loop(0, count[0], pair_step, 0)

    own_copy = pltpu.make_async_copy(sums.at[pl.ds(PAD, BASE_X)], own_out, copies.at[0])
    own_copy.start()

    for (step_x, step_y), out in zip(STEPS[1:], outs):
        base, rows, leads = place_of(step_x, step_y)

        def narrow(lead, base=base, rows=rows, leads=leads, out=out):
            lanes = pl.ds(pl.multiple_of(lead * LANES, LANES), LANES)
            values = []
            for k in range(2):
                start = pl.multiple_of(PAD + base + k * leads * rows + lead * rows, 8)
                values.append(sums[pl.ds(start, rows), :])
            if rows == RIM:
                out[:, lanes] = jnp.concatenate(values, 0).astype(out.dtype)
            else:
                for k in range(2):
                    out[k, :, lanes] = values[k].astype(out.dtype)

        for_leads(leads, narrow)

    def clear_grid(lead):
        start = pl.multiple_of(lead * GRID_ROWS, 8)
        grid[pl.ds(start, GRID_ROWS), :] = jnp.zeros((GRID_ROWS, LANES), jnp.float32)

    for_leads(GRID_ROWS, clear_grid)
    slab = SIDE - 16

    def deposit(step_x, step_y, k, base, rows, leads):
        holder_x = lax.rem(here_x + step_x + mesh_x, mesh_x)
        holder_y = lax.rem(here_y + step_y + mesh_y, mesh_y)
        orbit = (holder_x * mesh_y + holder_y) * 2 + k
        at_x = anchors[3 * orbit] - holder_x * slab
        at_y = anchors[3 * orbit + 1] - holder_y * slab
        at_z = anchors[3 * orbit + 2]
        row = at_x + step_x * slab + GRID_PAD + jnp.where(step_x < 0, LOW, 0)
        column = at_y + step_y * slab + GRID_PAD + jnp.where(step_y < 0, LOW, 0)
        start = column * GRID_ROWS + row
        from_lane = lax.broadcasted_iota(jnp.int32, (LANES, LANES), 0)
        apart = lax.broadcasted_iota(jnp.int32, (LANES, LANES), 1) - from_lane - at_z
        low = one_where((from_lane < SIDE) & (apart == 0))
        high = one_where((from_lane >= SIDE) & (apart == -SIDE))
        for half in (0, LANES):
            place[half : half + LANES, :LANES] = low
            place[half : half + LANES, LANES:] = high
        block = 16
        for first in range(0, leads, block):
            size = min(block, leads - first)
            value = window[pl.ds(pl.multiple_of(PAD + base + first * rows, 8), size * rows), :]
            placed = jnp.dot(halves(value * value), place[...], preferred_element_type=jnp.float32)
            for j in range(size):
                for odd_column in (0, 1):
                    at = pl.ds(start + (2 * (first + j) + odd_column) * GRID_ROWS, rows)
                    part = placed[j * rows : (j + 1) * rows, odd_column * LANES : (odd_column + 1) * LANES]
                    grid[at, :] = grid[at, :] + part

    for k in range(2):
        deposit(0, 0, k, k * HALF * SIDE, SIDE, HALF)

    def deposit_x(index, carry):
        deposit(2 * (index // 2) - 1, 0, lax.rem(index, 2), BASE_X + index * (HALF * RIM), RIM, HALF)
        return carry

    def deposit_y(index, carry):
        deposit(
            0, 2 * (index // 2) - 1, lax.rem(index, 2), BASE_Y + index * (RIM_LEADS * SIDE), SIDE, RIM_LEADS
        )
        return carry

    def deposit_corner(index, carry):
        deposit(
            2 * (index // 4) - 1,
            2 * lax.rem(index // 2, 2) - 1,
            lax.rem(index, 2),
            BASE_C + index * (RIM_LEADS * RIM),
            RIM,
            RIM_LEADS,
        )
        return carry

    lax.fori_loop(0, 4, deposit_x, 0)
    lax.fori_loop(0, 4, deposit_y, 0)
    lax.fori_loop(0, 8, deposit_corner, 0)
    grid_copy = pltpu.make_async_copy(grid.at[pl.ds(GRID_PAD * GRID_ROWS, EDGE_ROWS)], grid_out, copies.at[1])
    grid_copy.start()
    own_copy.wait()
    grid_copy.wait()


GRID_PAD = 8
GRID_ROWS = 88
EDGE = SIDE - 16 + RIM
EDGE_ROWS = (EDGE + 1) * GRID_ROWS
hbm = pl.BlockSpec(memory_space=pl.ANY)
MESH = pl.DeviceIdType.MESH

smem = pl.BlockSpec(memory_space=pltpu.SMEM)
vmem = pl.BlockSpec(memory_space=pltpu.VMEM)


def pairs_call(mesh_x, mesh_y, flat_anchors, flat_pairs, flat_count, pieces):
    term_shapes = [
        jax.ShapeDtypeStruct((BASE_X, LANES), jnp.float32),
        jax.ShapeDtypeStruct((EDGE_ROWS, LANES), jnp.float32),
    ] + [jax.ShapeDtypeStruct(piece.shape, jnp.bfloat16) for piece in pieces[1:]]

    def field(rows):
        return pltpu.VMEM((HALF + 2, rows, LANES), jnp.float32)

    return pl.pallas_call(
        functools.partial(pair_kernel, mesh_x, mesh_y),
        out_shape=term_shapes,
        in_specs=[smem] * 3 + [vmem] * 9,
        out_specs=[hbm] * 2 + [vmem] * 8,
        scratch_shapes=[
            pltpu.VMEM((WINDOW_ROWS + 2 * PAD, LANES), jnp.float32),
            pltpu.VMEM((WINDOW_ROWS + 2 * PAD, LANES), jnp.float32),
            pltpu.VMEM((2 * LANES, 2 * LANES), jnp.bfloat16),
            pltpu.VMEM((2 * LANES, LANES), jnp.bfloat16),
            pltpu.VMEM((2 * LANES, 2 * LANES), jnp.bfloat16),
            pltpu.VMEM((HALF, RIM, LANES), jnp.float32),
            field(RIM + 16),
            field(RIM + 16),
            field(RIM + 16),
            pltpu.VMEM((HALF, SIDE, LANES), jnp.float32),
            field(SIDE + 16),
            field(SIDE + 16),
            field(SIDE + 16),
            pltpu.VMEM((GRID_ROWS * GRID_ROWS, LANES), jnp.float32),
            pltpu.VMEM((2 * LANES, 2 * LANES), jnp.bfloat16),
            pltpu.SemaphoreType.DMA((2,)),
        ],
        compiler_params=pltpu.CompilerParams(vmem_limit_bytes=56 * 1024 * 1024),
        cost_estimate=pl.CostEstimate(flops=40_000_000, bytes_accessed=8_000_000, transcendentals=0),
        name="pair_terms",
    )(flat_anchors, flat_pairs, flat_count, *pieces)


def cube_root(value):
    inverse = jnp.exp(jnp.log(value) * (-1.0 / 3.0))
    inverse = inverse * (4.0 - value * inverse * inverse * inverse) * (1.0 / 3.0)
    return value * inverse * inverse


def greet(mesh_x, mesh_y):
    here_x = lax.axis_index("gx")
    here_y = lax.axis_index("gy")
    left = (lax.rem(here_x + mesh_x - 1, mesh_x), here_y)
    right = (lax.rem(here_x + 1, mesh_x), here_y)
    below = (here_x, lax.rem(here_y + mesh_y - 1, mesh_y))
    above = (here_x, lax.rem(here_y + 1, mesh_y))
    barrier = pltpu.get_barrier_semaphore()
    for neighbour in (left, right, below, above):
        pl.semaphore_signal(barrier, inc=1, device_id=neighbour, device_id_type=MESH)
    pl.semaphore_wait(barrier, 4)
    return left, right, below, above


def gather_kernel(mesh_x, mesh_y, own, *refs):
    outs = refs[:8]
    send_low, send_high, sent, landed = refs[8:]
    left, right, below, above = greet(mesh_x, mesh_y)
    started = []

    def send(source, slot, device):
        copy = pltpu.make_async_remote_copy(
            src_ref=source,
            dst_ref=outs[slot],
            send_sem=sent.at[slot],
            recv_sem=landed.at[slot],
            device_id=device,
            device_id_type=MESH,
        )
        copy.start()
        started.append(copy)
        return copy

    def prepare(lead):
        lanes = pl.ds(pl.multiple_of(lead * LANES, LANES), LANES)
        values = [own[k, :, lanes].astype(jnp.float32) for k in range(2)]
        send_low[:, lanes] = jnp.concatenate([value[:RIM] for value in values], 0).astype(jnp.bfloat16)
        send_high[:, lanes] = jnp.concatenate([value[LOW:] for value in values], 0).astype(jnp.bfloat16)

    for_leads(HALF, prepare)
    from_left = send(send_high, 0, right)
    from_right = send(send_low, 1, left)
    high = pl.ds(LOW * SIDE, RIM * SIDE)
    low = pl.ds(0, RIM * SIDE)
    send(own.at[:, :, high], 2, above)
    send(own.at[:, :, low], 3, below)
    from_left.wait_recv()
    send(outs[0].at[:, high], 4, above)
    send(outs[0].at[:, low], 5, below)
    from_right.wait_recv()
    send(outs[1].at[:, high], 6, above)
    send(outs[1].at[:, low], 7, below)
    for copy in started:
        copy.wait_send()
    for copy in started[2:]:
        copy.wait_recv()


def return_kernel(mesh_x, mesh_y, *refs):
    side_terms = refs[:2]
    column_terms = refs[2:4]
    corner_terms = refs[4:8]
    density, core, core_x, core_y, core_xy = refs[8:13]
    outs = refs[13:17]
    potential = refs[17]
    landed_corners, send_left, send_right, sent, landed = refs[18:]
    left, right, below, above = greet(mesh_x, mesh_y)

    def send(source, target, slot, device):
        copy = pltpu.make_async_remote_copy(
            src_ref=source,
            dst_ref=target,
            send_sem=sent.at[slot],
            recv_sem=landed.at[slot],
            device_id=device,
            device_id_type=MESH,
        )
        copy.start()
        return copy

    corners = [
        send(corner_terms[slot], landed_corners.at[slot], slot, device)
        for slot, device in enumerate((below, above, below, above))
    ]
    others = [
        send(column_terms[0], outs[2], 4, below),
        send(column_terms[1], outs[3], 5, above),
    ]
    slab = core.shape[0]

    def finish_at(row, column, core_part):
        at = pl.ds(column * GRID_ROWS + GRID_PAD + row, 8, stride=GRID_ROWS)
        potential[at, :] = -xc_factor * cube_root(density[at, :] + core_part)

    def own_rows(row):
        for column in range(0, slab, 8):
            finish_at(row, column, core[row, pl.ds(column, 8), :])
        beyond = core_y[row].astype(jnp.float32)
        for column in range(0, RIM, 8):
            finish_at(row, slab + column, beyond[column : column + 8])

    def rim_rows(row):
        beside = core_x[row].astype(jnp.float32)
        for column in range(0, slab, 8):
            finish_at(slab + row, column, beside[column : column + 8])
        beyond = core_xy[row].astype(jnp.float32)
        for column in range(0, RIM, 8):
            finish_at(slab + row, slab + column, beyond[column : column + 8])

    for_leads(RIM, rim_rows)
    for copy in corners:
        copy.wait_recv()

    for side, target in enumerate((send_left, send_right)):
        terms = side_terms[side]

        def merge(lead, terms=terms, target=target, corner=None, shift=0):
            lanes = pl.ds(pl.multiple_of(lead * LANES, LANES), LANES)
            value = terms[:, lanes]
            if corner is not None:
                part = pl.ds(pl.multiple_of((lead - shift) * LANES, LANES), LANES)
                value = value.astype(jnp.float32) + landed_corners[corner, :, part].astype(jnp.float32)
            target[:, lanes] = value.astype(jnp.bfloat16)

        for first, last, corner in (
            (0, RIM_LEADS, 2 * side + 1),
            (RIM_LEADS, LOW_LEADS, None),
            (LOW_LEADS, HALF, 2 * side),
        ):

            def part_step(index, first=first, corner=corner, merge=merge):
                merge(index + first, corner=corner, shift=first)

            for_leads(last - first, part_step)
    others.append(send(send_left, outs[0], 6, left))
    others.append(send(send_right, outs[1], 7, right))
    for_leads(slab, own_rows)
    for copy in corners:
        copy.wait_send()
    for copy in others:
        copy.wait()


def action_kernel(mesh_x, mesh_y, anchors, own, own_terms, from_right, from_left, from_above, from_below, grid, action, potential):
    here_x = lax.axis_index("gx")
    here_y = lax.axis_index("gy")
    slab = potential.shape[0]

    def copy_rows(row):
        for column in range(0, slab, 8):
            at = pl.ds(column * GRID_ROWS + GRID_PAD + row, 8, stride=GRID_ROWS)
            potential[row, pl.ds(column, 8), :] = grid[at, :]

    for_leads(slab, copy_rows)
    lane = lane_index(SIDE)
    first = (here_x * mesh_y + here_y) * 2
    starts, lows, highs = [], [], []
    for k in range(2):
        at_x = anchors[3 * (first + k)] - here_x * slab
        at_y = anchors[3 * (first + k) + 1] - here_y * slab
        at_z = anchors[3 * (first + k) + 2]
        starts.append(at_y * GRID_ROWS + at_x + GRID_PAD)
        lows.append(lax.rem(LANES - at_z, LANES))
        highs.append(lax.rem(LANES + SIDE - at_z, LANES))

    def apply(lead, column=None, shift=0):
        lanes = pl.ds(pl.multiple_of(lead * LANES, LANES), LANES)
        above_rows = from_right[:, lanes].astype(jnp.float32)
        below_rows = from_left[:, lanes].astype(jnp.float32)
        for k in range(2):
            low = grid[pl.ds(starts[k] + 2 * lead * GRID_ROWS, SIDE), :]
            high = grid[pl.ds(starts[k] + (2 * lead + 1) * GRID_ROWS, SIDE), :]
            sampled = jnp.where(lane < SIDE, pltpu.roll(low, lows[k], 1), pltpu.roll(high, highs[k], 1))
            terms = own_terms[pl.ds(pl.multiple_of((k * HALF + lead) * SIDE, SIDE), SIDE), :]
            if column is not None:
                part = pl.ds(pl.multiple_of((lead - shift) * LANES, LANES), LANES)
                terms = terms + column[k, :, part].astype(jnp.float32)
            rows = slice(k * RIM, (k + 1) * RIM)
            terms = jnp.concatenate(
                [terms[:RIM] + below_rows[rows], terms[RIM:LOW], terms[LOW:] + above_rows[rows]], 0
            )
            action[k, :, lanes] = sampled * own[k, :, lanes].astype(jnp.float32) - exx_share * terms

    for start, stop, column in ((0, RIM_LEADS, from_below), (RIM_LEADS, LOW_LEADS, None), (LOW_LEADS, HALF, from_above)):

        def part_step(index, start=start, column=column):
            apply(index + start, column=column, shift=start)

        for_leads(stop - start, part_step)


def shape_of(dims, dtype=jnp.bfloat16):
    return jax.ShapeDtypeStruct(dims, dtype)


def local(orbitals, anchors, pair_list, pair_count, core_density):
    mesh_x = lax.axis_size("gx")
    mesh_y = lax.axis_size("gy")
    own = orbitals[0, 0]
    flat_anchors = anchors.reshape(-1)
    flat_pairs = pair_list.reshape(-1)
    flat_count = pair_count.reshape(-1)
    side_shape = shape_of((2 * RIM, FLAT))
    column_shape = shape_of((2, SIDE, RIM * SIDE))
    corner_shape = shape_of((2 * RIM, RIM * SIDE))
    around = [side_shape] * 2 + [column_shape] * 2 + [corner_shape] * 4

    pieces = pl.pallas_call(
        functools.partial(gather_kernel, mesh_x, mesh_y),
        out_shape=around,
        in_specs=[vmem],
        out_specs=[hbm] * 8,
        scratch_shapes=[
            pltpu.VMEM(side_shape.shape, jnp.bfloat16),
            pltpu.VMEM(side_shape.shape, jnp.bfloat16),
            pltpu.SemaphoreType.DMA((8,)),
            pltpu.SemaphoreType.DMA((8,)),
        ],
        compiler_params=pltpu.CompilerParams(
            collective_id=0, has_side_effects=True, vmem_limit_bytes=16 * 1024 * 1024
        ),
        name="gather_rims",
    )(own)

    narrow_x = core_density[:RIM].astype(jnp.bfloat16)
    narrow_y = core_density[:, :RIM].astype(jnp.bfloat16)
    narrow_x, narrow_y, corner = lax.optimization_barrier((narrow_x, narrow_y, pieces[7]))
    pieces = list(pieces[:7]) + [corner]
    back_x = [((i + 1) % mesh_x, i) for i in range(mesh_x)]
    back_y = [((i + 1) % mesh_y, i) for i in range(mesh_y)]
    back_xy = [
        ((i + 1) % mesh_x * mesh_y + (j + 1) % mesh_y, i * mesh_y + j)
        for i in range(mesh_x)
        for j in range(mesh_y)
    ]
    core_x = lax.ppermute(narrow_x, "gx", back_x)
    core_y = lax.ppermute(narrow_y, "gy", back_y)
    core_xy = lax.ppermute(narrow_x[:, :RIM], ("gx", "gy"), back_xy)

    terms = pairs_call(mesh_x, mesh_y, flat_anchors, flat_pairs, flat_count, [own] + pieces)
    returned = pl.pallas_call(
        functools.partial(return_kernel, mesh_x, mesh_y),
        out_shape=[side_shape] * 2 + [column_shape] * 2 + [shape_of((EDGE_ROWS, LANES), jnp.float32)],
        in_specs=[vmem] * 2 + [hbm] * 6 + [vmem] * 5,
        out_specs=[hbm] * 4 + [vmem],
        scratch_shapes=[
            pltpu.VMEM((4,) + corner_shape.shape, jnp.bfloat16),
            pltpu.VMEM(side_shape.shape, jnp.bfloat16),
            pltpu.VMEM(side_shape.shape, jnp.bfloat16),
            pltpu.SemaphoreType.DMA((8,)),
            pltpu.SemaphoreType.DMA((8,)),
        ],
        compiler_params=pltpu.CompilerParams(
            collective_id=1, has_side_effects=True, vmem_limit_bytes=32 * 1024 * 1024
        ),
        name="return_terms",
    )(*terms[2:], terms[1], core_density, core_x, core_y, core_xy)
    action, potential = pl.pallas_call(
        functools.partial(action_kernel, mesh_x, mesh_y),
        out_shape=[shape_of(own.shape, jnp.float32), shape_of(core_density.shape, jnp.float32)],
        in_specs=[smem] + [vmem] * 7,
        out_specs=[vmem] * 2,
        compiler_params=pltpu.CompilerParams(vmem_limit_bytes=32 * 1024 * 1024),
        name="action_terms",
    )(flat_anchors, own, terms[0], *returned)
    return (action.reshape(orbitals.shape), potential)


def solution(mesh):
    placed = (
        P("gx", "gy", None, None, None),
        P(),
        P("gx", "gy", None, None),
        P("gx", "gy"),
        P("gx", "gy", None),
    )
    return jax.shard_map(
        local,
        mesh=mesh,
        in_specs=placed,
        out_specs=(P("gx", "gy", None, None, None), P("gx", "gy", None)),
        check_vma=False,
    )
```

```python
import functools
import math

import jax
import jax.numpy as jnp
from jax import lax
from jax.experimental import pallas as pl
from jax.experimental.pallas import tpu as pltpu
from jax.sharding import PartitionSpec as P

SWEEPS = 4
SIDE = 64
HALF = SIDE // 2
FLAT = SIDE * SIDE
RIM = 24
LOW = SIDE - RIM
RIM_LEADS = RIM // 2
LOW_LEADS = LOW // 2
LANES = 128
PAD = 512
CHUNKS = [(False, False, 32), (True, False, 32), (False, True, 12), (True, True, 12)]

screen_mass = 0.25
coupling = 2.0 * math.pi
exx_share = 0.25
xc_factor = (3.0 / math.pi) ** (1.0 / 3.0)

BASE_X = 2 * HALF * SIDE
BASE_Y = BASE_X + 4 * HALF * RIM
BASE_C = BASE_Y + 4 * RIM_LEADS * SIDE
WINDOW_ROWS = BASE_C + 8 * RIM_LEADS * RIM
STEPS = [(0, 0), (-1, 0), (1, 0), (0, -1), (0, 1), (-1, -1), (-1, 1), (1, -1), (1, 1)]


def place_of(step_x, step_y):
    rows = SIDE if step_x == 0 else RIM
    leads = HALF if step_y == 0 else RIM_LEADS
    if step_x == 0 and step_y == 0:
        base = 0
    elif step_y == 0:
        base = BASE_X + (2 * HALF * RIM if step_x > 0 else 0)
    elif step_x == 0:
        base = BASE_Y + (2 * RIM_LEADS * SIDE if step_y > 0 else 0)
    else:
        base = BASE_C + ((2 if step_x > 0 else 0) + (1 if step_y > 0 else 0)) * 2 * RIM_LEADS * RIM
    return base, rows, leads


def sweep_weights(sweep_count):
    return [
        1.0 / (1.0 + 0.7 * math.cos(math.pi * (2 * order + 1) / (2 * sweep_count)))
        for order in range(sweep_count)
    ]


def lane_index(rows):
    return lax.broadcasted_iota(jnp.int32, (rows, LANES), 1)


def one_where(condition):
    return jnp.where(condition, 1.0, 0.0).astype(jnp.bfloat16)


def halves(value):
    upper = value.astype(jnp.bfloat16)
    lower = (value - upper.astype(jnp.float32)).astype(jnp.bfloat16)
    return jnp.concatenate([upper, lower], 1)


def for_leads(count, step):
    lax.fori_loop(0, count, lambda index, _: (step(index), 0)[1], 0)


def pair_kernel(mesh_x, mesh_y, anchors, pairs, count, *refs):
    pieces = refs[:9]
    own_out, grid_out = refs[9:11]
    outs = refs[11:19]
    (
        window,
        sums,
        near,
        turn_in,
        turn_out,
        moved3,
        source3,
        even3,
        odd3,
        moved8,
        source8,
        even8,
        odd8,
        grid,
        place,
        copies,
    ) = refs[19:]
    here_x = lax.axis_index("gx")
    here_y = lax.axis_index("gy")
    span_x = mesh_x * (SIDE - 16)
    span_y = mesh_y * (SIDE - 16)

    for (step_x, step_y), piece in zip(STEPS, pieces):
        base, rows, leads = place_of(step_x, step_y)

        def widen(lead, base=base, rows=rows, leads=leads, piece=piece):
            lanes = pl.ds(pl.multiple_of(lead * LANES, LANES), LANES)
            if rows == RIM:
                both = piece[:, lanes].astype(jnp.float32)
            for k in range(2):
                start = pl.multiple_of(PAD + base + k * leads * rows + lead * rows, 8)
                if rows == RIM:
                    value = both[k * RIM : (k + 1) * RIM]
                else:
                    value = piece[k, :, lanes].astype(jnp.float32)
                window[pl.ds(start, rows), :] = value

        for_leads(leads, widen)

    zeros64 = jnp.zeros((SIDE, LANES), jnp.float32)

    def clear_sums(lead):
        sums[pl.ds(pl.multiple_of(lead * SIDE, SIDE), SIDE), :] = zeros64

    for_leads((WINDOW_ROWS + 2 * PAD) // SIDE, clear_sums)

    def clear_ends(lead):
        for start in (0, PAD + WINDOW_ROWS):
            window[pl.ds(pl.multiple_of(start + lead * SIDE, SIDE), SIDE), :] = zeros64

    for_leads(PAD // SIDE, clear_ends)

    for field in (source3, even3, odd3, source8, even8, odd8):
        rows = field.shape[1]
        field[0] = jnp.zeros((rows, LANES), jnp.float32)

        def clear_edge(lead, field=field, rows=rows):
            edge = jnp.zeros((8, LANES), jnp.float32)
            field[lead, pl.ds(0, 8), :] = edge
            field[lead, pl.ds(rows - 8, 8), :] = edge

        for_leads(HALF + 2, clear_edge)

    from_lane = lax.broadcasted_iota(jnp.int32, (LANES, LANES), 0)
    to_lane = lax.broadcasted_iota(jnp.int32, (LANES, LANES), 1)
    swap = jnp.abs(to_lane - from_lane) == SIDE
    step = (jnp.abs(to_lane - from_lane) == 1) & ((to_lane < SIDE) == (from_lane < SIDE))
    for start in (0, LANES):
        near[start : start + LANES, :LANES] = one_where(step | swap)
        near[start : start + LANES, LANES:] = one_where(swap)

    weights = sweep_weights(SWEEPS)
    diagonal = 6.0 + screen_mass
    scale = [weight / diagonal for weight in weights]
    keep = [(1.0 - weight) / part for weight, part in zip(weights, scale)]
    total_scale = coupling * scale[0] * scale[1] * scale[2] * scale[3]

    def pair_step(slot, carry):
        first = pairs[0, slot]
        second = pairs[1, slot]
        first_k = lax.rem(first, 2)
        second_k = lax.rem(second, 2)
        holder = lax.div(second, 2)
        step_x = lax.rem(lax.div(holder, mesh_y) - here_x + 1 + mesh_x, mesh_x) - 1
        step_y = lax.rem(lax.rem(holder, mesh_y) - here_y + 1 + mesh_y, mesh_y) - 1
        shift_x = anchors[0, second] - anchors[0, first]
        shift_y = anchors[1, second] - anchors[1, first]
        shift_z = anchors[2, second] - anchors[2, first]
        shift_x = shift_x + jnp.where(shift_x < -(span_x // 2), span_x, 0) - jnp.where(
            shift_x >= span_x // 2, span_x, 0
        )
        shift_y = shift_y + jnp.where(shift_y < -(span_y // 2), span_y, 0) - jnp.where(
            shift_y >= span_y // 2, span_y, 0
        )
        half_y = lax.shift_right_arithmetic(shift_y, 1)
        odd_y = shift_y - 2 * half_y
        side_x = step_x != 0
        side_y = step_y != 0
        stride = jnp.where(side_x, RIM, SIDE)
        leads = jnp.where(side_y, RIM_LEADS, HALF)
        plus_x = jnp.where(step_x > 0, 1, 0)
        plus_y = jnp.where(step_y > 0, 1, 0)
        base = jnp.where(
            side_x,
            jnp.where(
                side_y,
                BASE_C + (2 * plus_x + plus_y) * (2 * RIM_LEADS * RIM),
                BASE_X + plus_x * (2 * HALF * RIM),
            ),
            jnp.where(side_y, BASE_Y + plus_y * (2 * RIM_LEADS * SIDE), 0),
        )
        base = base + second_k * leads * stride
        start_x = plus_x * LOW
        start_lead = plus_y * LOW_LEADS
        origin_x = jnp.where(step_x < 0, LOW, 0)
        origin_lead = jnp.where(step_y < 0, LOW_LEADS, 0)
        far_start = PAD + base + (start_lead - half_y - origin_lead) * stride + start_x - shift_x - origin_x
        own_start = first_k * (HALF * SIDE) + start_lead * SIDE + start_x
        from_lane = lax.broadcasted_iota(jnp.int32, (LANES, LANES), 0)
        to_lane = lax.broadcasted_iota(jnp.int32, (LANES, LANES), 1)
        apart = to_lane - from_lane - shift_z
        depth = lax.rem(to_lane, SIDE) - shift_z
        valid = (depth >= 0) & (depth < SIDE)
        same = valid & (apart == SIDE * odd_y)
        other = valid & (apart == -SIDE) & (odd_y == 1)
        turn_in[:LANES] = one_where(same)
        turn_in[LANES:] = one_where(other)
        from_lane, to_lane = to_lane, from_lane
        apart = to_lane - from_lane - shift_z
        depth = lax.rem(to_lane, SIDE) - shift_z
        valid = (depth >= 0) & (depth < SIDE)
        same = one_where(valid & (apart == SIDE * odd_y))
        other = one_where(valid & (apart == -SIDE) & (odd_y == 1))
        turn_out[:LANES, :LANES] = same
        turn_out[LANES:, :LANES] = same
        turn_out[:LANES, LANES:] = other
        turn_out[LANES:, LANES:] = other

        def run(tiles, leads, chunk, moved, source, even, odd):
            rows = tiles * 8
            inner = pl.ds(8, rows)
            lane = lane_index(rows)
            upper = lane >= SIDE
            row = lax.broadcasted_iota(jnp.int32, (rows, LANES), 0) + start_x
            column_part = jnp.where(upper, 1, 0) - shift_y
            inside_x = (row >= shift_x) & (row < SIDE + shift_x)

            def inside(lead):
                column = column_part + 2 * lead
                return inside_x & (column >= 0) & (column < SIDE)

            def far_rows(lead):
                return pl.ds(far_start + lead * stride, rows)

            def own_rows(lead):
                return pl.ds(pl.multiple_of(PAD + own_start + lead * SIDE, 8), rows)

            def part(value, index):
                return value[index * rows : (index + 1) * rows]

            def build(index):
                lead = index * chunk
                loads = [window[far_rows(lead + j), :] for j in range(-1, chunk)]
                now = jnp.concatenate(loads[1:], 0).astype(jnp.bfloat16)
                before = jnp.concatenate(loads[:-1], 0).astype(jnp.bfloat16)
                turned = jnp.dot(
                    jnp.concatenate([now, before], 1), turn_in[...], preferred_element_type=jnp.float32
                )
                for j in range(chunk):
                    piece = jnp.where(inside(start_lead + lead + j), part(turned, j), 0.0)
                    moved[lead + j] = piece
                    source[lead + j + 1, inner, :] = piece * window[own_rows(lead + j), :]

            def near_fields(field, lead):
                values = [field[lead + j, inner, :] for j in range(chunk + 2)]
                product = jnp.dot(
                    halves(jnp.concatenate(values, 0)), near[...], preferred_element_type=jnp.float32
                )
                for j in range(chunk):
                    across = jnp.where(
                        upper, part(product, j + 2)[:, LANES:], part(product, j)[:, LANES:]
                    )
                    beside = field[lead + j + 1, pl.ds(7, rows), :] + field[lead + j + 1, pl.ds(9, rows), :]
                    yield values[j + 1], (part(product, j + 1)[:, :LANES] + across) + beside

            def sweep(old, new, own_part, source_part):
                def body(index):
                    lead = index * chunk
                    for j, (here, near_sum) in enumerate(near_fields(old, lead)):
                        value = own_part * here + near_sum
                        if source_part is not None:
                            value = value + source_part * source[lead + j + 1, inner, :]
                        new[lead + j + 1, inner, :] = value

                return body

            def finish(index):
                lead = index * chunk
                back = []
                for j, (here, near_sum) in enumerate(near_fields(odd, lead)):
                    value = keep[3] * here + near_sum
                    value = value + (1.0 / (scale[0] * scale[1] * scale[2])) * source[lead + j + 1, inner, :]
                    value = value * total_scale
                    sums[own_rows(lead + j), :] = sums[own_rows(lead + j), :] + value * moved[lead + j]
                    back.append(
                        jnp.where(inside(start_lead + lead + j), value * window[own_rows(lead + j), :], 0.0)
                    )
                turned = jnp.dot(
                    halves(jnp.concatenate(back, 0)), turn_out[...], preferred_element_type=jnp.float32
                )
                targets = [sums[far_rows(lead + j), :] for j in range(-1, chunk)]
                for j in range(-1, chunk):
                    total = targets[j + 1]
                    if j >= 0:
                        total = total + part(turned, j)[:, :LANES]
                    if j + 1 < chunk:
                        total = total + part(turned, j + 1)[:, LANES:]
                    targets[j + 1] = total
                for j in range(-1, chunk):
                    sums[far_rows(lead + j), :] = targets[j + 1]

            edge = jnp.zeros((rows, LANES), jnp.float32)
            for field in (source, even, odd):
                field[leads + 1, inner, :] = edge
            chunks = leads // chunk
            for_leads(chunks, build)
            for_leads(chunks, sweep(source, even, keep[1] + 1.0 / scale[0], None))
            for_leads(chunks, sweep(even, odd, keep[2], 1.0 / (scale[0] * scale[1])))
            for_leads(chunks, finish)

        for has_x, has_y, chunk in CHUNKS:
            narrow = side_x if has_x else jnp.logical_not(side_x)
            narrow = narrow & (side_y if has_y else jnp.logical_not(side_y))
            fields = (moved3, source3, even3, odd3) if has_x else (moved8, source8, even8, odd8)

            @pl.when(narrow)
            def _(has_x=has_x, has_y=has_y, chunk=chunk, fields=fields):
                run(
                    (RIM if has_x else SIDE) // 8,
                    RIM_LEADS if has_y else HALF,
                    chunk,
                    *fields,
                )

        return carry

    lax.fori_loop(0, count[0], pair_step, 0)

    own_copy = pltpu.make_async_copy(sums.at[pl.ds(PAD, BASE_X)], own_out, copies.at[0])
    own_copy.start()

    for (step_x, step_y), out in zip(STEPS[1:], outs):
        base, rows, leads = place_of(step_x, step_y)

        def narrow(lead, base=base, rows=rows, leads=leads, out=out):
            lanes = pl.ds(pl.multiple_of(lead * LANES, LANES), LANES)
            values = []
            for k in range(2):
                start = pl.multiple_of(PAD + base + k * leads * rows + lead * rows, 8)
                values.append(sums[pl.ds(start, rows), :])
            if rows == RIM:
                out[:, lanes] = jnp.concatenate(values, 0).astype(out.dtype)
            else:
                for k in range(2):
                    out[k, :, lanes] = values[k].astype(out.dtype)

        for_leads(leads, narrow)

    def clear_grid(lead):
        start = pl.multiple_of(lead * GRID_ROWS, 8)
        grid[pl.ds(start, GRID_ROWS), :] = jnp.zeros((GRID_ROWS, LANES), jnp.float32)

    for_leads(GRID_ROWS, clear_grid)
    slab = SIDE - 16

    def deposit(step_x, step_y, k, base, rows, leads):
        holder_x = lax.rem(here_x + step_x + mesh_x, mesh_x)
        holder_y = lax.rem(here_y + step_y + mesh_y, mesh_y)
        orbit = (holder_x * mesh_y + holder_y) * 2 + k
        at_x = anchors[0, orbit] - holder_x * slab
        at_y = anchors[1, orbit] - holder_y * slab
        at_z = anchors[2, orbit]
        row = at_x + step_x * slab + GRID_PAD + jnp.where(step_x < 0, LOW, 0)
        column = at_y + step_y * slab + GRID_PAD + jnp.where(step_y < 0, LOW, 0)
        start = column * GRID_ROWS + row
        from_lane = lax.broadcasted_iota(jnp.int32, (LANES, LANES), 0)
        apart = lax.broadcasted_iota(jnp.int32, (LANES, LANES), 1) - from_lane - at_z
        low = one_where((from_lane < SIDE) & (apart == 0))
        high = one_where((from_lane >= SIDE) & (apart == -SIDE))
        for half in (0, LANES):
            place[half : half + LANES, :LANES] = low
            place[half : half + LANES, LANES:] = high
        block = 16
        for first in range(0, leads, block):
            size = min(block, leads - first)
            value = window[pl.ds(pl.multiple_of(PAD + base + first * rows, 8), size * rows), :]
            placed = jnp.dot(halves(value * value), place[...], preferred_element_type=jnp.float32)
            for j in range(size):
                for odd_column in (0, 1):
                    at = pl.ds(start + (2 * (first + j) + odd_column) * GRID_ROWS, rows)
                    part = placed[j * rows : (j + 1) * rows, odd_column * LANES : (odd_column + 1) * LANES]
                    grid[at, :] = grid[at, :] + part

    for k in range(2):
        deposit(0, 0, k, k * HALF * SIDE, SIDE, HALF)

    def deposit_x(index, carry):
        deposit(2 * (index // 2) - 1, 0, lax.rem(index, 2), BASE_X + index * (HALF * RIM), RIM, HALF)
        return carry

    def deposit_y(index, carry):
        deposit(
            0, 2 * (index // 2) - 1, lax.rem(index, 2), BASE_Y + index * (RIM_LEADS * SIDE), SIDE, RIM_LEADS
        )
        return carry

    def deposit_corner(index, carry):
        deposit(
            2 * (index // 4) - 1,
            2 * lax.rem(index // 2, 2) - 1,
            lax.rem(index, 2),
            BASE_C + index * (RIM_LEADS * RIM),
            RIM,
            RIM_LEADS,
        )
        return carry

    lax.fori_loop(0, 4, deposit_x, 0)
    lax.fori_loop(0, 4, deposit_y, 0)
    lax.fori_loop(0, 8, deposit_corner, 0)
    grid_copy = pltpu.make_async_copy(grid.at[pl.ds(GRID_PAD * GRID_ROWS, EDGE_ROWS)], grid_out, copies.at[1])
    grid_copy.start()
    own_copy.wait()
    grid_copy.wait()


GRID_PAD = 8
GRID_ROWS = 88
EDGE = SIDE - 16 + RIM
EDGE_ROWS = (EDGE + 1) * GRID_ROWS
hbm = pl.BlockSpec(memory_space=pl.ANY)
MESH = pl.DeviceIdType.MESH

smem = pl.BlockSpec(memory_space=pltpu.SMEM)
vmem = pl.BlockSpec(memory_space=pltpu.VMEM)


def pairs_call(mesh_x, mesh_y, flat_anchors, flat_pairs, flat_count, pieces):
    term_shapes = [
        jax.ShapeDtypeStruct((BASE_X, LANES), jnp.float32),
        jax.ShapeDtypeStruct((EDGE_ROWS, LANES), jnp.float32),
    ] + [jax.ShapeDtypeStruct(piece.shape, jnp.bfloat16) for piece in pieces[1:]]

    def field(rows):
        return pltpu.VMEM((HALF + 2, rows, LANES), jnp.float32)

    return pl.pallas_call(
        functools.partial(pair_kernel, mesh_x, mesh_y),
        out_shape=term_shapes,
        in_specs=[smem] * 3 + [vmem] * 9,
        out_specs=[hbm] * 2 + [vmem] * 8,
        scratch_shapes=[
            pltpu.VMEM((WINDOW_ROWS + 2 * PAD, LANES), jnp.float32),
            pltpu.VMEM((WINDOW_ROWS + 2 * PAD, LANES), jnp.float32),
            pltpu.VMEM((2 * LANES, 2 * LANES), jnp.bfloat16),
            pltpu.VMEM((2 * LANES, LANES), jnp.bfloat16),
            pltpu.VMEM((2 * LANES, 2 * LANES), jnp.bfloat16),
            pltpu.VMEM((HALF, RIM, LANES), jnp.float32),
            field(RIM + 16),
            field(RIM + 16),
            field(RIM + 16),
            pltpu.VMEM((HALF, SIDE, LANES), jnp.float32),
            field(SIDE + 16),
            field(SIDE + 16),
            field(SIDE + 16),
            pltpu.VMEM((GRID_ROWS * GRID_ROWS, LANES), jnp.float32),
            pltpu.VMEM((2 * LANES, 2 * LANES), jnp.bfloat16),
            pltpu.SemaphoreType.DMA((2,)),
        ],
        compiler_params=pltpu.CompilerParams(vmem_limit_bytes=56 * 1024 * 1024),
        cost_estimate=pl.CostEstimate(flops=40_000_000, bytes_accessed=8_000_000, transcendentals=0),
        name="pair_terms",
    )(flat_anchors, flat_pairs, flat_count, *pieces)


def cube_root(value):
    inverse = jnp.exp(jnp.log(value) * (-1.0 / 3.0))
    inverse = inverse * (4.0 - value * inverse * inverse * inverse) * (1.0 / 3.0)
    return value * inverse * inverse


def greet(mesh_x, mesh_y, diagonal=False):
    here_x = lax.axis_index("gx")
    here_y = lax.axis_index("gy")
    left = (lax.rem(here_x + mesh_x - 1, mesh_x), here_y)
    right = (lax.rem(here_x + 1, mesh_x), here_y)
    below = (here_x, lax.rem(here_y + mesh_y - 1, mesh_y))
    above = (here_x, lax.rem(here_y + 1, mesh_y))
    barrier = pltpu.get_barrier_semaphore()
    neighbours = [left, right, below, above]
    if diagonal:
        neighbours += [(left[0], below[1]), (right[0], above[1])]
    for neighbour in neighbours:
        pl.semaphore_signal(barrier, inc=1, device_id=neighbour, device_id_type=MESH)
    pl.semaphore_wait(barrier, len(neighbours))
    return left, right, below, above


def gather_kernel(mesh_x, mesh_y, own, *refs):
    outs = refs[:8]
    send_low, send_high, sent, landed = refs[8:]
    left, right, below, above = greet(mesh_x, mesh_y)
    started = []

    def send(source, slot, device):
        copy = pltpu.make_async_remote_copy(
            src_ref=source,
            dst_ref=outs[slot],
            send_sem=sent.at[slot],
            recv_sem=landed.at[slot],
            device_id=device,
            device_id_type=MESH,
        )
        copy.start()
        started.append(copy)
        return copy

    def prepare(lead):
        lanes = pl.ds(pl.multiple_of(lead * LANES, LANES), LANES)
        values = [own[k, :, lanes].astype(jnp.float32) for k in range(2)]
        send_low[:, lanes] = jnp.concatenate([value[:RIM] for value in values], 0).astype(jnp.bfloat16)
        send_high[:, lanes] = jnp.concatenate([value[LOW:] for value in values], 0).astype(jnp.bfloat16)

    for_leads(HALF, prepare)
    from_left = send(send_high, 0, right)
    from_right = send(send_low, 1, left)
    high = pl.ds(LOW * SIDE, RIM * SIDE)
    low = pl.ds(0, RIM * SIDE)
    send(own.at[:, :, high], 2, above)
    send(own.at[:, :, low], 3, below)
    from_left.wait_recv()
    send(outs[0].at[:, high], 4, above)
    send(outs[0].at[:, low], 5, below)
    from_right.wait_recv()
    send(outs[1].at[:, high], 6, above)
    send(outs[1].at[:, low], 7, below)
    for copy in started:
        copy.wait_send()
    for copy in started[2:]:
        copy.wait_recv()


def return_kernel(mesh_x, mesh_y, *refs):
    side_terms = refs[:2]
    column_terms = refs[2:4]
    corner_terms = refs[4:8]
    density, core = refs[8:10]
    outs = refs[10:14]
    potential = refs[14]
    landed_corners, send_left, send_right, narrow_x, narrow_y, core_x, core_y, core_xy, sent, landed = refs[15:]
    left, right, below, above = greet(mesh_x, mesh_y, diagonal=True)

    def send(source, target, slot, device):
        copy = pltpu.make_async_remote_copy(
            src_ref=source,
            dst_ref=target,
            send_sem=sent.at[slot],
            recv_sem=landed.at[slot],
            device_id=device,
            device_id_type=MESH,
        )
        copy.start()
        return copy

    corners = [
        send(corner_terms[slot], landed_corners.at[slot], slot, device)
        for slot, device in enumerate((below, above, below, above))
    ]
    others = [
        send(column_terms[0], outs[2], 4, below),
        send(column_terms[1], outs[3], 5, above),
    ]
    slab = core.shape[0]

    def narrow(row):
        narrow_x[row] = core[row].astype(jnp.bfloat16)
        narrow_y[row] = jnp.concatenate([core[2 * row, :RIM], core[2 * row + 1, :RIM]], 0).astype(jnp.bfloat16)

    for_leads(RIM, narrow)
    from_right = send(narrow_x, core_x, 8, left)

    def finish_at(row, column, core_part):
        at = pl.ds(column * GRID_ROWS + GRID_PAD + row, 8, stride=GRID_ROWS)
        potential[at, :] = -xc_factor * cube_root(density[at, :] + core_part)

    def own_rows(row):
        for column in range(0, slab, 8):
            finish_at(row, column, core[row, pl.ds(column, 8), :])

    def right_rows(row):
        beside = core_x[row].astype(jnp.float32)
        for column in range(0, slab, 8):
            finish_at(slab + row, column, beside[column : column + 8])

    def above_rows(pair, source=core_y, beyond=0):
        part = source[pair].astype(jnp.float32)
        for j in range(2):
            for column in range(0, RIM, 8):
                start = j * RIM + column
                finish_at(beyond + 2 * pair + j, slab + column, part[start : start + 8])

    def corner_rows(pair):
        above_rows(pair, source=core_xy, beyond=slab)

    for copy in corners:
        copy.wait_recv()

    for side, target in enumerate((send_left, send_right)):
        terms = side_terms[side]

        def merge(lead, terms=terms, target=target, corner=None, shift=0):
            lanes = pl.ds(pl.multiple_of(lead * LANES, LANES), LANES)
            value = terms[:, lanes]
            if corner is not None:
                part = pl.ds(pl.multiple_of((lead - shift) * LANES, LANES), LANES)
                value = value.astype(jnp.float32) + landed_corners[corner, :, part].astype(jnp.float32)
            target[:, lanes] = value.astype(jnp.bfloat16)

        for first, last, corner in (
            (0, RIM_LEADS, 2 * side + 1),
            (RIM_LEADS, LOW_LEADS, None),
            (LOW_LEADS, HALF, 2 * side),
        ):

            def part_step(index, first=first, corner=corner, merge=merge):
                merge(index + first, corner=corner, shift=first)

            for_leads(last - first, part_step)
    others.append(send(send_left, outs[0], 6, left))
    others.append(send(send_right, outs[1], 7, right))
    from_above = send(narrow_y, core_y, 9, below)
    from_corner = send(narrow_y.at[pl.ds(0, RIM // 2)], core_xy, 10, (left[0], below[1]))
    for_leads(slab, own_rows)
    from_right.wait()
    for_leads(RIM, right_rows)
    from_above.wait()
    for_leads(slab // 2, above_rows)
    from_corner.wait()
    for_leads(RIM // 2, corner_rows)
    for copy in corners:
        copy.wait_send()
    for copy in others:
        copy.wait()


def action_kernel(mesh_x, mesh_y, anchors, own, own_terms, from_right, from_left, from_above, from_below, grid, action, potential):
    here_x = lax.axis_index("gx")
    here_y = lax.axis_index("gy")
    slab = potential.shape[0]

    def copy_rows(row):
        for column in range(0, slab, 8):
            at = pl.ds(column * GRID_ROWS + GRID_PAD + row, 8, stride=GRID_ROWS)
            potential[row, pl.ds(column, 8), :] = grid[at, :]

    for_leads(slab, copy_rows)
    lane = lane_index(SIDE)
    first = (here_x * mesh_y + here_y) * 2
    starts, lows, highs = [], [], []
    for k in range(2):
        at_x = anchors[0, first + k] - here_x * slab
        at_y = anchors[1, first + k] - here_y * slab
        at_z = anchors[2, first + k]
        starts.append(at_y * GRID_ROWS + at_x + GRID_PAD)
        lows.append(lax.rem(LANES - at_z, LANES))
        highs.append(lax.rem(LANES + SIDE - at_z, LANES))

    def apply(lead, column=None, shift=0):
        lanes = pl.ds(pl.multiple_of(lead * LANES, LANES), LANES)
        above_rows = from_right[:, lanes].astype(jnp.float32)
        below_rows = from_left[:, lanes].astype(jnp.float32)
        for k in range(2):
            low = grid[pl.ds(starts[k] + 2 * lead * GRID_ROWS, SIDE), :]
            high = grid[pl.ds(starts[k] + (2 * lead + 1) * GRID_ROWS, SIDE), :]
            sampled = jnp.where(lane < SIDE, pltpu.roll(low, lows[k], 1), pltpu.roll(high, highs[k], 1))
            terms = own_terms[pl.ds(pl.multiple_of((k * HALF + lead) * SIDE, SIDE), SIDE), :]
            if column is not None:
                part = pl.ds(pl.multiple_of((lead - shift) * LANES, LANES), LANES)
                terms = terms + column[k, :, part].astype(jnp.float32)
            rows = slice(k * RIM, (k + 1) * RIM)
            terms = jnp.concatenate(
                [terms[:RIM] + below_rows[rows], terms[RIM:LOW], terms[LOW:] + above_rows[rows]], 0
            )
            action[k, :, lanes] = sampled * own[k, :, lanes].astype(jnp.float32) - exx_share * terms

    for start, stop, column in ((0, RIM_LEADS, from_below), (RIM_LEADS, LOW_LEADS, None), (LOW_LEADS, HALF, from_above)):

        def part_step(index, start=start, column=column):
            apply(index + start, column=column, shift=start)

        for_leads(stop - start, part_step)


def shape_of(dims, dtype=jnp.bfloat16):
    return jax.ShapeDtypeStruct(dims, dtype)


def local(orbitals, anchors, pair_list, pair_count, core_density):
    mesh_x = lax.axis_size("gx")
    mesh_y = lax.axis_size("gy")
    own = orbitals[0, 0]
    flat_anchors = anchors.T
    flat_pairs = pair_list[0, 0].T
    flat_count = pair_count.reshape(-1)
    side_shape = shape_of((2 * RIM, FLAT))
    column_shape = shape_of((2, SIDE, RIM * SIDE))
    corner_shape = shape_of((2 * RIM, RIM * SIDE))
    around = [side_shape] * 2 + [column_shape] * 2 + [corner_shape] * 4

    pieces = pl.pallas_call(
        functools.partial(gather_kernel, mesh_x, mesh_y),
        out_shape=around,
        in_specs=[vmem],
        out_specs=[hbm] * 8,
        scratch_shapes=[
            pltpu.VMEM(side_shape.shape, jnp.bfloat16),
            pltpu.VMEM(side_shape.shape, jnp.bfloat16),
            pltpu.SemaphoreType.DMA((8,)),
            pltpu.SemaphoreType.DMA((8,)),
        ],
        compiler_params=pltpu.CompilerParams(
            collective_id=0, has_side_effects=True, vmem_limit_bytes=56 * 1024 * 1024
        ),
        name="gather_rims",
    )(own)

    terms = pairs_call(mesh_x, mesh_y, flat_anchors, flat_pairs, flat_count, [own] + list(pieces))
    returned = pl.pallas_call(
        functools.partial(return_kernel, mesh_x, mesh_y),
        out_shape=[side_shape] * 2 + [column_shape] * 2 + [shape_of((EDGE_ROWS, LANES), jnp.float32)],
        in_specs=[vmem] * 2 + [hbm] * 6 + [vmem] * 2,
        out_specs=[hbm] * 4 + [vmem],
        scratch_shapes=[
            pltpu.VMEM((4,) + corner_shape.shape, jnp.bfloat16),
            pltpu.VMEM(side_shape.shape, jnp.bfloat16),
            pltpu.VMEM(side_shape.shape, jnp.bfloat16),
            pltpu.VMEM((RIM, SIDE - 16, LANES), jnp.bfloat16),
            pltpu.VMEM((RIM, 2 * RIM, LANES), jnp.bfloat16),
            pltpu.VMEM((RIM, SIDE - 16, LANES), jnp.bfloat16),
            pltpu.VMEM((RIM, 2 * RIM, LANES), jnp.bfloat16),
            pltpu.VMEM((RIM // 2, 2 * RIM, LANES), jnp.bfloat16),
            pltpu.SemaphoreType.DMA((11,)),
            pltpu.SemaphoreType.DMA((11,)),
        ],
        compiler_params=pltpu.CompilerParams(
            collective_id=1, has_side_effects=True, vmem_limit_bytes=56 * 1024 * 1024
        ),
        name="return_terms",
    )(*terms[2:], terms[1], core_density)
    action, potential = pl.pallas_call(
        functools.partial(action_kernel, mesh_x, mesh_y),
        out_shape=[shape_of(own.shape, jnp.float32), shape_of(core_density.shape, jnp.float32)],
        in_specs=[smem] + [vmem] * 7,
        out_specs=[vmem] * 2,
        compiler_params=pltpu.CompilerParams(vmem_limit_bytes=56 * 1024 * 1024),
        name="action_terms",
    )(flat_anchors, own, terms[0], *returned)
    return (action.reshape(orbitals.shape), potential)


def solution(mesh):
    placed = (
        P("gx", "gy", None, None, None),
        P(),
        P("gx", "gy", None, None),
        P("gx", "gy"),
        P("gx", "gy", None),
    )
    return jax.shard_map(
        local,
        mesh=mesh,
        in_specs=placed,
        out_specs=(P("gx", "gy", None, None, None), P("gx", "gy", None)),
        check_vma=False,
    )
```

```python
import functools
import math

import jax
import jax.numpy as jnp
from jax import lax
from jax.experimental import pallas as pl
from jax.experimental.pallas import tpu as pltpu
from jax.sharding import PartitionSpec as P

SWEEPS = 4
SIDE = 64
HALF = SIDE // 2
FLAT = SIDE * SIDE
RIM = 24
LOW = SIDE - RIM
RIM_LEADS = RIM // 2
LOW_LEADS = LOW // 2
LANES = 128
PAD = 512
CHUNKS = [(False, False, 32), (True, False, 32), (False, True, 12), (True, True, 12)]

screen_mass = 0.25
coupling = 2.0 * math.pi
exx_share = 0.25
xc_factor = (3.0 / math.pi) ** (1.0 / 3.0)

BASE_X = 2 * HALF * SIDE
BASE_Y = BASE_X + 4 * HALF * RIM
BASE_C = BASE_Y + 4 * RIM_LEADS * SIDE
WINDOW_ROWS = BASE_C + 8 * RIM_LEADS * RIM
STEPS = [(0, 0), (-1, 0), (1, 0), (0, -1), (0, 1), (-1, -1), (-1, 1), (1, -1), (1, 1)]


def place_of(step_x, step_y):
    rows = SIDE if step_x == 0 else RIM
    leads = HALF if step_y == 0 else RIM_LEADS
    if step_x == 0 and step_y == 0:
        base = 0
    elif step_y == 0:
        base = BASE_X + (2 * HALF * RIM if step_x > 0 else 0)
    elif step_x == 0:
        base = BASE_Y + (2 * RIM_LEADS * SIDE if step_y > 0 else 0)
    else:
        base = BASE_C + ((2 if step_x > 0 else 0) + (1 if step_y > 0 else 0)) * 2 * RIM_LEADS * RIM
    return base, rows, leads


def sweep_weights(sweep_count):
    return [
        1.0 / (1.0 + 0.7 * math.cos(math.pi * (2 * order + 1) / (2 * sweep_count)))
        for order in range(sweep_count)
    ]


def lane_index(rows):
    return lax.broadcasted_iota(jnp.int32, (rows, LANES), 1)


def one_where(condition):
    return jnp.where(condition, 1.0, 0.0).astype(jnp.bfloat16)


def halves(value):
    upper = value.astype(jnp.bfloat16)
    lower = (value - upper.astype(jnp.float32)).astype(jnp.bfloat16)
    return jnp.concatenate([upper, lower], 1)


def for_leads(count, step):
    lax.fori_loop(0, count, lambda index, _: (step(index), 0)[1], 0)


def pair_kernel(mesh_x, mesh_y, anchors, pairs, count, *refs):
    sources = refs[:9]
    own_out, grid_out = refs[9:11]
    targets_out = refs[11:19]
    (
        window,
        sums,
        near,
        turn_in,
        turn_out,
        moved3,
        source3,
        even3,
        odd3,
        moved8,
        source8,
        even8,
        odd8,
        grid,
        place,
        copies,
    ) = refs[19:35]
    pieces = refs[35:44]
    outs = refs[44:52]
    here_x = lax.axis_index("gx")
    here_y = lax.axis_index("gy")
    span_x = mesh_x * (SIDE - 16)
    span_y = mesh_y * (SIDE - 16)

    incoming = [
        pltpu.make_async_copy(source, piece, copies.at[2 + index])
        for index, (source, piece) in enumerate(zip(sources, pieces))
    ]
    for copy in incoming:
        copy.start()
    zeros64 = jnp.zeros((SIDE, LANES), jnp.float32)

    def clear_sums(lead):
        sums[pl.ds(pl.multiple_of(lead * SIDE, SIDE), SIDE), :] = zeros64

    for_leads((WINDOW_ROWS + 2 * PAD) // SIDE, clear_sums)

    def clear_ends(lead):
        for start in (0, PAD + WINDOW_ROWS):
            window[pl.ds(pl.multiple_of(start + lead * SIDE, SIDE), SIDE), :] = zeros64

    for_leads(PAD // SIDE, clear_ends)

    for field in (source3, even3, odd3, source8, even8, odd8):
        rows = field.shape[1]
        field[0] = jnp.zeros((rows, LANES), jnp.float32)

        def clear_edge(lead, field=field, rows=rows):
            edge = jnp.zeros((8, LANES), jnp.float32)
            field[lead, pl.ds(0, 8), :] = edge
            field[lead, pl.ds(rows - 8, 8), :] = edge

        for_leads(HALF + 2, clear_edge)

    from_lane = lax.broadcasted_iota(jnp.int32, (LANES, LANES), 0)
    to_lane = lax.broadcasted_iota(jnp.int32, (LANES, LANES), 1)
    swap = jnp.abs(to_lane - from_lane) == SIDE
    step = (jnp.abs(to_lane - from_lane) == 1) & ((to_lane < SIDE) == (from_lane < SIDE))
    for start in (0, LANES):
        near[start : start + LANES, :LANES] = one_where(step | swap)
        near[start : start + LANES, LANES:] = one_where(swap)

    def clear_grid(lead):
        start = pl.multiple_of(lead * GRID_ROWS, 8)
        grid[pl.ds(start, GRID_ROWS), :] = jnp.zeros((GRID_ROWS, LANES), jnp.float32)

    for_leads(GRID_ROWS, clear_grid)

    for (step_x, step_y), piece, copy in zip(STEPS, pieces, incoming):
        base, rows, leads = place_of(step_x, step_y)

        def widen(lead, base=base, rows=rows, leads=leads, piece=piece):
            lanes = pl.ds(pl.multiple_of(lead * LANES, LANES), LANES)
            if rows == RIM:
                both = piece[:, lanes].astype(jnp.float32)
            for k in range(2):
                start = pl.multiple_of(PAD + base + k * leads * rows + lead * rows, 8)
                if rows == RIM:
                    value = both[k * RIM : (k + 1) * RIM]
                else:
                    value = piece[k, :, lanes].astype(jnp.float32)
                window[pl.ds(start, rows), :] = value

        copy.wait()
        for_leads(leads, widen)

    weights = sweep_weights(SWEEPS)
    diagonal = 6.0 + screen_mass
    scale = [weight / diagonal for weight in weights]
    keep = [(1.0 - weight) / part for weight, part in zip(weights, scale)]
    total_scale = coupling * scale[0] * scale[1] * scale[2] * scale[3]

    def pair_step(slot, carry):
        first = pairs[0, slot]
        second = pairs[1, slot]
        first_k = lax.rem(first, 2)
        second_k = lax.rem(second, 2)
        holder = lax.div(second, 2)
        step_x = lax.rem(lax.div(holder, mesh_y) - here_x + 1 + mesh_x, mesh_x) - 1
        step_y = lax.rem(lax.rem(holder, mesh_y) - here_y + 1 + mesh_y, mesh_y) - 1
        shift_x = anchors[0, second] - anchors[0, first]
        shift_y = anchors[1, second] - anchors[1, first]
        shift_z = anchors[2, second] - anchors[2, first]
        shift_x = shift_x + jnp.where(shift_x < -(span_x // 2), span_x, 0) - jnp.where(
            shift_x >= span_x // 2, span_x, 0
        )
        shift_y = shift_y + jnp.where(shift_y < -(span_y // 2), span_y, 0) - jnp.where(
            shift_y >= span_y // 2, span_y, 0
        )
        half_y = lax.shift_right_arithmetic(shift_y, 1)
        odd_y = shift_y - 2 * half_y
        side_x = step_x != 0
        side_y = step_y != 0
        stride = jnp.where(side_x, RIM, SIDE)
        leads = jnp.where(side_y, RIM_LEADS, HALF)
        plus_x = jnp.where(step_x > 0, 1, 0)
        plus_y = jnp.where(step_y > 0, 1, 0)
        base = jnp.where(
            side_x,
            jnp.where(
                side_y,
                BASE_C + (2 * plus_x + plus_y) * (2 * RIM_LEADS * RIM),
                BASE_X + plus_x * (2 * HALF * RIM),
            ),
            jnp.where(side_y, BASE_Y + plus_y * (2 * RIM_LEADS * SIDE), 0),
        )
        base = base + second_k * leads * stride
        start_x = plus_x * LOW
        start_lead = plus_y * LOW_LEADS
        origin_x = jnp.where(step_x < 0, LOW, 0)
        origin_lead = jnp.where(step_y < 0, LOW_LEADS, 0)
        far_start = PAD + base + (start_lead - half_y - origin_lead) * stride + start_x - shift_x - origin_x
        own_start = first_k * (HALF * SIDE) + start_lead * SIDE + start_x
        from_lane = lax.broadcasted_iota(jnp.int32, (LANES, LANES), 0)
        to_lane = lax.broadcasted_iota(jnp.int32, (LANES, LANES), 1)
        apart = to_lane - from_lane - shift_z
        depth = lax.rem(to_lane, SIDE) - shift_z
        valid = (depth >= 0) & (depth < SIDE)
        same = valid & (apart == SIDE * odd_y)
        other = valid & (apart == -SIDE) & (odd_y == 1)
        turn_in[:LANES] = one_where(same)
        turn_in[LANES:] = one_where(other)
        from_lane, to_lane = to_lane, from_lane
        apart = to_lane - from_lane - shift_z
        depth = lax.rem(to_lane, SIDE) - shift_z
        valid = (depth >= 0) & (depth < SIDE)
        same = one_where(valid & (apart == SIDE * odd_y))
        other = one_where(valid & (apart == -SIDE) & (odd_y == 1))
        turn_out[:LANES, :LANES] = same
        turn_out[LANES:, :LANES] = same
        turn_out[:LANES, LANES:] = other
        turn_out[LANES:, LANES:] = other

        def run(tiles, leads, chunk, moved, source, even, odd):
            rows = tiles * 8
            inner = pl.ds(8, rows)
            lane = lane_index(rows)
            upper = lane >= SIDE
            row = lax.broadcasted_iota(jnp.int32, (rows, LANES), 0) + start_x
            column_part = jnp.where(upper, 1, 0) - shift_y
            inside_x = (row >= shift_x) & (row < SIDE + shift_x)

            def inside(lead):
                column = column_part + 2 * lead
                return inside_x & (column >= 0) & (column < SIDE)

            def far_rows(lead):
                return pl.ds(far_start + lead * stride, rows)

            def own_rows(lead):
                return pl.ds(pl.multiple_of(PAD + own_start + lead * SIDE, 8), rows)

            def part(value, index):
                return value[index * rows : (index + 1) * rows]

            def build(index):
                lead = index * chunk
                loads = [window[far_rows(lead + j), :] for j in range(-1, chunk)]
                now = jnp.concatenate(loads[1:], 0).astype(jnp.bfloat16)
                before = jnp.concatenate(loads[:-1], 0).astype(jnp.bfloat16)
                turned = jnp.dot(
                    jnp.concatenate([now, before], 1), turn_in[...], preferred_element_type=jnp.float32
                )
                for j in range(chunk):
                    piece = jnp.where(inside(start_lead + lead + j), part(turned, j), 0.0)
                    moved[lead + j] = piece
                    source[lead + j + 1, inner, :] = piece * window[own_rows(lead + j), :]

            def near_fields(field, lead):
                values = [field[lead + j, inner, :] for j in range(chunk + 2)]
                product = jnp.dot(
                    halves(jnp.concatenate(values, 0)), near[...], preferred_element_type=jnp.float32
                )
                for j in range(chunk):
                    across = jnp.where(
                        upper, part(product, j + 2)[:, LANES:], part(product, j)[:, LANES:]
                    )
                    beside = field[lead + j + 1, pl.ds(7, rows), :] + field[lead + j + 1, pl.ds(9, rows), :]
                    yield values[j + 1], (part(product, j + 1)[:, :LANES] + across) + beside

            def sweep(old, new, own_part, source_part):
                def body(index):
                    lead = index * chunk
                    for j, (here, near_sum) in enumerate(near_fields(old, lead)):
                        value = own_part * here + near_sum
                        if source_part is not None:
                            value = value + source_part * source[lead + j + 1, inner, :]
                        new[lead + j + 1, inner, :] = value

                return body

            def finish(index):
                lead = index * chunk
                back = []
                for j, (here, near_sum) in enumerate(near_fields(odd, lead)):
                    value = keep[3] * here + near_sum
                    value = value + (1.0 / (scale[0] * scale[1] * scale[2])) * source[lead + j + 1, inner, :]
                    value = value * total_scale
                    sums[own_rows(lead + j), :] = sums[own_rows(lead + j), :] + value * moved[lead + j]
                    back.append(
                        jnp.where(inside(start_lead + lead + j), value * window[own_rows(lead + j), :], 0.0)
                    )
                turned = jnp.dot(
                    halves(jnp.concatenate(back, 0)), turn_out[...], preferred_element_type=jnp.float32
                )
                targets = [sums[far_rows(lead + j), :] for j in range(-1, chunk)]
                for j in range(-1, chunk):
                    total = targets[j + 1]
                    if j >= 0:
                        total = total + part(turned, j)[:, :LANES]
                    if j + 1 < chunk:
                        total = total + part(turned, j + 1)[:, LANES:]
                    targets[j + 1] = total
                for j in range(-1, chunk):
                    sums[far_rows(lead + j), :] = targets[j + 1]

            edge = jnp.zeros((rows, LANES), jnp.float32)
            for field in (source, even, odd):
                field[leads + 1, inner, :] = edge
            chunks = leads // chunk
            for_leads(chunks, build)
            for_leads(chunks, sweep(source, even, keep[1] + 1.0 / scale[0], None))
            for_leads(chunks, sweep(even, odd, keep[2], 1.0 / (scale[0] * scale[1])))
            for_leads(chunks, finish)

        for has_x, has_y, chunk in CHUNKS:
            narrow = side_x if has_x else jnp.logical_not(side_x)
            narrow = narrow & (side_y if has_y else jnp.logical_not(side_y))
            fields = (moved3, source3, even3, odd3) if has_x else (moved8, source8, even8, odd8)

            @pl.when(narrow)
            def _(has_x=has_x, has_y=has_y, chunk=chunk, fields=fields):
                run(
                    (RIM if has_x else SIDE) // 8,
                    RIM_LEADS if has_y else HALF,
                    chunk,
                    *fields,
                )

        return carry

    lax.fori_loop(0, count[0], pair_step, 0)

    own_copy = pltpu.make_async_copy(sums.at[pl.ds(PAD, BASE_X)], own_out, copies.at[0])
    own_copy.start()

    outgoing = []
    for (step_x, step_y), out, target in zip(STEPS[1:], outs, targets_out):
        base, rows, leads = place_of(step_x, step_y)

        def narrow(lead, base=base, rows=rows, leads=leads, out=out):
            lanes = pl.ds(pl.multiple_of(lead * LANES, LANES), LANES)
            values = []
            for k in range(2):
                start = pl.multiple_of(PAD + base + k * leads * rows + lead * rows, 8)
                values.append(sums[pl.ds(start, rows), :])
            if rows == RIM:
                out[:, lanes] = jnp.concatenate(values, 0).astype(out.dtype)
            else:
                for k in range(2):
                    out[k, :, lanes] = values[k].astype(out.dtype)

        for_leads(leads, narrow)
        copy = pltpu.make_async_copy(out, target, copies.at[11 + len(outgoing)])
        copy.start()
        outgoing.append(copy)

    slab = SIDE - 16

    def deposit(step_x, step_y, k, base, rows, leads):
        holder_x = lax.rem(here_x + step_x + mesh_x, mesh_x)
        holder_y = lax.rem(here_y + step_y + mesh_y, mesh_y)
        orbit = (holder_x * mesh_y + holder_y) * 2 + k
        at_x = anchors[0, orbit] - holder_x * slab
        at_y = anchors[1, orbit] - holder_y * slab
        at_z = anchors[2, orbit]
        row = at_x + step_x * slab + GRID_PAD + jnp.where(step_x < 0, LOW, 0)
        column = at_y + step_y * slab + GRID_PAD + jnp.where(step_y < 0, LOW, 0)
        start = column * GRID_ROWS + row
        from_lane = lax.broadcasted_iota(jnp.int32, (LANES, LANES), 0)
        apart = lax.broadcasted_iota(jnp.int32, (LANES, LANES), 1) - from_lane - at_z
        low = one_where((from_lane < SIDE) & (apart == 0))
        high = one_where((from_lane >= SIDE) & (apart == -SIDE))
        place[:, :LANES] = low
        place[:, LANES:] = high
        block = 16
        for first in range(0, leads, block):
            size = min(block, leads - first)
            value = window[pl.ds(pl.multiple_of(PAD + base + first * rows, 8), size * rows), :]
            placed = jnp.dot(value.astype(jnp.bfloat16), place[...], preferred_element_type=jnp.float32)
            for j in range(size):
                for odd_column in (0, 1):
                    at = pl.ds(start + (2 * (first + j) + odd_column) * GRID_ROWS, rows)
                    part = placed[j * rows : (j + 1) * rows, odd_column * LANES : (odd_column + 1) * LANES]
                    grid[at, :] = grid[at, :] + part * part

    for k in range(2):
        deposit(0, 0, k, k * HALF * SIDE, SIDE, HALF)

    def deposit_x(index, carry):
        deposit(2 * (index // 2) - 1, 0, lax.rem(index, 2), BASE_X + index * (HALF * RIM), RIM, HALF)
        return carry

    def deposit_y(index, carry):
        deposit(
            0, 2 * (index // 2) - 1, lax.rem(index, 2), BASE_Y + index * (RIM_LEADS * SIDE), SIDE, RIM_LEADS
        )
        return carry

    def deposit_corner(index, carry):
        deposit(
            2 * (index // 4) - 1,
            2 * lax.rem(index // 2, 2) - 1,
            lax.rem(index, 2),
            BASE_C + index * (RIM_LEADS * RIM),
            RIM,
            RIM_LEADS,
        )
        return carry

    lax.fori_loop(0, 4, deposit_x, 0)
    lax.fori_loop(0, 4, deposit_y, 0)
    lax.fori_loop(0, 8, deposit_corner, 0)
    grid_copy = pltpu.make_async_copy(grid.at[pl.ds(GRID_PAD * GRID_ROWS, EDGE_ROWS)], grid_out, copies.at[1])
    grid_copy.start()
    for copy in [own_copy, *outgoing, grid_copy]:
        copy.wait()


GRID_PAD = 8
GRID_ROWS = 88
EDGE = SIDE - 16 + RIM
EDGE_ROWS = (EDGE + 1) * GRID_ROWS
hbm = pl.BlockSpec(memory_space=pl.ANY)
MESH = pl.DeviceIdType.MESH

smem = pl.BlockSpec(memory_space=pltpu.SMEM)
vmem = pl.BlockSpec(memory_space=pltpu.VMEM)


def pairs_call(mesh_x, mesh_y, flat_anchors, flat_pairs, flat_count, pieces):
    term_shapes = [
        jax.ShapeDtypeStruct((BASE_X, LANES), jnp.float32),
        jax.ShapeDtypeStruct((EDGE_ROWS, LANES), jnp.float32),
    ] + [jax.ShapeDtypeStruct(piece.shape, jnp.bfloat16) for piece in pieces[1:]]

    def field(rows):
        return pltpu.VMEM((HALF + 2, rows, LANES), jnp.float32)

    return pl.pallas_call(
        functools.partial(pair_kernel, mesh_x, mesh_y),
        out_shape=term_shapes,
        in_specs=[smem] * 3 + [hbm] * 9,
        out_specs=[hbm] * 10,
        scratch_shapes=[
            pltpu.VMEM((WINDOW_ROWS + 2 * PAD, LANES), jnp.float32),
            pltpu.VMEM((WINDOW_ROWS + 2 * PAD, LANES), jnp.float32),
            pltpu.VMEM((2 * LANES, 2 * LANES), jnp.bfloat16),
            pltpu.VMEM((2 * LANES, LANES), jnp.bfloat16),
            pltpu.VMEM((2 * LANES, 2 * LANES), jnp.bfloat16),
            pltpu.VMEM((HALF, RIM, LANES), jnp.float32),
            field(RIM + 16),
            field(RIM + 16),
            field(RIM + 16),
            pltpu.VMEM((HALF, SIDE, LANES), jnp.float32),
            field(SIDE + 16),
            field(SIDE + 16),
            field(SIDE + 16),
            pltpu.VMEM((GRID_ROWS * GRID_ROWS, LANES), jnp.float32),
            pltpu.VMEM((LANES, 2 * LANES), jnp.bfloat16),
            pltpu.SemaphoreType.DMA((19,)),
        ]
        + [pltpu.VMEM(piece.shape, jnp.bfloat16) for piece in pieces]
        + [pltpu.VMEM(piece.shape, jnp.bfloat16) for piece in pieces[1:]],
        compiler_params=pltpu.CompilerParams(vmem_limit_bytes=64 * 1024 * 1024),
        cost_estimate=pl.CostEstimate(flops=40_000_000, bytes_accessed=8_000_000, transcendentals=0),
        name="pair_terms",
    )(flat_anchors, flat_pairs, flat_count, *pieces)


def cube_root(value):
    inverse = jnp.exp(jnp.log(value) * (-1.0 / 3.0))
    inverse = inverse * (4.0 - value * inverse * inverse * inverse) * (1.0 / 3.0)
    return value * inverse * inverse


def greet(mesh_x, mesh_y, diagonal=False):
    here_x = lax.axis_index("gx")
    here_y = lax.axis_index("gy")
    left = (lax.rem(here_x + mesh_x - 1, mesh_x), here_y)
    right = (lax.rem(here_x + 1, mesh_x), here_y)
    below = (here_x, lax.rem(here_y + mesh_y - 1, mesh_y))
    above = (here_x, lax.rem(here_y + 1, mesh_y))
    barrier = pltpu.get_barrier_semaphore()
    neighbours = [left, right, below, above]
    if diagonal:
        neighbours += [(left[0], below[1]), (right[0], above[1])]
    for neighbour in neighbours:
        pl.semaphore_signal(barrier, inc=1, device_id=neighbour, device_id_type=MESH)
    pl.semaphore_wait(barrier, len(neighbours))
    return left, right, below, above


def gather_kernel(mesh_x, mesh_y, own, core_source, *refs):
    outs = refs[:8]
    narrow_outs = refs[8:11]
    send_low, send_high, core, narrow_x, narrow_y, sent, landed, copies = refs[11:]
    core_copy = pltpu.make_async_copy(core_source, core, copies.at[3])
    core_copy.start()
    left, right, below, above = greet(mesh_x, mesh_y)
    started = []

    def send(source, slot, device):
        copy = pltpu.make_async_remote_copy(
            src_ref=source,
            dst_ref=outs[slot],
            send_sem=sent.at[slot],
            recv_sem=landed.at[slot],
            device_id=device,
            device_id_type=MESH,
        )
        copy.start()
        started.append(copy)
        return copy

    def prepare(lead):
        lanes = pl.ds(pl.multiple_of(lead * LANES, LANES), LANES)
        values = [own[k, :, lanes].astype(jnp.float32) for k in range(2)]
        send_low[:, lanes] = jnp.concatenate([value[:RIM] for value in values], 0).astype(jnp.bfloat16)
        send_high[:, lanes] = jnp.concatenate([value[LOW:] for value in values], 0).astype(jnp.bfloat16)

    for_leads(HALF, prepare)
    from_left = send(send_high, 0, right)
    from_right = send(send_low, 1, left)
    high = pl.ds(LOW * SIDE, RIM * SIDE)
    low = pl.ds(0, RIM * SIDE)
    send(own.at[:, :, high], 2, above)
    send(own.at[:, :, low], 3, below)
    core_copy.wait()

    def narrow(row):
        narrow_x[row] = core[row].astype(jnp.bfloat16)
        narrow_y[row] = jnp.concatenate([core[2 * row, :RIM], core[2 * row + 1, :RIM]], 0).astype(jnp.bfloat16)

    for_leads(RIM, narrow)
    narrow_copies = [
        pltpu.make_async_copy(source, target, copies.at[index])
        for index, (source, target) in enumerate(
            zip((narrow_x, narrow_y, narrow_y.at[pl.ds(0, RIM // 2)]), narrow_outs)
        )
    ]
    for copy in narrow_copies:
        copy.start()
    from_left.wait_recv()
    send(outs[0].at[:, high], 4, above)
    send(outs[0].at[:, low], 5, below)
    from_right.wait_recv()
    send(outs[1].at[:, high], 6, above)
    send(outs[1].at[:, low], 7, below)
    for copy in started:
        copy.wait_send()
    for copy in started[2:]:
        copy.wait_recv()
    for copy in narrow_copies:
        copy.wait()


def return_kernel(mesh_x, mesh_y, anchors, *refs):
    side_sources = refs[:2]
    column_terms = refs[2:4]
    corner_terms = refs[4:8]
    outs = refs[14:18]
    applied_out, potential_out = refs[18:20]
    landed_corners, send_left, send_right, left_terms, right_terms = refs[20:25]
    loads = refs[25:31]
    density, core, core_x, core_y, core_xy, own = loads
    potential, applied, sent, landed, copies = refs[31:]
    here_x = lax.axis_index("gx")
    here_y = lax.axis_index("gy")
    incoming = [
        pltpu.make_async_copy(source, target, copies.at[index])
        for index, (source, target) in enumerate(
            zip(refs[8:14] + side_sources, loads + (left_terms, right_terms))
        )
    ]
    left, right, below, above = greet(mesh_x, mesh_y)

    def send(source, target, slot, device):
        copy = pltpu.make_async_remote_copy(
            src_ref=source,
            dst_ref=target,
            send_sem=sent.at[slot],
            recv_sem=landed.at[slot],
            device_id=device,
            device_id_type=MESH,
        )
        copy.start()
        return copy

    corners = [
        send(corner_terms[slot], landed_corners.at[slot], slot, device)
        for slot, device in enumerate((below, above, below, above))
    ]
    others = [
        send(column_terms[0], outs[2], 4, below),
        send(column_terms[1], outs[3], 5, above),
    ]
    for copy in incoming:
        copy.start()
    for copy in incoming:
        copy.wait()
    slab = core.shape[0]

    def finish_at(row, column, core_part):
        at = pl.ds(column * GRID_ROWS + GRID_PAD + row, 8, stride=GRID_ROWS)
        value = -xc_factor * cube_root(density[at, :] + core_part)
        density[at, :] = value
        return value

    def own_rows(row):
        for column in range(0, slab, 8):
            potential[row, pl.ds(column, 8), :] = finish_at(row, column, core[row, pl.ds(column, 8), :])

    def right_rows(row):
        beside = core_x[row].astype(jnp.float32)
        for column in range(0, slab, 8):
            finish_at(slab + row, column, beside[column : column + 8])

    def above_rows(pair, source=core_y, beyond=0):
        part = source[pair].astype(jnp.float32)
        for j in range(2):
            for column in range(0, RIM, 8):
                start = j * RIM + column
                finish_at(beyond + 2 * pair + j, slab + column, part[start : start + 8])

    def corner_rows(pair):
        above_rows(pair, source=core_xy, beyond=slab)

    for_leads(slab, own_rows)
    potential_copy = pltpu.make_async_copy(potential, potential_out, copies.at[8])
    potential_copy.start()
    for_leads(RIM, right_rows)
    for copy in corners:
        copy.wait_recv()

    for side, (terms, target) in enumerate(((left_terms, send_left), (right_terms, send_right))):

        def merge(lead, corner, shift, terms=terms, target=target):
            lanes = pl.ds(pl.multiple_of(lead * LANES, LANES), LANES)
            value = terms[:, lanes]
            if corner is not None:
                part = pl.ds(pl.multiple_of((lead - shift) * LANES, LANES), LANES)
                value = value.astype(jnp.float32) + landed_corners[corner, :, part].astype(jnp.float32)
            target[:, lanes] = value.astype(jnp.bfloat16)

        for first, last, corner in (
            (0, RIM_LEADS, 2 * side + 1),
            (RIM_LEADS, LOW_LEADS, None),
            (LOW_LEADS, HALF, 2 * side),
        ):

            def part_step(index, first=first, corner=corner, merge=merge):
                merge(index + first, corner, first)

            for_leads(last - first, part_step)
        others.append(send(target, outs[side], 6 + side, (left, right)[side]))
    for_leads(slab // 2, above_rows)
    for_leads(RIM // 2, corner_rows)

    lane = lane_index(SIDE)
    orbit = (here_x * mesh_y + here_y) * 2
    for k in range(2):
        at_x = jnp.clip(anchors[0, orbit + k] - here_x * slab, 0, GRID_PAD - 1)
        at_y = jnp.clip(anchors[1, orbit + k] - here_y * slab, 0, GRID_PAD - 1)
        at_z = anchors[2, orbit + k]
        start = at_y * GRID_ROWS + at_x + GRID_PAD
        turn_low = lax.rem(LANES - at_z, LANES)
        turn_high = lax.rem(LANES + SIDE - at_z, LANES)

        def sample(lead, k=k, start=start, turn_low=turn_low, turn_high=turn_high):
            lanes = pl.ds(pl.multiple_of(lead * LANES, LANES), LANES)
            low = density[pl.ds(start + 2 * lead * GRID_ROWS, SIDE), :]
            high = density[pl.ds(start + (2 * lead + 1) * GRID_ROWS, SIDE), :]
            sampled = jnp.where(lane < SIDE, pltpu.roll(low, turn_low, 1), pltpu.roll(high, turn_high, 1))
            at = pl.ds(pl.multiple_of((k * HALF + lead) * SIDE, SIDE), SIDE)
            applied[at, :] = sampled * own[k, :, lanes].astype(jnp.float32)

        for_leads(HALF, sample)
    applied_copy = pltpu.make_async_copy(applied, applied_out, copies.at[9])
    applied_copy.start()
    for copy in corners:
        copy.wait_send()
    for copy in others:
        copy.wait()
    applied_copy.wait()
    potential_copy.wait()


def action_kernel(applied, own_terms, from_right, from_left, from_above, from_below, potential_source, action, potential, copied):
    copy = pltpu.make_async_copy(potential_source, potential, copied.at[0])
    copy.start()

    def apply(lead, column=None, shift=0):
        lanes = pl.ds(pl.multiple_of(lead * LANES, LANES), LANES)
        high_rows = from_right[:, lanes].astype(jnp.float32)
        low_rows = from_left[:, lanes].astype(jnp.float32)
        for k in range(2):
            at = pl.ds(pl.multiple_of((k * HALF + lead) * SIDE, SIDE), SIDE)
            terms = own_terms[at, :]
            if column is not None:
                part = pl.ds(pl.multiple_of((lead - shift) * LANES, LANES), LANES)
                terms = terms + column[k, :, part].astype(jnp.float32)
            rows = slice(k * RIM, (k + 1) * RIM)
            terms = jnp.concatenate(
                [terms[:RIM] + low_rows[rows], terms[RIM:LOW], terms[LOW:] + high_rows[rows]], 0
            )
            action[k, :, lanes] = applied[at, :] - exx_share * terms

    for start, stop, column in ((0, RIM_LEADS, from_below), (RIM_LEADS, LOW_LEADS, None), (LOW_LEADS, HALF, from_above)):

        def part_step(index, start=start, column=column):
            apply(index + start, column=column, shift=start)

        for_leads(stop - start, part_step)
    copy.wait()


def shape_of(dims, dtype=jnp.bfloat16):
    return jax.ShapeDtypeStruct(dims, dtype)


def local(orbitals, anchors, pair_list, pair_count, core_density):
    mesh_x = lax.axis_size("gx")
    mesh_y = lax.axis_size("gy")
    own = orbitals[0, 0]
    flat_anchors = anchors.T
    flat_pairs = pair_list[0, 0].T
    flat_count = pair_count.reshape(-1)
    side_shape = shape_of((2 * RIM, FLAT))
    column_shape = shape_of((2, SIDE, RIM * SIDE))
    corner_shape = shape_of((2 * RIM, RIM * SIDE))
    around = [side_shape] * 2 + [column_shape] * 2 + [corner_shape] * 4

    core_shape = core_density.shape
    narrow_shapes = [
        (RIM, core_shape[1], LANES),
        (core_shape[0] // 2, 2 * RIM, LANES),
        (RIM // 2, 2 * RIM, LANES),
    ]
    grant = 64 * 1024 * 1024

    gathered = pl.pallas_call(
        functools.partial(gather_kernel, mesh_x, mesh_y),
        out_shape=around + [shape_of(dims) for dims in narrow_shapes],
        in_specs=[vmem, hbm],
        out_specs=[hbm] * 11,
        scratch_shapes=[
            pltpu.VMEM(side_shape.shape, jnp.bfloat16),
            pltpu.VMEM(side_shape.shape, jnp.bfloat16),
            pltpu.VMEM(core_shape, jnp.float32),
            pltpu.VMEM(narrow_shapes[0], jnp.bfloat16),
            pltpu.VMEM(narrow_shapes[1], jnp.bfloat16),
            pltpu.SemaphoreType.DMA((8,)),
            pltpu.SemaphoreType.DMA((8,)),
            pltpu.SemaphoreType.DMA((4,)),
        ],
        compiler_params=pltpu.CompilerParams(
            collective_id=0, has_side_effects=True, vmem_limit_bytes=grant
        ),
        name="gather_rims",
    )(own, core_density)
    pieces = gathered[:8]

    back_x = [((i + 1) % mesh_x, i) for i in range(mesh_x)]
    back_y = [((i + 1) % mesh_y, i) for i in range(mesh_y)]
    back_xy = [
        ((i + 1) % mesh_x * mesh_y + (j + 1) % mesh_y, i * mesh_y + j)
        for i in range(mesh_x)
        for j in range(mesh_y)
    ]
    core_rims = [
        lax.ppermute(gathered[8], "gx", back_x),
        lax.ppermute(gathered[9], "gy", back_y),
        lax.ppermute(gathered[10], ("gx", "gy"), back_xy),
    ]

    terms = pairs_call(mesh_x, mesh_y, flat_anchors, flat_pairs, flat_count, [own] + list(pieces))
    grid_shape = terms[1].shape
    *returned, applied, potential = pl.pallas_call(
        functools.partial(return_kernel, mesh_x, mesh_y),
        out_shape=[side_shape] * 2
        + [column_shape] * 2
        + [shape_of((BASE_X, LANES), jnp.float32), shape_of(core_shape, jnp.float32)],
        in_specs=[smem] + [hbm] * 14,
        out_specs=[hbm] * 6,
        scratch_shapes=[
            pltpu.VMEM((4,) + corner_shape.shape, jnp.bfloat16),
            pltpu.VMEM(side_shape.shape, jnp.bfloat16),
            pltpu.VMEM(side_shape.shape, jnp.bfloat16),
            pltpu.VMEM(side_shape.shape, jnp.bfloat16),
            pltpu.VMEM(side_shape.shape, jnp.bfloat16),
            pltpu.VMEM(grid_shape, jnp.float32),
            pltpu.VMEM(core_shape, jnp.float32),
            pltpu.VMEM(narrow_shapes[0], jnp.bfloat16),
            pltpu.VMEM(narrow_shapes[1], jnp.bfloat16),
            pltpu.VMEM(narrow_shapes[2], jnp.bfloat16),
            pltpu.VMEM(own.shape, jnp.bfloat16),
            pltpu.VMEM(core_shape, jnp.float32),
            pltpu.VMEM((BASE_X, LANES), jnp.float32),
            pltpu.SemaphoreType.DMA((8,)),
            pltpu.SemaphoreType.DMA((8,)),
            pltpu.SemaphoreType.DMA((10,)),
        ],
        compiler_params=pltpu.CompilerParams(
            collective_id=1, has_side_effects=True, vmem_limit_bytes=grant
        ),
        name="return_terms",
    )(flat_anchors, *terms[2:], terms[1], core_density, *core_rims, own)
    action, potential = pl.pallas_call(
        action_kernel,
        out_shape=[shape_of(own.shape, jnp.float32), shape_of(core_shape, jnp.float32)],
        in_specs=[vmem] * 6 + [hbm],
        out_specs=[vmem, hbm],
        scratch_shapes=[pltpu.SemaphoreType.DMA((1,))],
        compiler_params=pltpu.CompilerParams(vmem_limit_bytes=grant),
        name="action_terms",
    )(applied, terms[0], *returned, potential)
    return (action.reshape(orbitals.shape), potential)


def solution(mesh):
    placed = (
        P("gx", "gy", None, None, None),
        P(),
        P("gx", "gy", None, None),
        P("gx", "gy"),
        P("gx", "gy", None),
    )
    return jax.shard_map(
        local,
        mesh=mesh,
        in_specs=placed,
        out_specs=(P("gx", "gy", None, None, None), P("gx", "gy", None)),
        check_vma=False,
    )
```

```python
import functools
import math

import jax
import jax.numpy as jnp
from jax import lax
from jax.experimental import pallas as pl
from jax.experimental.pallas import tpu as pltpu
from jax.sharding import PartitionSpec as P

SWEEPS = 4
SIDE = 64
HALF = SIDE // 2
FLAT = SIDE * SIDE
RIM = 24
LOW = SIDE - RIM
RIM_LEADS = RIM // 2
LOW_LEADS = LOW // 2
LANES = 128
PAD = 512
CHUNKS = [(False, False, 32), (True, False, 32), (False, True, 12), (True, True, 12)]

screen_mass = 0.25
coupling = 2.0 * math.pi
exx_share = 0.25
xc_factor = (3.0 / math.pi) ** (1.0 / 3.0)

BASE_X = 2 * HALF * SIDE
BASE_Y = BASE_X + 4 * HALF * RIM
BASE_C = BASE_Y + 4 * RIM_LEADS * SIDE
WINDOW_ROWS = BASE_C + 8 * RIM_LEADS * RIM
STEPS = [(0, 0), (-1, 0), (1, 0), (0, -1), (0, 1), (-1, -1), (-1, 1), (1, -1), (1, 1)]


def place_of(step_x, step_y):
    rows = SIDE if step_x == 0 else RIM
    leads = HALF if step_y == 0 else RIM_LEADS
    if step_x == 0 and step_y == 0:
        base = 0
    elif step_y == 0:
        base = BASE_X + (2 * HALF * RIM if step_x > 0 else 0)
    elif step_x == 0:
        base = BASE_Y + (2 * RIM_LEADS * SIDE if step_y > 0 else 0)
    else:
        base = BASE_C + ((2 if step_x > 0 else 0) + (1 if step_y > 0 else 0)) * 2 * RIM_LEADS * RIM
    return base, rows, leads


def sweep_weights(sweep_count):
    return [
        1.0 / (1.0 + 0.7 * math.cos(math.pi * (2 * order + 1) / (2 * sweep_count)))
        for order in range(sweep_count)
    ]


def lane_index(rows):
    return lax.broadcasted_iota(jnp.int32, (rows, LANES), 1)


def one_where(condition):
    return jnp.where(condition, 1.0, 0.0).astype(jnp.bfloat16)


def halves(value):
    upper = value.astype(jnp.bfloat16)
    lower = (value - upper.astype(jnp.float32)).astype(jnp.bfloat16)
    return jnp.concatenate([upper, lower], 1)


def for_leads(count, step):
    lax.fori_loop(0, count, lambda index, _: (step(index), 0)[1], 0)


def pair_kernel(mesh_x, mesh_y, anchors, pairs, count, *refs):
    sources = refs[:9]
    own_out, grid_out = refs[9:11]
    targets_out = refs[11:19]
    (
        window,
        sums,
        near,
        turn_in,
        turn_out,
        moved3,
        source3,
        even3,
        odd3,
        moved8,
        source8,
        even8,
        odd8,
        grid,
        place,
        copies,
    ) = refs[19:35]
    pieces = refs[35:44]
    outs = refs[44:52]
    here_x = lax.axis_index("gx")
    here_y = lax.axis_index("gy")
    span_x = mesh_x * (SIDE - 16)
    span_y = mesh_y * (SIDE - 16)

    incoming = [
        pltpu.make_async_copy(source, piece, copies.at[2 + index])
        for index, (source, piece) in enumerate(zip(sources, pieces))
    ]
    for copy in incoming:
        copy.start()
    zeros64 = jnp.zeros((SIDE, LANES), jnp.float32)

    def clear_sums(lead):
        sums[pl.ds(pl.multiple_of(lead * SIDE, SIDE), SIDE), :] = zeros64

    for_leads((WINDOW_ROWS + 2 * PAD) // SIDE, clear_sums)

    def clear_ends(lead):
        for start in (0, PAD + WINDOW_ROWS):
            window[pl.ds(pl.multiple_of(start + lead * SIDE, SIDE), SIDE), :] = zeros64

    for_leads(PAD // SIDE, clear_ends)

    for field in (source3, even3, odd3, source8, even8, odd8):
        rows = field.shape[1]
        field[0] = jnp.zeros((rows, LANES), jnp.float32)

        def clear_edge(lead, field=field, rows=rows):
            edge = jnp.zeros((8, LANES), jnp.float32)
            field[lead, pl.ds(0, 8), :] = edge
            field[lead, pl.ds(rows - 8, 8), :] = edge

        for_leads(HALF + 2, clear_edge)

    from_lane = lax.broadcasted_iota(jnp.int32, (LANES, LANES), 0)
    to_lane = lax.broadcasted_iota(jnp.int32, (LANES, LANES), 1)
    swap = jnp.abs(to_lane - from_lane) == SIDE
    step = (jnp.abs(to_lane - from_lane) == 1) & ((to_lane < SIDE) == (from_lane < SIDE))
    for start in (0, LANES):
        near[start : start + LANES, :LANES] = one_where(step | swap)
        near[start : start + LANES, LANES:] = one_where(swap)

    def clear_grid(lead):
        start = pl.multiple_of(lead * GRID_ROWS, 8)
        grid[pl.ds(start, GRID_ROWS), :] = jnp.zeros((GRID_ROWS, LANES), jnp.float32)

    for_leads(GRID_ROWS, clear_grid)

    for (step_x, step_y), piece, copy in zip(STEPS, pieces, incoming):
        base, rows, leads = place_of(step_x, step_y)

        def widen(lead, base=base, rows=rows, leads=leads, piece=piece):
            lanes = pl.ds(pl.multiple_of(lead * LANES, LANES), LANES)
            if rows == RIM:
                both = piece[:, lanes].astype(jnp.float32)
            for k in range(2):
                start = pl.multiple_of(PAD + base + k * leads * rows + lead * rows, 8)
                if rows == RIM:
                    value = both[k * RIM : (k + 1) * RIM]
                else:
                    value = piece[k, :, lanes].astype(jnp.float32)
                window[pl.ds(start, rows), :] = value

        copy.wait()
        for_leads(leads, widen)

    weights = sweep_weights(SWEEPS)
    diagonal = 6.0 + screen_mass
    scale = [weight / diagonal for weight in weights]
    keep = [(1.0 - weight) / part for weight, part in zip(weights, scale)]
    total_scale = coupling * scale[0] * scale[1] * scale[2] * scale[3]

    def pair_step(slot, carry):
        first = pairs[0, slot]
        second = pairs[1, slot]
        first_k = lax.rem(first, 2)
        second_k = lax.rem(second, 2)
        holder = lax.div(second, 2)
        step_x = lax.rem(lax.div(holder, mesh_y) - here_x + 1 + mesh_x, mesh_x) - 1
        step_y = lax.rem(lax.rem(holder, mesh_y) - here_y + 1 + mesh_y, mesh_y) - 1
        shift_x = anchors[0, second] - anchors[0, first]
        shift_y = anchors[1, second] - anchors[1, first]
        shift_z = anchors[2, second] - anchors[2, first]
        shift_x = shift_x + jnp.where(shift_x < -(span_x // 2), span_x, 0) - jnp.where(
            shift_x >= span_x // 2, span_x, 0
        )
        shift_y = shift_y + jnp.where(shift_y < -(span_y // 2), span_y, 0) - jnp.where(
            shift_y >= span_y // 2, span_y, 0
        )
        half_y = lax.shift_right_arithmetic(shift_y, 1)
        odd_y = shift_y - 2 * half_y
        side_x = step_x != 0
        side_y = step_y != 0
        stride = jnp.where(side_x, RIM, SIDE)
        leads = jnp.where(side_y, RIM_LEADS, HALF)
        plus_x = jnp.where(step_x > 0, 1, 0)
        plus_y = jnp.where(step_y > 0, 1, 0)
        base = jnp.where(
            side_x,
            jnp.where(
                side_y,
                BASE_C + (2 * plus_x + plus_y) * (2 * RIM_LEADS * RIM),
                BASE_X + plus_x * (2 * HALF * RIM),
            ),
            jnp.where(side_y, BASE_Y + plus_y * (2 * RIM_LEADS * SIDE), 0),
        )
        base = base + second_k * leads * stride
        start_x = plus_x * LOW
        start_lead = plus_y * LOW_LEADS
        origin_x = jnp.where(step_x < 0, LOW, 0)
        origin_lead = jnp.where(step_y < 0, LOW_LEADS, 0)
        far_start = PAD + base + (start_lead - half_y - origin_lead) * stride + start_x - shift_x - origin_x
        own_start = first_k * (HALF * SIDE) + start_lead * SIDE + start_x
        from_lane = lax.broadcasted_iota(jnp.int32, (LANES, LANES), 0)
        to_lane = lax.broadcasted_iota(jnp.int32, (LANES, LANES), 1)
        apart = to_lane - from_lane - shift_z
        depth = lax.rem(to_lane, SIDE) - shift_z
        valid = (depth >= 0) & (depth < SIDE)
        same = valid & (apart == SIDE * odd_y)
        other = valid & (apart == -SIDE) & (odd_y == 1)
        turn_in[:LANES] = one_where(same)
        turn_in[LANES:] = one_where(other)
        from_lane, to_lane = to_lane, from_lane
        apart = to_lane - from_lane - shift_z
        depth = lax.rem(to_lane, SIDE) - shift_z
        valid = (depth >= 0) & (depth < SIDE)
        same = one_where(valid & (apart == SIDE * odd_y))
        other = one_where(valid & (apart == -SIDE) & (odd_y == 1))
        turn_out[:LANES, :LANES] = same
        turn_out[LANES:, :LANES] = same
        turn_out[:LANES, LANES:] = other
        turn_out[LANES:, LANES:] = other

        def run(tiles, leads, chunk, moved, source, even, odd):
            rows = tiles * 8
            inner = pl.ds(8, rows)
            lane = lane_index(rows)
            upper = lane >= SIDE
            row = lax.broadcasted_iota(jnp.int32, (rows, LANES), 0) + start_x
            column_part = jnp.where(upper, 1, 0) - shift_y
            inside_x = (row >= shift_x) & (row < SIDE + shift_x)

            def inside(lead):
                column = column_part + 2 * lead
                return inside_x & (column >= 0) & (column < SIDE)

            def far_rows(lead):
                return pl.ds(far_start + lead * stride, rows)

            def own_rows(lead):
                return pl.ds(pl.multiple_of(PAD + own_start + lead * SIDE, 8), rows)

            def part(value, index):
                return value[index * rows : (index + 1) * rows]

            def build(index):
                lead = index * chunk
                loads = [window[far_rows(lead + j), :] for j in range(-1, chunk)]
                now = jnp.concatenate(loads[1:], 0).astype(jnp.bfloat16)
                before = jnp.concatenate(loads[:-1], 0).astype(jnp.bfloat16)
                turned = jnp.dot(
                    jnp.concatenate([now, before], 1), turn_in[...], preferred_element_type=jnp.float32
                )
                for j in range(chunk):
                    piece = jnp.where(inside(start_lead + lead + j), part(turned, j), 0.0)
                    moved[lead + j] = piece
                    source[lead + j + 1, inner, :] = piece * window[own_rows(lead + j), :]

            def near_fields(field, lead):
                values = [field[lead + j, inner, :] for j in range(chunk + 2)]
                product = jnp.dot(
                    halves(jnp.concatenate(values, 0)), near[...], preferred_element_type=jnp.float32
                )
                for j in range(chunk):
                    across = jnp.where(
                        upper, part(product, j + 2)[:, LANES:], part(product, j)[:, LANES:]
                    )
                    beside = field[lead + j + 1, pl.ds(7, rows), :] + field[lead + j + 1, pl.ds(9, rows), :]
                    yield values[j + 1], (part(product, j + 1)[:, :LANES] + across) + beside

            def sweep(old, new, own_part, source_part):
                def body(index):
                    lead = index * chunk
                    for j, (here, near_sum) in enumerate(near_fields(old, lead)):
                        value = own_part * here + near_sum
                        if source_part is not None:
                            value = value + source_part * source[lead + j + 1, inner, :]
                        new[lead + j + 1, inner, :] = value

                return body

            def finish(index):
                lead = index * chunk
                back = []
                for j, (here, near_sum) in enumerate(near_fields(odd, lead)):
                    value = keep[3] * here + near_sum
                    value = value + (1.0 / (scale[0] * scale[1] * scale[2])) * source[lead + j + 1, inner, :]
                    value = value * total_scale
                    sums[own_rows(lead + j), :] = sums[own_rows(lead + j), :] + value * moved[lead + j]
                    back.append(
                        jnp.where(inside(start_lead + lead + j), value * window[own_rows(lead + j), :], 0.0)
                    )
                turned = jnp.dot(
                    halves(jnp.concatenate(back, 0)), turn_out[...], preferred_element_type=jnp.float32
                )
                targets = [sums[far_rows(lead + j), :] for j in range(-1, chunk)]
                for j in range(-1, chunk):
                    total = targets[j + 1]
                    if j >= 0:
                        total = total + part(turned, j)[:, :LANES]
                    if j + 1 < chunk:
                        total = total + part(turned, j + 1)[:, LANES:]
                    targets[j + 1] = total
                for j in range(-1, chunk):
                    sums[far_rows(lead + j), :] = targets[j + 1]

            edge = jnp.zeros((rows, LANES), jnp.float32)
            for field in (source, even, odd):
                field[leads + 1, inner, :] = edge
            chunks = leads // chunk
            for_leads(chunks, build)
            for_leads(chunks, sweep(source, even, keep[1] + 1.0 / scale[0], None))
            for_leads(chunks, sweep(even, odd, keep[2], 1.0 / (scale[0] * scale[1])))
            for_leads(chunks, finish)

        for has_x, has_y, chunk in CHUNKS:
            narrow = side_x if has_x else jnp.logical_not(side_x)
            narrow = narrow & (side_y if has_y else jnp.logical_not(side_y))
            fields = (moved3, source3, even3, odd3) if has_x else (moved8, source8, even8, odd8)

            @pl.when(narrow)
            def _(has_x=has_x, has_y=has_y, chunk=chunk, fields=fields):
                run(
                    (RIM if has_x else SIDE) // 8,
                    RIM_LEADS if has_y else HALF,
                    chunk,
                    *fields,
                )

        return carry

    lax.fori_loop(0, count[0], pair_step, 0)

    own_copy = pltpu.make_async_copy(sums.at[pl.ds(PAD, BASE_X)], own_out, copies.at[0])
    own_copy.start()

    outgoing = []
    for (step_x, step_y), out, target in zip(STEPS[1:], outs, targets_out):
        base, rows, leads = place_of(step_x, step_y)

        def narrow(lead, base=base, rows=rows, leads=leads, out=out):
            lanes = pl.ds(pl.multiple_of(lead * LANES, LANES), LANES)
            values = []
            for k in range(2):
                start = pl.multiple_of(PAD + base + k * leads * rows + lead * rows, 8)
                values.append(sums[pl.ds(start, rows), :])
            if rows == RIM:
                out[:, lanes] = jnp.concatenate(values, 0).astype(out.dtype)
            else:
                for k in range(2):
                    out[k, :, lanes] = values[k].astype(out.dtype)

        for_leads(leads, narrow)
        copy = pltpu.make_async_copy(out, target, copies.at[11 + len(outgoing)])
        copy.start()
        outgoing.append(copy)

    slab = SIDE - 16

    def deposit(step_x, step_y, k, base, rows, leads):
        holder_x = lax.rem(here_x + step_x + mesh_x, mesh_x)
        holder_y = lax.rem(here_y + step_y + mesh_y, mesh_y)
        orbit = (holder_x * mesh_y + holder_y) * 2 + k
        at_x = anchors[0, orbit] - holder_x * slab
        at_y = anchors[1, orbit] - holder_y * slab
        at_z = anchors[2, orbit]
        row = at_x + step_x * slab + GRID_PAD + jnp.where(step_x < 0, LOW, 0)
        column = at_y + step_y * slab + GRID_PAD + jnp.where(step_y < 0, LOW, 0)
        start = column * GRID_ROWS + row
        from_lane = lax.broadcasted_iota(jnp.int32, (LANES, LANES), 0)
        apart = lax.broadcasted_iota(jnp.int32, (LANES, LANES), 1) - from_lane - at_z
        low = one_where((from_lane < SIDE) & (apart == 0))
        high = one_where((from_lane >= SIDE) & (apart == -SIDE))
        place[:, :LANES] = low
        place[:, LANES:] = high
        block = 16
        for first in range(0, leads, block):
            size = min(block, leads - first)
            value = window[pl.ds(pl.multiple_of(PAD + base + first * rows, 8), size * rows), :]
            placed = jnp.dot(value.astype(jnp.bfloat16), place[...], preferred_element_type=jnp.float32)
            for j in range(size):
                for odd_column in (0, 1):
                    at = pl.ds(start + (2 * (first + j) + odd_column) * GRID_ROWS, rows)
                    part = placed[j * rows : (j + 1) * rows, odd_column * LANES : (odd_column + 1) * LANES]
                    grid[at, :] = grid[at, :] + part * part

    for k in range(2):
        deposit(0, 0, k, k * HALF * SIDE, SIDE, HALF)

    def deposit_x(index, carry):
        deposit(2 * (index // 2) - 1, 0, lax.rem(index, 2), BASE_X + index * (HALF * RIM), RIM, HALF)
        return carry

    def deposit_y(index, carry):
        deposit(
            0, 2 * (index // 2) - 1, lax.rem(index, 2), BASE_Y + index * (RIM_LEADS * SIDE), SIDE, RIM_LEADS
        )
        return carry

    def deposit_corner(index, carry):
        deposit(
            2 * (index // 4) - 1,
            2 * lax.rem(index // 2, 2) - 1,
            lax.rem(index, 2),
            BASE_C + index * (RIM_LEADS * RIM),
            RIM,
            RIM_LEADS,
        )
        return carry

    lax.fori_loop(0, 4, deposit_x, 0)
    lax.fori_loop(0, 4, deposit_y, 0)
    lax.fori_loop(0, 8, deposit_corner, 0)
    grid_copy = pltpu.make_async_copy(grid.at[pl.ds(GRID_PAD * GRID_ROWS, EDGE_ROWS)], grid_out, copies.at[1])
    grid_copy.start()
    for copy in [own_copy, *outgoing, grid_copy]:
        copy.wait()


GRID_PAD = 8
GRID_ROWS = 88
EDGE = SIDE - 16 + RIM
EDGE_ROWS = (EDGE + 1) * GRID_ROWS
hbm = pl.BlockSpec(memory_space=pl.ANY)
MESH = pl.DeviceIdType.MESH

smem = pl.BlockSpec(memory_space=pltpu.SMEM)
vmem = pl.BlockSpec(memory_space=pltpu.VMEM)


def pairs_call(mesh_x, mesh_y, flat_anchors, flat_pairs, flat_count, pieces):
    term_shapes = [
        jax.ShapeDtypeStruct((BASE_X, LANES), jnp.float32),
        jax.ShapeDtypeStruct((EDGE_ROWS, LANES), jnp.float32),
    ] + [jax.ShapeDtypeStruct(piece.shape, jnp.bfloat16) for piece in pieces[1:]]

    def field(rows):
        return pltpu.VMEM((HALF + 2, rows, LANES), jnp.float32)

    return pl.pallas_call(
        functools.partial(pair_kernel, mesh_x, mesh_y),
        out_shape=term_shapes,
        in_specs=[smem] * 3 + [hbm] * 9,
        out_specs=[hbm] * 10,
        scratch_shapes=[
            pltpu.VMEM((WINDOW_ROWS + 2 * PAD, LANES), jnp.float32),
            pltpu.VMEM((WINDOW_ROWS + 2 * PAD, LANES), jnp.float32),
            pltpu.VMEM((2 * LANES, 2 * LANES), jnp.bfloat16),
            pltpu.VMEM((2 * LANES, LANES), jnp.bfloat16),
            pltpu.VMEM((2 * LANES, 2 * LANES), jnp.bfloat16),
            pltpu.VMEM((HALF, RIM, LANES), jnp.float32),
            field(RIM + 16),
            field(RIM + 16),
            field(RIM + 16),
            pltpu.VMEM((HALF, SIDE, LANES), jnp.float32),
            field(SIDE + 16),
            field(SIDE + 16),
            field(SIDE + 16),
            pltpu.VMEM((GRID_ROWS * GRID_ROWS, LANES), jnp.float32),
            pltpu.VMEM((LANES, 2 * LANES), jnp.bfloat16),
            pltpu.SemaphoreType.DMA((19,)),
        ]
        + [pltpu.VMEM(piece.shape, jnp.bfloat16) for piece in pieces]
        + [pltpu.VMEM(piece.shape, jnp.bfloat16) for piece in pieces[1:]],
        compiler_params=pltpu.CompilerParams(vmem_limit_bytes=64 * 1024 * 1024),
        cost_estimate=pl.CostEstimate(flops=40_000_000, bytes_accessed=8_000_000, transcendentals=0),
        name="pair_terms",
    )(flat_anchors, flat_pairs, flat_count, *pieces)


def cube_root(value):
    inverse = jnp.exp(jnp.log(value) * (-1.0 / 3.0))
    inverse = inverse * (4.0 - value * inverse * inverse * inverse) * (1.0 / 3.0)
    return value * inverse * inverse


def greet(mesh_x, mesh_y, diagonal=False):
    here_x = lax.axis_index("gx")
    here_y = lax.axis_index("gy")
    left = (lax.rem(here_x + mesh_x - 1, mesh_x), here_y)
    right = (lax.rem(here_x + 1, mesh_x), here_y)
    below = (here_x, lax.rem(here_y + mesh_y - 1, mesh_y))
    above = (here_x, lax.rem(here_y + 1, mesh_y))
    barrier = pltpu.get_barrier_semaphore()
    neighbours = [left, right, below, above]
    if diagonal:
        neighbours += [(left[0], below[1]), (right[0], above[1])]
    for neighbour in neighbours:
        pl.semaphore_signal(barrier, inc=1, device_id=neighbour, device_id_type=MESH)
    pl.semaphore_wait(barrier, len(neighbours))
    return left, right, below, above


def gather_kernel(mesh_x, mesh_y, own, core_source, *refs):
    outs = refs[:8]
    narrow_outs = refs[8:11]
    send_low, send_high, core, narrow_x, narrow_y, sent, landed, copies = refs[11:]
    core_copy = pltpu.make_async_copy(core_source, core, copies.at[3])
    core_copy.start()
    left, right, below, above = greet(mesh_x, mesh_y)
    started = []

    def send(source, slot, device):
        copy = pltpu.make_async_remote_copy(
            src_ref=source,
            dst_ref=outs[slot],
            send_sem=sent.at[slot],
            recv_sem=landed.at[slot],
            device_id=device,
            device_id_type=MESH,
        )
        copy.start()
        started.append(copy)
        return copy

    def prepare(lead):
        lanes = pl.ds(pl.multiple_of(lead * LANES, LANES), LANES)
        values = [own[k, :, lanes].astype(jnp.float32) for k in range(2)]
        send_low[:, lanes] = jnp.concatenate([value[:RIM] for value in values], 0).astype(jnp.bfloat16)
        send_high[:, lanes] = jnp.concatenate([value[LOW:] for value in values], 0).astype(jnp.bfloat16)

    for_leads(HALF, prepare)
    from_left = send(send_high, 0, right)
    from_right = send(send_low, 1, left)
    high = pl.ds(LOW * SIDE, RIM * SIDE)
    low = pl.ds(0, RIM * SIDE)
    send(own.at[:, :, high], 2, above)
    send(own.at[:, :, low], 3, below)
    core_copy.wait()

    def narrow(row):
        narrow_x[row] = core[row].astype(jnp.bfloat16)
        narrow_y[row] = jnp.concatenate([core[2 * row, :RIM], core[2 * row + 1, :RIM]], 0).astype(jnp.bfloat16)

    for_leads(RIM, narrow)
    narrow_copies = [
        pltpu.make_async_copy(source, target, copies.at[index])
        for index, (source, target) in enumerate(
            zip((narrow_x, narrow_y, narrow_y.at[pl.ds(0, RIM // 2)]), narrow_outs)
        )
    ]
    for copy in narrow_copies:
        copy.start()
    from_left.wait_recv()
    send(outs[0].at[:, high], 4, above)
    send(outs[0].at[:, low], 5, below)
    from_right.wait_recv()
    send(outs[1].at[:, high], 6, above)
    send(outs[1].at[:, low], 7, below)
    for copy in started:
        copy.wait_send()
    for copy in started[2:]:
        copy.wait_recv()
    for copy in narrow_copies:
        copy.wait()


def return_kernel(mesh_x, mesh_y, anchors, *refs):
    side_sources = refs[:2]
    column_terms = refs[2:4]
    corner_terms = refs[4:8]
    outs = refs[14:18]
    applied_out, potential_out = refs[18:20]
    landed_corners, send_left, send_right, left_terms, right_terms = refs[20:25]
    loads = refs[25:31]
    density, core, core_x, core_y, core_xy, own = loads
    potential, applied, sent, landed, copies = refs[31:]
    here_x = lax.axis_index("gx")
    here_y = lax.axis_index("gy")
    incoming = [
        pltpu.make_async_copy(source, target, copies.at[index])
        for index, (source, target) in enumerate(
            zip(refs[8:14] + side_sources, loads + (left_terms, right_terms))
        )
    ]
    left, right, below, above = greet(mesh_x, mesh_y)

    def send(source, target, slot, device):
        copy = pltpu.make_async_remote_copy(
            src_ref=source,
            dst_ref=target,
            send_sem=sent.at[slot],
            recv_sem=landed.at[slot],
            device_id=device,
            device_id_type=MESH,
        )
        copy.start()
        return copy

    corners = [
        send(corner_terms[slot], landed_corners.at[slot], slot, device)
        for slot, device in enumerate((below, above, below, above))
    ]
    others = [
        send(column_terms[0], outs[2], 4, below),
        send(column_terms[1], outs[3], 5, above),
    ]
    for copy in incoming:
        copy.start()
    for copy in incoming:
        copy.wait()
    slab = core.shape[0]

    def finish_at(row, column, core_part):
        at = pl.ds(column * GRID_ROWS + GRID_PAD + row, 8, stride=GRID_ROWS)
        value = -xc_factor * cube_root(density[at, :] + core_part)
        density[at, :] = value
        return value

    def own_rows(row):
        for column in range(0, slab, 8):
            potential[row, pl.ds(column, 8), :] = finish_at(row, column, core[row, pl.ds(column, 8), :])

    def right_rows(row):
        beside = core_x[row].astype(jnp.float32)
        for column in range(0, slab, 8):
            finish_at(slab + row, column, beside[column : column + 8])

    def above_rows(pair, source=core_y, beyond=0):
        part = source[pair].astype(jnp.float32)
        for j in range(2):
            for column in range(0, RIM, 8):
                start = j * RIM + column
                finish_at(beyond + 2 * pair + j, slab + column, part[start : start + 8])

    def corner_rows(pair):
        above_rows(pair, source=core_xy, beyond=slab)

    for_leads(slab, own_rows)
    potential_copy = pltpu.make_async_copy(potential, potential_out, copies.at[8])
    potential_copy.start()
    for_leads(RIM, right_rows)
    for copy in corners:
        copy.wait_recv()

    for side, (terms, target) in enumerate(((left_terms, send_left), (right_terms, send_right))):

        def merge(lead, corner, shift, terms=terms, target=target):
            lanes = pl.ds(pl.multiple_of(lead * LANES, LANES), LANES)
            value = terms[:, lanes]
            if corner is not None:
                part = pl.ds(pl.multiple_of((lead - shift) * LANES, LANES), LANES)
                value = value.astype(jnp.float32) + landed_corners[corner, :, part].astype(jnp.float32)
            target[:, lanes] = value.astype(jnp.bfloat16)

        for first, last, corner in (
            (0, RIM_LEADS, 2 * side + 1),
            (RIM_LEADS, LOW_LEADS, None),
            (LOW_LEADS, HALF, 2 * side),
        ):

            def part_step(index, first=first, corner=corner, merge=merge):
                merge(index + first, corner, first)

            for_leads(last - first, part_step)
        others.append(send(target, outs[side], 6 + side, (left, right)[side]))
    for_leads(slab // 2, above_rows)
    for_leads(RIM // 2, corner_rows)

    lane = lane_index(SIDE)
    orbit = (here_x * mesh_y + here_y) * 2
    for k in range(2):
        at_x = jnp.clip(anchors[0, orbit + k] - here_x * slab, 0, GRID_PAD - 1)
        at_y = jnp.clip(anchors[1, orbit + k] - here_y * slab, 0, GRID_PAD - 1)
        at_z = anchors[2, orbit + k]
        start = at_y * GRID_ROWS + at_x + GRID_PAD
        turn_low = lax.rem(LANES - at_z, LANES)
        turn_high = lax.rem(LANES + SIDE - at_z, LANES)

        def sample(lead, k=k, start=start, turn_low=turn_low, turn_high=turn_high):
            lanes = pl.ds(pl.multiple_of(lead * LANES, LANES), LANES)
            low = density[pl.ds(start + 2 * lead * GRID_ROWS, SIDE), :]
            high = density[pl.ds(start + (2 * lead + 1) * GRID_ROWS, SIDE), :]
            sampled = jnp.where(lane < SIDE, pltpu.roll(low, turn_low, 1), pltpu.roll(high, turn_high, 1))
            at = pl.ds(pl.multiple_of((k * HALF + lead) * SIDE, SIDE), SIDE)
            applied[at, :] = sampled * own[k, :, lanes].astype(jnp.float32)

        for_leads(HALF, sample)
    applied_copy = pltpu.make_async_copy(applied, applied_out, copies.at[9])
    applied_copy.start()
    for copy in corners:
        copy.wait_send()
    for copy in others:
        copy.wait()
    applied_copy.wait()
    potential_copy.wait()


def action_kernel(applied, own_terms, from_right, from_left, from_above, from_below, potential_source, action, potential, staged, copied):
    copy = pltpu.make_async_copy(potential_source, staged, copied.at[0])
    copy.start()

    def apply(lead, column=None, shift=0):
        lanes = pl.ds(pl.multiple_of(lead * LANES, LANES), LANES)
        high_rows = from_right[:, lanes].astype(jnp.float32)
        low_rows = from_left[:, lanes].astype(jnp.float32)
        for k in range(2):
            at = pl.ds(pl.multiple_of((k * HALF + lead) * SIDE, SIDE), SIDE)
            terms = own_terms[at, :]
            if column is not None:
                part = pl.ds(pl.multiple_of((lead - shift) * LANES, LANES), LANES)
                terms = terms + column[k, :, part].astype(jnp.float32)
            rows = slice(k * RIM, (k + 1) * RIM)
            terms = jnp.concatenate(
                [terms[:RIM] + low_rows[rows], terms[RIM:LOW], terms[LOW:] + high_rows[rows]], 0
            )
            action[k, :, lanes] = applied[at, :] - exx_share * terms

    copy.wait()
    copy = pltpu.make_async_copy(staged, potential, copied.at[1])
    copy.start()
    for start, stop, column in ((0, RIM_LEADS, from_below), (RIM_LEADS, LOW_LEADS, None), (LOW_LEADS, HALF, from_above)):

        def part_step(index, start=start, column=column):
            apply(index + start, column=column, shift=start)

        for_leads(stop - start, part_step)
    copy.wait()


def shape_of(dims, dtype=jnp.bfloat16):
    return jax.ShapeDtypeStruct(dims, dtype)


def local(orbitals, anchors, pair_list, pair_count, core_density):
    mesh_x = lax.axis_size("gx")
    mesh_y = lax.axis_size("gy")
    own = orbitals[0, 0]
    flat_anchors = anchors.T
    flat_pairs = pair_list[0, 0].T
    flat_count = pair_count.reshape(-1)
    side_shape = shape_of((2 * RIM, FLAT))
    column_shape = shape_of((2, SIDE, RIM * SIDE))
    corner_shape = shape_of((2 * RIM, RIM * SIDE))
    around = [side_shape] * 2 + [column_shape] * 2 + [corner_shape] * 4

    core_shape = core_density.shape
    narrow_shapes = [
        (RIM, core_shape[1], LANES),
        (core_shape[0] // 2, 2 * RIM, LANES),
        (RIM // 2, 2 * RIM, LANES),
    ]
    grant = 64 * 1024 * 1024

    gathered = pl.pallas_call(
        functools.partial(gather_kernel, mesh_x, mesh_y),
        out_shape=around + [shape_of(dims) for dims in narrow_shapes],
        in_specs=[vmem, hbm],
        out_specs=[hbm] * 11,
        scratch_shapes=[
            pltpu.VMEM(side_shape.shape, jnp.bfloat16),
            pltpu.VMEM(side_shape.shape, jnp.bfloat16),
            pltpu.VMEM(core_shape, jnp.float32),
            pltpu.VMEM(narrow_shapes[0], jnp.bfloat16),
            pltpu.VMEM(narrow_shapes[1], jnp.bfloat16),
            pltpu.SemaphoreType.DMA((8,)),
            pltpu.SemaphoreType.DMA((8,)),
            pltpu.SemaphoreType.DMA((4,)),
        ],
        compiler_params=pltpu.CompilerParams(
            collective_id=0, has_side_effects=True, vmem_limit_bytes=grant
        ),
        name="gather_rims",
    )(own, core_density)
    pieces = gathered[:8]

    back_x = [((i + 1) % mesh_x, i) for i in range(mesh_x)]
    back_y = [((i + 1) % mesh_y, i) for i in range(mesh_y)]
    back_xy = [
        ((i + 1) % mesh_x * mesh_y + (j + 1) % mesh_y, i * mesh_y + j)
        for i in range(mesh_x)
        for j in range(mesh_y)
    ]
    core_rims = [
        lax.ppermute(gathered[8], "gx", back_x),
        lax.ppermute(gathered[9], "gy", back_y),
        lax.ppermute(gathered[10], ("gx", "gy"), back_xy),
    ]

    terms = pairs_call(mesh_x, mesh_y, flat_anchors, flat_pairs, flat_count, [own] + list(pieces))
    grid_shape = terms[1].shape
    *returned, applied, potential = pl.pallas_call(
        functools.partial(return_kernel, mesh_x, mesh_y),
        out_shape=[side_shape] * 2
        + [column_shape] * 2
        + [shape_of((BASE_X, LANES), jnp.float32), shape_of(core_shape, jnp.float32)],
        in_specs=[smem] + [hbm] * 14,
        out_specs=[hbm] * 6,
        scratch_shapes=[
            pltpu.VMEM((4,) + corner_shape.shape, jnp.bfloat16),
            pltpu.VMEM(side_shape.shape, jnp.bfloat16),
            pltpu.VMEM(side_shape.shape, jnp.bfloat16),
            pltpu.VMEM(side_shape.shape, jnp.bfloat16),
            pltpu.VMEM(side_shape.shape, jnp.bfloat16),
            pltpu.VMEM(grid_shape, jnp.float32),
            pltpu.VMEM(core_shape, jnp.float32),
            pltpu.VMEM(narrow_shapes[0], jnp.bfloat16),
            pltpu.VMEM(narrow_shapes[1], jnp.bfloat16),
            pltpu.VMEM(narrow_shapes[2], jnp.bfloat16),
            pltpu.VMEM(own.shape, jnp.bfloat16),
            pltpu.VMEM(core_shape, jnp.float32),
            pltpu.VMEM((BASE_X, LANES), jnp.float32),
            pltpu.SemaphoreType.DMA((8,)),
            pltpu.SemaphoreType.DMA((8,)),
            pltpu.SemaphoreType.DMA((10,)),
        ],
        compiler_params=pltpu.CompilerParams(
            collective_id=1, has_side_effects=True, vmem_limit_bytes=grant
        ),
        name="return_terms",
    )(flat_anchors, *terms[2:], terms[1], core_density, *core_rims, own)
    action, potential = pl.pallas_call(
        action_kernel,
        out_shape=[shape_of(own.shape, jnp.float32), shape_of(core_shape, jnp.float32)],
        in_specs=[vmem] * 6 + [hbm],
        out_specs=[vmem, hbm],
        scratch_shapes=[pltpu.VMEM(core_shape, jnp.float32), pltpu.SemaphoreType.DMA((2,))],
        compiler_params=pltpu.CompilerParams(vmem_limit_bytes=grant),
        name="action_terms",
    )(applied, terms[0], *returned, potential)
    return (action.reshape(orbitals.shape), potential)


def solution(mesh):
    placed = (
        P("gx", "gy", None, None, None),
        P(),
        P("gx", "gy", None, None),
        P("gx", "gy"),
        P("gx", "gy", None),
    )
    return jax.shard_map(
        local,
        mesh=mesh,
        in_specs=placed,
        out_specs=(P("gx", "gy", None, None, None), P("gx", "gy", None)),
        check_vma=False,
    )
```

```python
import functools
import math

import jax
import jax.numpy as jnp
from jax import lax
from jax.experimental import pallas as pl
from jax.experimental.pallas import tpu as pltpu
from jax.sharding import PartitionSpec as P

SWEEPS = 4
SIDE = 64
HALF = SIDE // 2
FLAT = SIDE * SIDE
RIM = 24
LOW = SIDE - RIM
RIM_LEADS = RIM // 2
LOW_LEADS = LOW // 2
LANES = 128
PAD = 512
CHUNKS = [(False, False, 32), (True, False, 32), (False, True, 12), (True, True, 12)]

screen_mass = 0.25
coupling = 2.0 * math.pi
exx_share = 0.25
xc_factor = (3.0 / math.pi) ** (1.0 / 3.0)

AHEAD = [2, 4, 7, 8]
BASE_X = 2 * HALF * SIDE
BASE_Y = BASE_X + 4 * HALF * RIM
BASE_C = BASE_Y + 4 * RIM_LEADS * SIDE
WINDOW_ROWS = BASE_C + 8 * RIM_LEADS * RIM
STEPS = [(0, 0), (-1, 0), (1, 0), (0, -1), (0, 1), (-1, -1), (-1, 1), (1, -1), (1, 1)]


def place_of(step_x, step_y):
    rows = SIDE if step_x == 0 else RIM
    leads = HALF if step_y == 0 else RIM_LEADS
    if step_x == 0 and step_y == 0:
        base = 0
    elif step_y == 0:
        base = BASE_X + (2 * HALF * RIM if step_x > 0 else 0)
    elif step_x == 0:
        base = BASE_Y + (2 * RIM_LEADS * SIDE if step_y > 0 else 0)
    else:
        base = BASE_C + ((2 if step_x > 0 else 0) + (1 if step_y > 0 else 0)) * 2 * RIM_LEADS * RIM
    return base, rows, leads


def sweep_weights(sweep_count):
    return [
        1.0 / (1.0 + 0.7 * math.cos(math.pi * (2 * order + 1) / (2 * sweep_count)))
        for order in range(sweep_count)
    ]


def lane_index(rows):
    return lax.broadcasted_iota(jnp.int32, (rows, LANES), 1)


def one_where(condition):
    return jnp.where(condition, 1.0, 0.0).astype(jnp.bfloat16)


def halves(value):
    upper = value.astype(jnp.bfloat16)
    lower = (value - upper.astype(jnp.float32)).astype(jnp.bfloat16)
    return jnp.concatenate([upper, lower], 1)


def for_leads(count, step):
    lax.fori_loop(0, count, lambda index, _: (step(index), 0)[1], 0)


def pair_kernel(mesh_x, mesh_y, anchors, lists, *refs):
    sources = refs[:9]
    own_out, grid_out = refs[9:11]
    targets_out = refs[11:15]
    (
        window,
        sums,
        near,
        turn_in,
        turn_out,
        moved3,
        source3,
        even3,
        odd3,
        moved8,
        source8,
        even8,
        odd8,
        grid,
        place,
        copies,
    ) = refs[15:31]
    pieces = refs[31:40]
    outs = refs[40:44]
    here_x = lax.axis_index("gx")
    here_y = lax.axis_index("gy")
    span_x = mesh_x * (SIDE - 16)
    span_y = mesh_y * (SIDE - 16)

    incoming = [
        pltpu.make_async_copy(source, piece, copies.at[2 + index])
        for index, (source, piece) in enumerate(zip(sources, pieces))
    ]
    for copy in incoming:
        copy.start()
    zeros64 = jnp.zeros((SIDE, LANES), jnp.float32)

    def clear_sums(lead):
        sums[pl.ds(pl.multiple_of(lead * SIDE, SIDE), SIDE), :] = zeros64

    for_leads((WINDOW_ROWS + 2 * PAD) // SIDE, clear_sums)

    def clear_ends(lead):
        for start in (0, PAD + WINDOW_ROWS):
            window[pl.ds(pl.multiple_of(start + lead * SIDE, SIDE), SIDE), :] = zeros64

    for_leads(PAD // SIDE, clear_ends)

    for field in (source3, even3, odd3, source8, even8, odd8):
        rows = field.shape[1]
        field[0] = jnp.zeros((rows, LANES), jnp.float32)

        def clear_edge(lead, field=field, rows=rows):
            edge = jnp.zeros((8, LANES), jnp.float32)
            field[lead, pl.ds(0, 8), :] = edge
            field[lead, pl.ds(rows - 8, 8), :] = edge

        for_leads(HALF + 2, clear_edge)

    from_lane = lax.broadcasted_iota(jnp.int32, (LANES, LANES), 0)
    to_lane = lax.broadcasted_iota(jnp.int32, (LANES, LANES), 1)
    swap = jnp.abs(to_lane - from_lane) == SIDE
    step = (jnp.abs(to_lane - from_lane) == 1) & ((to_lane < SIDE) == (from_lane < SIDE))
    for start in (0, LANES):
        near[start : start + LANES, :LANES] = one_where(step | swap)
        near[start : start + LANES, LANES:] = one_where(swap)

    def clear_grid(lead):
        start = pl.multiple_of(lead * GRID_ROWS, 8)
        grid[pl.ds(start, GRID_ROWS), :] = jnp.zeros((GRID_ROWS, LANES), jnp.float32)

    for_leads(GRID_ROWS, clear_grid)

    for (step_x, step_y), piece, copy in zip(STEPS, pieces, incoming):
        base, rows, leads = place_of(step_x, step_y)

        def widen(lead, base=base, rows=rows, leads=leads, piece=piece):
            lanes = pl.ds(pl.multiple_of(lead * LANES, LANES), LANES)
            if rows == RIM:
                both = piece[:, lanes].astype(jnp.float32)
            for k in range(2):
                start = pl.multiple_of(PAD + base + k * leads * rows + lead * rows, 8)
                if rows == RIM:
                    value = both[k * RIM : (k + 1) * RIM]
                else:
                    value = piece[k, :, lanes].astype(jnp.float32)
                window[pl.ds(start, rows), :] = value

        copy.wait()
        for_leads(leads, widen)

    weights = sweep_weights(SWEEPS)
    diagonal = 6.0 + screen_mass
    scale = [weight / diagonal for weight in weights]
    keep = [(1.0 - weight) / part for weight, part in zip(weights, scale)]
    total_scale = coupling * scale[0] * scale[1] * scale[2] * scale[3]

    def slot_of(offset_x, offset_y, k):
        plus_x = jnp.where(offset_x > 0, 1, 0)
        plus_y = jnp.where(offset_y > 0, 1, 0)
        rows = jnp.where(offset_x != 0, RIM, SIDE)
        leads = jnp.where(offset_y != 0, RIM_LEADS, HALF)
        base = jnp.where(
            offset_x != 0,
            jnp.where(
                offset_y != 0,
                BASE_C + (2 * plus_x + plus_y) * (2 * RIM_LEADS * RIM),
                BASE_X + plus_x * (2 * HALF * RIM),
            ),
            jnp.where(offset_y != 0, BASE_Y + plus_y * (2 * RIM_LEADS * SIDE), 0),
        )
        origin_x = jnp.where(offset_x < 0, LOW, 0)
        origin_lead = jnp.where(offset_y < 0, LOW_LEADS, 0)
        return PAD + base + k * leads * rows, rows, origin_x, origin_lead

    def pair_step(source, slot, carry):
        from_x = jnp.where((source >= 1) & (source <= 3), 1, 0)
        from_y = jnp.where(source == 1, -1, jnp.where(source >= 3, 1, 0))
        first = lists[source, 0, slot]
        second = lists[source, 1, slot]
        holder = lax.div(second, 2)
        to_x = lax.rem(lax.div(holder, mesh_y) - here_x + 1 + mesh_x, mesh_x) - 1
        to_y = lax.rem(lax.rem(holder, mesh_y) - here_y + 1 + mesh_y, mesh_y) - 1
        is_own = (to_x == 0) & (to_y == 0)
        ahead = (to_x == 1) | ((to_x == 0) & (to_y == 1))
        mine = is_own | (ahead & (source == 0))
        pl.when(mine)(functools.partial(pair_work, first, second, from_x, from_y, to_x, to_y))
        return carry

    def pair_work(first, second, from_x, from_y, to_x, to_y):
        step_x = to_x - from_x
        step_y = to_y - from_y
        shift_x = anchors[0, second] - anchors[0, first]
        shift_y = anchors[1, second] - anchors[1, first]
        shift_z = anchors[2, second] - anchors[2, first]
        shift_x = shift_x + jnp.where(shift_x < -(span_x // 2), span_x, 0) - jnp.where(
            shift_x >= span_x // 2, span_x, 0
        )
        shift_y = shift_y + jnp.where(shift_y < -(span_y // 2), span_y, 0) - jnp.where(
            shift_y >= span_y // 2, span_y, 0
        )
        half_y = lax.shift_right_arithmetic(shift_y, 1)
        odd_y = shift_y - 2 * half_y
        side_x = step_x != 0
        side_y = step_y != 0
        start_x = jnp.where(step_x > 0, LOW, 0)
        start_lead = jnp.where(step_y > 0, LOW_LEADS, 0)
        near_base, near_stride, near_x, near_lead = slot_of(from_x, from_y, lax.rem(first, 2))
        far_base, far_stride, far_x, far_lead = slot_of(to_x, to_y, lax.rem(second, 2))
        near_start = near_base + (start_lead - near_lead) * near_stride + start_x - near_x
        far_start = (
            far_base + (start_lead - half_y - far_lead) * far_stride + start_x - shift_x - far_x
        )
        from_lane = lax.broadcasted_iota(jnp.int32, (LANES, LANES), 0)
        to_lane = lax.broadcasted_iota(jnp.int32, (LANES, LANES), 1)
        apart = to_lane - from_lane - shift_z
        depth = lax.rem(to_lane, SIDE) - shift_z
        valid = (depth >= 0) & (depth < SIDE)
        same = valid & (apart == SIDE * odd_y)
        other = valid & (apart == -SIDE) & (odd_y == 1)
        turn_in[:LANES] = one_where(same)
        turn_in[LANES:] = one_where(other)
        from_lane, to_lane = to_lane, from_lane
        apart = to_lane - from_lane - shift_z
        depth = lax.rem(to_lane, SIDE) - shift_z
        valid = (depth >= 0) & (depth < SIDE)
        same = one_where(valid & (apart == SIDE * odd_y))
        other = one_where(valid & (apart == -SIDE) & (odd_y == 1))
        turn_out[:LANES, :LANES] = same
        turn_out[LANES:, :LANES] = same
        turn_out[:LANES, LANES:] = other
        turn_out[LANES:, LANES:] = other

        def run(tiles, leads, chunk, moved, source, even, odd):
            rows = tiles * 8
            inner = pl.ds(8, rows)
            lane = lane_index(rows)
            upper = lane >= SIDE
            row = lax.broadcasted_iota(jnp.int32, (rows, LANES), 0) + start_x
            column_part = jnp.where(upper, 1, 0) - shift_y
            inside_x = (row >= shift_x) & (row < SIDE + shift_x)

            def inside(lead):
                column = column_part + 2 * lead
                return inside_x & (column >= 0) & (column < SIDE)

            def far_rows(lead):
                return pl.ds(far_start + lead * far_stride, rows)

            def own_rows(lead):
                return pl.ds(pl.multiple_of(near_start + lead * near_stride, 8), rows)

            def part(value, index):
                return value[index * rows : (index + 1) * rows]

            def build(index):
                lead = index * chunk
                loads = [window[far_rows(lead + j), :] for j in range(-1, chunk)]
                now = jnp.concatenate(loads[1:], 0).astype(jnp.bfloat16)
                before = jnp.concatenate(loads[:-1], 0).astype(jnp.bfloat16)
                turned = jnp.dot(
                    jnp.concatenate([now, before], 1), turn_in[...], preferred_element_type=jnp.float32
                )
                for j in range(chunk):
                    piece = jnp.where(inside(start_lead + lead + j), part(turned, j), 0.0)
                    moved[lead + j] = piece
                    source[lead + j + 1, inner, :] = piece * window[own_rows(lead + j), :]

            def near_fields(field, lead):
                values = [field[lead + j, inner, :] for j in range(chunk + 2)]
                product = jnp.dot(
                    halves(jnp.concatenate(values, 0)), near[...], preferred_element_type=jnp.float32
                )
                for j in range(chunk):
                    across = jnp.where(
                        upper, part(product, j + 2)[:, LANES:], part(product, j)[:, LANES:]
                    )
                    beside = field[lead + j + 1, pl.ds(7, rows), :] + field[lead + j + 1, pl.ds(9, rows), :]
                    yield values[j + 1], (part(product, j + 1)[:, :LANES] + across) + beside

            def sweep(old, new, own_part, source_part):
                def body(index):
                    lead = index * chunk
                    for j, (here, near_sum) in enumerate(near_fields(old, lead)):
                        value = own_part * here + near_sum
                        if source_part is not None:
                            value = value + source_part * source[lead + j + 1, inner, :]
                        new[lead + j + 1, inner, :] = value

                return body

            def finish(index):
                lead = index * chunk
                back = []
                for j, (here, near_sum) in enumerate(near_fields(odd, lead)):
                    value = keep[3] * here + near_sum
                    value = value + (1.0 / (scale[0] * scale[1] * scale[2])) * source[lead + j + 1, inner, :]
                    value = value * total_scale
                    sums[own_rows(lead + j), :] = sums[own_rows(lead + j), :] + value * moved[lead + j]
                    back.append(
                        jnp.where(inside(start_lead + lead + j), value * window[own_rows(lead + j), :], 0.0)
                    )
                turned = jnp.dot(
                    halves(jnp.concatenate(back, 0)), turn_out[...], preferred_element_type=jnp.float32
                )
                targets = [sums[far_rows(lead + j), :] for j in range(-1, chunk)]
                for j in range(-1, chunk):
                    total = targets[j + 1]
                    if j >= 0:
                        total = total + part(turned, j)[:, :LANES]
                    if j + 1 < chunk:
                        total = total + part(turned, j + 1)[:, LANES:]
                    targets[j + 1] = total
                for j in range(-1, chunk):
                    sums[far_rows(lead + j), :] = targets[j + 1]

            edge = jnp.zeros((rows, LANES), jnp.float32)
            for field in (source, even, odd):
                field[leads + 1, inner, :] = edge
            chunks = leads // chunk
            for_leads(chunks, build)
            for_leads(chunks, sweep(source, even, keep[1] + 1.0 / scale[0], None))
            for_leads(chunks, sweep(even, odd, keep[2], 1.0 / (scale[0] * scale[1])))
            for_leads(chunks, finish)

        for has_x, has_y, chunk in CHUNKS:
            narrow = side_x if has_x else jnp.logical_not(side_x)
            narrow = narrow & (side_y if has_y else jnp.logical_not(side_y))
            fields = (moved3, source3, even3, odd3) if has_x else (moved8, source8, even8, odd8)

            @pl.when(narrow)
            def _(has_x=has_x, has_y=has_y, chunk=chunk, fields=fields):
                run(
                    (RIM if has_x else SIDE) // 8,
                    RIM_LEADS if has_y else HALF,
                    chunk,
                    *fields,
                )

    def list_step(source, carry):
        return lax.fori_loop(0, lists[source, 2, 0], functools.partial(pair_step, source), carry)

    lax.fori_loop(0, 5, list_step, 0)

    own_copy = pltpu.make_async_copy(sums.at[pl.ds(PAD, BASE_X)], own_out, copies.at[0])
    own_copy.start()

    outgoing = []
    for step, out, target in zip([STEPS[index] for index in AHEAD], outs, targets_out):
        base, rows, leads = place_of(*step)

        def narrow(lead, base=base, rows=rows, leads=leads, out=out):
            lanes = pl.ds(pl.multiple_of(lead * LANES, LANES), LANES)
            values = []
            for k in range(2):
                start = pl.multiple_of(PAD + base + k * leads * rows + lead * rows, 8)
                values.append(sums[pl.ds(start, rows), :])
            if rows == RIM:
                out[:, lanes] = jnp.concatenate(values, 0).astype(out.dtype)
            else:
                for k in range(2):
                    out[k, :, lanes] = values[k].astype(out.dtype)

        for_leads(leads, narrow)
        copy = pltpu.make_async_copy(out, target, copies.at[11 + len(outgoing)])
        copy.start()
        outgoing.append(copy)

    slab = SIDE - 16

    def deposit(step_x, step_y, k, base, rows, leads):
        holder_x = lax.rem(here_x + step_x + mesh_x, mesh_x)
        holder_y = lax.rem(here_y + step_y + mesh_y, mesh_y)
        orbit = (holder_x * mesh_y + holder_y) * 2 + k
        at_x = anchors[0, orbit] - holder_x * slab
        at_y = anchors[1, orbit] - holder_y * slab
        at_z = anchors[2, orbit]
        row = at_x + step_x * slab + GRID_PAD + jnp.where(step_x < 0, LOW, 0)
        column = at_y + step_y * slab + GRID_PAD + jnp.where(step_y < 0, LOW, 0)
        start = column * GRID_ROWS + row
        from_lane = lax.broadcasted_iota(jnp.int32, (LANES, LANES), 0)
        apart = lax.broadcasted_iota(jnp.int32, (LANES, LANES), 1) - from_lane - at_z
        low = one_where((from_lane < SIDE) & (apart == 0))
        high = one_where((from_lane >= SIDE) & (apart == -SIDE))
        place[:, :LANES] = low
        place[:, LANES:] = high
        block = 16
        for first in range(0, leads, block):
            size = min(block, leads - first)
            value = window[pl.ds(pl.multiple_of(PAD + base + first * rows, 8), size * rows), :]
            placed = jnp.dot(value.astype(jnp.bfloat16), place[...], preferred_element_type=jnp.float32)
            for j in range(size):
                for odd_column in (0, 1):
                    at = pl.ds(start + (2 * (first + j) + odd_column) * GRID_ROWS, rows)
                    part = placed[j * rows : (j + 1) * rows, odd_column * LANES : (odd_column + 1) * LANES]
                    grid[at, :] = grid[at, :] + part * part

    for k in range(2):
        deposit(0, 0, k, k * HALF * SIDE, SIDE, HALF)

    def deposit_x(index, carry):
        deposit(2 * (index // 2) - 1, 0, lax.rem(index, 2), BASE_X + index * (HALF * RIM), RIM, HALF)
        return carry

    def deposit_y(index, carry):
        deposit(
            0, 2 * (index // 2) - 1, lax.rem(index, 2), BASE_Y + index * (RIM_LEADS * SIDE), SIDE, RIM_LEADS
        )
        return carry

    def deposit_corner(index, carry):
        deposit(
            2 * (index // 4) - 1,
            2 * lax.rem(index // 2, 2) - 1,
            lax.rem(index, 2),
            BASE_C + index * (RIM_LEADS * RIM),
            RIM,
            RIM_LEADS,
        )
        return carry

    lax.fori_loop(0, 4, deposit_x, 0)
    lax.fori_loop(0, 4, deposit_y, 0)
    lax.fori_loop(0, 8, deposit_corner, 0)
    grid_copy = pltpu.make_async_copy(grid.at[pl.ds(GRID_PAD * GRID_ROWS, EDGE_ROWS)], grid_out, copies.at[1])
    grid_copy.start()
    for copy in [own_copy, *outgoing, grid_copy]:
        copy.wait()


GRID_PAD = 8
GRID_ROWS = 88
EDGE = SIDE - 16 + RIM
EDGE_ROWS = (EDGE + 1) * GRID_ROWS
hbm = pl.BlockSpec(memory_space=pl.ANY)
MESH = pl.DeviceIdType.MESH

smem = pl.BlockSpec(memory_space=pltpu.SMEM)
vmem = pl.BlockSpec(memory_space=pltpu.VMEM)


def pairs_call(mesh_x, mesh_y, flat_anchors, lists, pieces):
    term_shapes = [
        jax.ShapeDtypeStruct((BASE_X, LANES), jnp.float32),
        jax.ShapeDtypeStruct((EDGE_ROWS, LANES), jnp.float32),
    ] + [jax.ShapeDtypeStruct(pieces[index].shape, jnp.bfloat16) for index in AHEAD]

    def field(rows):
        return pltpu.VMEM((HALF + 2, rows, LANES), jnp.float32)

    return pl.pallas_call(
        functools.partial(pair_kernel, mesh_x, mesh_y),
        out_shape=term_shapes,
        in_specs=[smem] * 2 + [hbm] * 9,
        out_specs=[hbm] * 6,
        scratch_shapes=[
            pltpu.VMEM((WINDOW_ROWS + 2 * PAD, LANES), jnp.float32),
            pltpu.VMEM((WINDOW_ROWS + 2 * PAD, LANES), jnp.float32),
            pltpu.VMEM((2 * LANES, 2 * LANES), jnp.bfloat16),
            pltpu.VMEM((2 * LANES, LANES), jnp.bfloat16),
            pltpu.VMEM((2 * LANES, 2 * LANES), jnp.bfloat16),
            pltpu.VMEM((HALF, RIM, LANES), jnp.float32),
            field(RIM + 16),
            field(RIM + 16),
            field(RIM + 16),
            pltpu.VMEM((HALF, SIDE, LANES), jnp.float32),
            field(SIDE + 16),
            field(SIDE + 16),
            field(SIDE + 16),
            pltpu.VMEM((GRID_ROWS * GRID_ROWS, LANES), jnp.float32),
            pltpu.VMEM((LANES, 2 * LANES), jnp.bfloat16),
            pltpu.SemaphoreType.DMA((19,)),
        ]
        + [pltpu.VMEM(piece.shape, jnp.bfloat16) for piece in pieces]
        + [pltpu.VMEM(pieces[index].shape, jnp.bfloat16) for index in AHEAD],
        compiler_params=pltpu.CompilerParams(vmem_limit_bytes=64 * 1024 * 1024),
        cost_estimate=pl.CostEstimate(flops=40_000_000, bytes_accessed=8_000_000, transcendentals=0),
        name="pair_terms",
    )(flat_anchors, lists, *pieces)


def cube_root(value):
    inverse = jnp.exp(jnp.log(value) * (-1.0 / 3.0))
    inverse = inverse * (4.0 - value * inverse * inverse * inverse) * (1.0 / 3.0)
    return value * inverse * inverse


def greet(mesh_x, mesh_y, diagonal=False):
    here_x = lax.axis_index("gx")
    here_y = lax.axis_index("gy")
    left = (lax.rem(here_x + mesh_x - 1, mesh_x), here_y)
    right = (lax.rem(here_x + 1, mesh_x), here_y)
    below = (here_x, lax.rem(here_y + mesh_y - 1, mesh_y))
    above = (here_x, lax.rem(here_y + 1, mesh_y))
    barrier = pltpu.get_barrier_semaphore()
    neighbours = [left, right, below, above]
    if diagonal:
        neighbours += [(side[0], end[1]) for side in (left, right) for end in (below, above)]
    for neighbour in neighbours:
        pl.semaphore_signal(barrier, inc=1, device_id=neighbour, device_id_type=MESH)
    pl.semaphore_wait(barrier, len(neighbours))
    return left, right, below, above


def gather_kernel(mesh_x, mesh_y, own, core_source, list_source, *refs):
    outs = refs[:8]
    narrow_outs = refs[8:11]
    lists = refs[11]
    send_low, send_high, core, narrow_x, narrow_y, sent, landed, copies = refs[12:]
    core_copy = pltpu.make_async_copy(core_source, core, copies.at[3])
    core_copy.start()
    list_copy = pltpu.make_async_copy(list_source, lists.at[0], copies.at[4])
    list_copy.start()
    left, right, below, above = greet(mesh_x, mesh_y, diagonal=True)
    started = []

    def send(source, slot, device, target=None):
        copy = pltpu.make_async_remote_copy(
            src_ref=source,
            dst_ref=outs[slot] if target is None else target,
            send_sem=sent.at[slot],
            recv_sem=landed.at[slot],
            device_id=device,
            device_id_type=MESH,
        )
        copy.start()
        started.append(copy)
        return copy

    def prepare(lead):
        lanes = pl.ds(pl.multiple_of(lead * LANES, LANES), LANES)
        values = [own[k, :, lanes].astype(jnp.float32) for k in range(2)]
        send_low[:, lanes] = jnp.concatenate([value[:RIM] for value in values], 0).astype(jnp.bfloat16)
        send_high[:, lanes] = jnp.concatenate([value[LOW:] for value in values], 0).astype(jnp.bfloat16)

    for_leads(HALF, prepare)
    from_left = send(send_high, 0, right)
    from_right = send(send_low, 1, left)
    high = pl.ds(LOW * SIDE, RIM * SIDE)
    low = pl.ds(0, RIM * SIDE)
    send(own.at[:, :, high], 2, above)
    send(own.at[:, :, low], 3, below)
    for index, device in enumerate(((left[0], above[1]), left, (left[0], below[1]), below)):
        send(list_source, 8 + index, device, target=lists.at[1 + index])
    core_copy.wait()

    def narrow(row):
        narrow_x[row] = core[row].astype(jnp.bfloat16)
        narrow_y[row] = jnp.concatenate([core[2 * row, :RIM], core[2 * row + 1, :RIM]], 0).astype(jnp.bfloat16)

    for_leads(RIM, narrow)
    narrow_copies = [
        pltpu.make_async_copy(source, target, copies.at[index])
        for index, (source, target) in enumerate(
            zip((narrow_x, narrow_y, narrow_y.at[pl.ds(0, RIM // 2)]), narrow_outs)
        )
    ]
    for copy in narrow_copies:
        copy.start()
    from_left.wait_recv()
    send(outs[0].at[:, high], 4, above)
    send(outs[0].at[:, low], 5, below)
    from_right.wait_recv()
    send(outs[1].at[:, high], 6, above)
    send(outs[1].at[:, low], 7, below)
    for copy in started:
        copy.wait_send()
    for copy in started[2:]:
        copy.wait_recv()
    for copy in narrow_copies:
        copy.wait()
    list_copy.wait()


def return_kernel(mesh_x, mesh_y, anchors, *refs):
    side_source, column_terms = refs[:2]
    corner_terms = refs[2:4]
    out_side, out_column, applied_out, potential_out = refs[10:14]
    landed_corners, send_right, right_terms = refs[14:17]
    loads = refs[17:23]
    density, core, core_x, core_y, core_xy, own = loads
    potential, applied, sent, landed, copies = refs[23:]
    here_x = lax.axis_index("gx")
    here_y = lax.axis_index("gy")
    incoming = [
        pltpu.make_async_copy(source, target, copies.at[index])
        for index, (source, target) in enumerate(
            zip(refs[4:10] + (side_source,), loads + (right_terms,))
        )
    ]
    left, right, below, above = greet(mesh_x, mesh_y)

    def send(source, target, slot, device):
        copy = pltpu.make_async_remote_copy(
            src_ref=source,
            dst_ref=target,
            send_sem=sent.at[slot],
            recv_sem=landed.at[slot],
            device_id=device,
            device_id_type=MESH,
        )
        copy.start()
        return copy

    corners = [
        send(corner_terms[slot], landed_corners.at[slot], slot, device)
        for slot, device in enumerate((below, above))
    ]
    high = pl.ds(LOW * SIDE, RIM * SIDE)
    low = pl.ds(0, RIM * SIDE)
    middle = pl.ds(RIM * SIDE, (LOW - RIM) * SIDE)
    others = [send(side_source.at[:, middle], out_side.at[:, middle], 2, right)]
    for copy in incoming:
        copy.start()
    for copy in incoming:
        copy.wait()
    slab = core.shape[0]

    def finish_at(row, column, core_part):
        at = pl.ds(column * GRID_ROWS + GRID_PAD + row, 8, stride=GRID_ROWS)
        value = -xc_factor * cube_root(density[at, :] + core_part)
        density[at, :] = value
        return value

    def own_rows(row):
        for column in range(0, slab, 8):
            potential[row, pl.ds(column, 8), :] = finish_at(row, column, core[row, pl.ds(column, 8), :])

    def right_rows(row):
        beside = core_x[row].astype(jnp.float32)
        for column in range(0, slab, 8):
            finish_at(slab + row, column, beside[column : column + 8])

    def above_rows(pair, source=core_y, beyond=0):
        part = source[pair].astype(jnp.float32)
        for j in range(2):
            for column in range(0, RIM, 8):
                start = j * RIM + column
                finish_at(beyond + 2 * pair + j, slab + column, part[start : start + 8])

    def corner_rows(pair):
        above_rows(pair, source=core_xy, beyond=slab)

    for_leads(slab, own_rows)
    others.append(send(column_terms, out_column, 3, above))
    potential_copy = pltpu.make_async_copy(potential, potential_out, copies.at[7])
    potential_copy.start()
    for_leads(RIM, right_rows)
    for corner, (first, columns) in enumerate(((LOW_LEADS, high), (0, low))):
        corners[corner].wait_recv()

        def merge(index, first=first, corner=corner):
            lanes = pl.ds(pl.multiple_of((index + first) * LANES, LANES), LANES)
            at = pl.ds(pl.multiple_of(index * LANES, LANES), LANES)
            value = right_terms[:, lanes].astype(jnp.float32) + landed_corners[corner, :, at].astype(jnp.float32)
            send_right[:, lanes] = value.astype(jnp.bfloat16)

        for_leads(RIM_LEADS, merge)
        others.append(send(send_right.at[:, columns], out_side.at[:, columns], 4 + corner, right))
    for_leads(slab // 2, above_rows)
    for_leads(RIM // 2, corner_rows)

    lane = lane_index(SIDE)
    orbit = (here_x * mesh_y + here_y) * 2
    for k in range(2):
        at_x = jnp.clip(anchors[0, orbit + k] - here_x * slab, 0, GRID_PAD - 1)
        at_y = jnp.clip(anchors[1, orbit + k] - here_y * slab, 0, GRID_PAD - 1)
        at_z = anchors[2, orbit + k]
        start = at_y * GRID_ROWS + at_x + GRID_PAD
        turn_low = lax.rem(LANES - at_z, LANES)
        turn_high = lax.rem(LANES + SIDE - at_z, LANES)

        def sample(lead, k=k, start=start, turn_low=turn_low, turn_high=turn_high):
            lanes = pl.ds(pl.multiple_of(lead * LANES, LANES), LANES)
            low = density[pl.ds(start + 2 * lead * GRID_ROWS, SIDE), :]
            high = density[pl.ds(start + (2 * lead + 1) * GRID_ROWS, SIDE), :]
            sampled = jnp.where(lane < SIDE, pltpu.roll(low, turn_low, 1), pltpu.roll(high, turn_high, 1))
            at = pl.ds(pl.multiple_of((k * HALF + lead) * SIDE, SIDE), SIDE)
            applied[at, :] = sampled * own[k, :, lanes].astype(jnp.float32)

        for_leads(HALF, sample)
    applied_copy = pltpu.make_async_copy(applied, applied_out, copies.at[8])
    applied_copy.start()
    for copy in corners:
        copy.wait_send()
    for copy in others:
        copy.wait()
    applied_copy.wait()
    potential_copy.wait()


def action_kernel(
    applied, own_terms, from_left, from_below, potential_source, action, potential, staged, copied
):
    copy = pltpu.make_async_copy(potential_source, staged, copied.at[0])
    copy.start()

    def apply(lead, column=None, shift=0):
        lanes = pl.ds(pl.multiple_of(lead * LANES, LANES), LANES)
        low_rows = from_left[:, lanes].astype(jnp.float32)
        for k in range(2):
            at = pl.ds(pl.multiple_of((k * HALF + lead) * SIDE, SIDE), SIDE)
            terms = own_terms[at, :]
            if column is not None:
                part = pl.ds(pl.multiple_of((lead - shift) * LANES, LANES), LANES)
                terms = terms + column[k, :, part].astype(jnp.float32)
            rows = slice(k * RIM, (k + 1) * RIM)
            terms = jnp.concatenate([terms[:RIM] + low_rows[rows], terms[RIM:]], 0)
            action[k, :, lanes] = applied[at, :] - exx_share * terms

    copy.wait()
    copy = pltpu.make_async_copy(staged, potential, copied.at[1])
    copy.start()
    for start, stop, column in ((0, RIM_LEADS, from_below), (RIM_LEADS, HALF, None)):

        def part_step(index, start=start, column=column):
            apply(index + start, column=column, shift=start)

        for_leads(stop - start, part_step)
    copy.wait()


def shape_of(dims, dtype=jnp.bfloat16):
    return jax.ShapeDtypeStruct(dims, dtype)


def local(orbitals, anchors, pair_list, pair_count, core_density):
    mesh_x = lax.axis_size("gx")
    mesh_y = lax.axis_size("gy")
    own = orbitals[0, 0]
    flat_anchors = anchors.T
    slots = pair_list.shape[2]
    own_list = jnp.concatenate([pair_list[0, 0].T, jnp.broadcast_to(pair_count, (1, slots))], 0)
    own_list = jnp.pad(own_list, ((0, 5), (0, LANES - slots)))
    side_shape = shape_of((2 * RIM, FLAT))
    column_shape = shape_of((2, SIDE, RIM * SIDE))
    corner_shape = shape_of((2 * RIM, RIM * SIDE))
    around = [side_shape] * 2 + [column_shape] * 2 + [corner_shape] * 4

    core_shape = core_density.shape
    narrow_shapes = [
        (RIM, core_shape[1], LANES),
        (core_shape[0] // 2, 2 * RIM, LANES),
        (RIM // 2, 2 * RIM, LANES),
    ]
    grant = 64 * 1024 * 1024

    gathered = pl.pallas_call(
        functools.partial(gather_kernel, mesh_x, mesh_y),
        out_shape=around
        + [shape_of(dims) for dims in narrow_shapes]
        + [shape_of((5,) + own_list.shape, jnp.int32)],
        in_specs=[vmem, hbm, hbm],
        out_specs=[hbm] * 12,
        scratch_shapes=[
            pltpu.VMEM(side_shape.shape, jnp.bfloat16),
            pltpu.VMEM(side_shape.shape, jnp.bfloat16),
            pltpu.VMEM(core_shape, jnp.float32),
            pltpu.VMEM(narrow_shapes[0], jnp.bfloat16),
            pltpu.VMEM(narrow_shapes[1], jnp.bfloat16),
            pltpu.SemaphoreType.DMA((12,)),
            pltpu.SemaphoreType.DMA((12,)),
            pltpu.SemaphoreType.DMA((5,)),
        ],
        compiler_params=pltpu.CompilerParams(
            collective_id=0, has_side_effects=True, vmem_limit_bytes=grant
        ),
        name="gather_rims",
    )(own, core_density, own_list)
    pieces = gathered[:8]

    back_x = [((i + 1) % mesh_x, i) for i in range(mesh_x)]
    back_y = [((i + 1) % mesh_y, i) for i in range(mesh_y)]
    back_xy = [
        ((i + 1) % mesh_x * mesh_y + (j + 1) % mesh_y, i * mesh_y + j)
        for i in range(mesh_x)
        for j in range(mesh_y)
    ]
    core_rims = [
        lax.ppermute(gathered[8], "gx", back_x),
        lax.ppermute(gathered[9], "gy", back_y),
        lax.ppermute(gathered[10], ("gx", "gy"), back_xy),
    ]

    terms = pairs_call(mesh_x, mesh_y, flat_anchors, gathered[11], [own] + list(pieces))
    grid_shape = terms[1].shape
    *returned, applied, potential = pl.pallas_call(
        functools.partial(return_kernel, mesh_x, mesh_y),
        out_shape=[side_shape, column_shape]
        + [shape_of((BASE_X, LANES), jnp.float32), shape_of(core_shape, jnp.float32)],
        in_specs=[smem] + [hbm] * 10,
        out_specs=[hbm] * 4,
        scratch_shapes=[
            pltpu.VMEM((2,) + corner_shape.shape, jnp.bfloat16),
            pltpu.VMEM(side_shape.shape, jnp.bfloat16),
            pltpu.VMEM(side_shape.shape, jnp.bfloat16),
            pltpu.VMEM(grid_shape, jnp.float32),
            pltpu.VMEM(core_shape, jnp.float32),
            pltpu.VMEM(narrow_shapes[0], jnp.bfloat16),
            pltpu.VMEM(narrow_shapes[1], jnp.bfloat16),
            pltpu.VMEM(narrow_shapes[2], jnp.bfloat16),
            pltpu.VMEM(own.shape, jnp.bfloat16),
            pltpu.VMEM(core_shape, jnp.float32),
            pltpu.VMEM((BASE_X, LANES), jnp.float32),
            pltpu.SemaphoreType.DMA((12,)),
            pltpu.SemaphoreType.DMA((12,)),
            pltpu.SemaphoreType.DMA((10,)),
        ],
        compiler_params=pltpu.CompilerParams(
            collective_id=1, has_side_effects=True, vmem_limit_bytes=grant
        ),
        name="return_terms",
    )(flat_anchors, *terms[2:], terms[1], core_density, *core_rims, own)
    action, potential = pl.pallas_call(
        action_kernel,
        out_shape=[shape_of(own.shape, jnp.float32), shape_of(core_shape, jnp.float32)],
        in_specs=[vmem] * 4 + [hbm],
        out_specs=[vmem, hbm],
        scratch_shapes=[pltpu.VMEM(core_shape, jnp.float32), pltpu.SemaphoreType.DMA((2,))],
        compiler_params=pltpu.CompilerParams(vmem_limit_bytes=grant),
        name="action_terms",
    )(applied, terms[0], *returned, potential)
    return (action.reshape(orbitals.shape), potential)


def solution(mesh):
    placed = (
        P("gx", "gy", None, None, None),
        P(),
        P("gx", "gy", None, None),
        P("gx", "gy"),
        P("gx", "gy", None),
    )
    return jax.shard_map(
        local,
        mesh=mesh,
        in_specs=placed,
        out_specs=(P("gx", "gy", None, None, None), P("gx", "gy", None)),
        check_vma=False,
    )
```

```python
import functools
import math

import jax
import jax.numpy as jnp
from jax import lax
from jax.experimental import pallas as pl
from jax.experimental.pallas import tpu as pltpu
from jax.sharding import PartitionSpec as P

SWEEPS = 4
SIDE = 64
HALF = SIDE // 2
FLAT = SIDE * SIDE
RIM = 24
LOW = SIDE - RIM
RIM_LEADS = RIM // 2
LOW_LEADS = LOW // 2
LANES = 128
PAD = 512
CHUNKS = [(False, False, 32), (True, False, 32), (False, True, 12), (True, True, 12)]

screen_mass = 0.25
coupling = 2.0 * math.pi
exx_share = 0.25
xc_factor = (3.0 / math.pi) ** (1.0 / 3.0)

AHEAD = [2, 4, 7, 8]
BASE_X = 2 * HALF * SIDE
BASE_Y = BASE_X + 4 * HALF * RIM
BASE_C = BASE_Y + 4 * RIM_LEADS * SIDE
WINDOW_ROWS = BASE_C + 8 * RIM_LEADS * RIM
STEPS = [(0, 0), (-1, 0), (1, 0), (0, -1), (0, 1), (-1, -1), (-1, 1), (1, -1), (1, 1)]


def place_of(step_x, step_y):
    rows = SIDE if step_x == 0 else RIM
    leads = HALF if step_y == 0 else RIM_LEADS
    if step_x == 0 and step_y == 0:
        base = 0
    elif step_y == 0:
        base = BASE_X + (2 * HALF * RIM if step_x > 0 else 0)
    elif step_x == 0:
        base = BASE_Y + (2 * RIM_LEADS * SIDE if step_y > 0 else 0)
    else:
        base = BASE_C + ((2 if step_x > 0 else 0) + (1 if step_y > 0 else 0)) * 2 * RIM_LEADS * RIM
    return base, rows, leads


def sweep_weights(sweep_count):
    return [
        1.0 / (1.0 + 0.7 * math.cos(math.pi * (2 * order + 1) / (2 * sweep_count)))
        for order in range(sweep_count)
    ]


def lane_index(rows):
    return lax.broadcasted_iota(jnp.int32, (rows, LANES), 1)


def one_where(condition):
    return jnp.where(condition, 1.0, 0.0).astype(jnp.bfloat16)


def halves(value):
    upper = value.astype(jnp.bfloat16)
    lower = (value - upper.astype(jnp.float32)).astype(jnp.bfloat16)
    return jnp.concatenate([upper, lower], 1)


def for_leads(count, step):
    lax.fori_loop(0, count, lambda index, _: (step(index), 0)[1], 0)


def pair_kernel(mesh_x, mesh_y, anchors, lists, *refs):
    sources = refs[:9]
    own_out, grid_out = refs[9:11]
    targets_out = refs[11:15]
    (
        window,
        sums,
        near,
        turn_in,
        turn_out,
        moved3,
        source3,
        even3,
        odd3,
        moved8,
        source8,
        even8,
        odd8,
        grid,
        place,
        copies,
    ) = refs[15:31]
    pieces = refs[31:40]
    outs = refs[40:44]
    here_x = lax.axis_index("gx")
    here_y = lax.axis_index("gy")
    span_x = mesh_x * (SIDE - 16)
    span_y = mesh_y * (SIDE - 16)

    incoming = [
        pltpu.make_async_copy(source, piece, copies.at[2 + index])
        for index, (source, piece) in enumerate(zip(sources, pieces))
    ]
    for copy in incoming:
        copy.start()
    zeros64 = jnp.zeros((SIDE, LANES), jnp.float32)

    def clear_sums(lead):
        sums[pl.ds(pl.multiple_of(lead * SIDE, SIDE), SIDE), :] = zeros64

    for_leads((WINDOW_ROWS + 2 * PAD) // SIDE, clear_sums)

    def clear_ends(lead):
        for start in (0, PAD + WINDOW_ROWS):
            window[pl.ds(pl.multiple_of(start + lead * SIDE, SIDE), SIDE), :] = zeros64

    for_leads(PAD // SIDE, clear_ends)

    for field in (source3, even3, odd3, source8, even8, odd8):
        rows = field.shape[1]
        field[0] = jnp.zeros((rows, LANES), jnp.float32)

        def clear_edge(lead, field=field, rows=rows):
            edge = jnp.zeros((8, LANES), jnp.float32)
            field[lead, pl.ds(0, 8), :] = edge
            field[lead, pl.ds(rows - 8, 8), :] = edge

        for_leads(HALF + 2, clear_edge)

    from_lane = lax.broadcasted_iota(jnp.int32, (LANES, LANES), 0)
    to_lane = lax.broadcasted_iota(jnp.int32, (LANES, LANES), 1)
    swap = jnp.abs(to_lane - from_lane) == SIDE
    step = (jnp.abs(to_lane - from_lane) == 1) & ((to_lane < SIDE) == (from_lane < SIDE))
    for start in (0, LANES):
        near[start : start + LANES, :LANES] = one_where(step | swap)
        near[start : start + LANES, LANES:] = one_where(swap)

    def clear_grid(lead):
        start = pl.multiple_of(lead * GRID_ROWS, 8)
        grid[pl.ds(start, GRID_ROWS), :] = jnp.zeros((GRID_ROWS, LANES), jnp.float32)

    for_leads(GRID_ROWS, clear_grid)

    for (step_x, step_y), piece, copy in zip(STEPS, pieces, incoming):
        base, rows, leads = place_of(step_x, step_y)

        def widen(lead, base=base, rows=rows, leads=leads, piece=piece):
            lanes = pl.ds(pl.multiple_of(lead * LANES, LANES), LANES)
            if rows == RIM:
                both = piece[:, lanes].astype(jnp.float32)
            for k in range(2):
                start = pl.multiple_of(PAD + base + k * leads * rows + lead * rows, 8)
                if rows == RIM:
                    value = both[k * RIM : (k + 1) * RIM]
                else:
                    value = piece[k, :, lanes].astype(jnp.float32)
                window[pl.ds(start, rows), :] = value

        copy.wait()
        for_leads(leads, widen)

    weights = sweep_weights(SWEEPS)
    diagonal = 6.0 + screen_mass
    scale = [weight / diagonal for weight in weights]
    keep = [(1.0 - weight) / part for weight, part in zip(weights, scale)]
    total_scale = coupling * scale[0] * scale[1] * scale[2] * scale[3]

    def slot_of(offset_x, offset_y, k):
        plus_x = jnp.where(offset_x > 0, 1, 0)
        plus_y = jnp.where(offset_y > 0, 1, 0)
        rows = jnp.where(offset_x != 0, RIM, SIDE)
        leads = jnp.where(offset_y != 0, RIM_LEADS, HALF)
        base = jnp.where(
            offset_x != 0,
            jnp.where(
                offset_y != 0,
                BASE_C + (2 * plus_x + plus_y) * (2 * RIM_LEADS * RIM),
                BASE_X + plus_x * (2 * HALF * RIM),
            ),
            jnp.where(offset_y != 0, BASE_Y + plus_y * (2 * RIM_LEADS * SIDE), 0),
        )
        origin_x = jnp.where(offset_x < 0, LOW, 0)
        origin_lead = jnp.where(offset_y < 0, LOW_LEADS, 0)
        return PAD + base + k * leads * rows, rows, origin_x, origin_lead

    def pair_step(source, slot, carry):
        from_x = jnp.where((source >= 1) & (source <= 3), 1, 0)
        from_y = jnp.where(source == 1, -1, jnp.where(source >= 3, 1, 0))
        first = lists[source, 0, slot]
        second = lists[source, 1, slot]
        holder = lax.div(second, 2)
        to_x = lax.rem(lax.div(holder, mesh_y) - here_x + 1 + mesh_x, mesh_x) - 1
        to_y = lax.rem(lax.rem(holder, mesh_y) - here_y + 1 + mesh_y, mesh_y) - 1
        is_own = (to_x == 0) & (to_y == 0)
        ahead = (to_x == 1) | ((to_x == 0) & (to_y == 1))
        mine = is_own | (ahead & (source == 0))
        pl.when(mine)(functools.partial(pair_work, first, second, from_x, from_y, to_x, to_y))
        return carry

    def pair_work(first, second, from_x, from_y, to_x, to_y):
        step_x = to_x - from_x
        step_y = to_y - from_y
        shift_x = anchors[0, second] - anchors[0, first]
        shift_y = anchors[1, second] - anchors[1, first]
        shift_z = anchors[2, second] - anchors[2, first]
        shift_x = shift_x + jnp.where(shift_x < -(span_x // 2), span_x, 0) - jnp.where(
            shift_x >= span_x // 2, span_x, 0
        )
        shift_y = shift_y + jnp.where(shift_y < -(span_y // 2), span_y, 0) - jnp.where(
            shift_y >= span_y // 2, span_y, 0
        )
        half_y = lax.shift_right_arithmetic(shift_y, 1)
        odd_y = shift_y - 2 * half_y
        side_x = step_x != 0
        side_y = step_y != 0
        start_x = jnp.where(step_x > 0, LOW, 0)
        start_lead = jnp.where(step_y > 0, LOW_LEADS, 0)
        near_base, near_stride, near_x, near_lead = slot_of(from_x, from_y, lax.rem(first, 2))
        far_base, far_stride, far_x, far_lead = slot_of(to_x, to_y, lax.rem(second, 2))
        near_start = near_base + (start_lead - near_lead) * near_stride + start_x - near_x
        far_start = (
            far_base + (start_lead - half_y - far_lead) * far_stride + start_x - shift_x - far_x
        )
        from_lane = lax.broadcasted_iota(jnp.int32, (LANES, LANES), 0)
        to_lane = lax.broadcasted_iota(jnp.int32, (LANES, LANES), 1)
        apart = to_lane - from_lane - shift_z
        depth = lax.rem(to_lane, SIDE) - shift_z
        valid = (depth >= 0) & (depth < SIDE)
        same = valid & (apart == SIDE * odd_y)
        other = valid & (apart == -SIDE) & (odd_y == 1)
        turn_in[:LANES] = one_where(same)
        turn_in[LANES:] = one_where(other)
        from_lane, to_lane = to_lane, from_lane
        apart = to_lane - from_lane - shift_z
        depth = lax.rem(to_lane, SIDE) - shift_z
        valid = (depth >= 0) & (depth < SIDE)
        same = one_where(valid & (apart == SIDE * odd_y))
        other = one_where(valid & (apart == -SIDE) & (odd_y == 1))
        turn_out[:LANES, :LANES] = same
        turn_out[LANES:, :LANES] = same
        turn_out[:LANES, LANES:] = other
        turn_out[LANES:, LANES:] = other

        def run(tiles, leads, chunk, moved, source, even, odd):
            rows = tiles * 8
            inner = pl.ds(8, rows)
            lane = lane_index(rows)
            upper = lane >= SIDE
            row = lax.broadcasted_iota(jnp.int32, (rows, LANES), 0) + start_x
            column_part = jnp.where(upper, 1, 0) - shift_y
            inside_x = (row >= shift_x) & (row < SIDE + shift_x)

            def inside(lead):
                column = column_part + 2 * lead
                return inside_x & (column >= 0) & (column < SIDE)

            def far_rows(lead):
                return pl.ds(far_start + lead * far_stride, rows)

            def own_rows(lead):
                return pl.ds(pl.multiple_of(near_start + lead * near_stride, 8), rows)

            def part(value, index):
                return value[index * rows : (index + 1) * rows]

            def build(index):
                lead = index * chunk
                loads = [window[far_rows(lead + j), :] for j in range(-1, chunk)]
                now = jnp.concatenate(loads[1:], 0).astype(jnp.bfloat16)
                before = jnp.concatenate(loads[:-1], 0).astype(jnp.bfloat16)
                turned = jnp.dot(
                    jnp.concatenate([now, before], 1), turn_in[...], preferred_element_type=jnp.float32
                )
                for j in range(chunk):
                    piece = jnp.where(inside(start_lead + lead + j), part(turned, j), 0.0)
                    moved[lead + j] = piece
                    source[lead + j + 1, inner, :] = piece * window[own_rows(lead + j), :]

            def near_fields(field, lead):
                values = [field[lead + j, inner, :] for j in range(chunk + 2)]
                product = jnp.dot(
                    halves(jnp.concatenate(values, 0)), near[...], preferred_element_type=jnp.float32
                )
                for j in range(chunk):
                    across = jnp.where(
                        upper, part(product, j + 2)[:, LANES:], part(product, j)[:, LANES:]
                    )
                    beside = field[lead + j + 1, pl.ds(7, rows), :] + field[lead + j + 1, pl.ds(9, rows), :]
                    yield values[j + 1], (part(product, j + 1)[:, :LANES] + across) + beside

            def sweep(old, new, own_part, source_part):
                def body(index):
                    lead = index * chunk
                    for j, (here, near_sum) in enumerate(near_fields(old, lead)):
                        value = own_part * here + near_sum
                        if source_part is not None:
                            value = value + source_part * source[lead + j + 1, inner, :]
                        new[lead + j + 1, inner, :] = value

                return body

            def finish(index):
                lead = index * chunk
                back = []
                for j, (here, near_sum) in enumerate(near_fields(odd, lead)):
                    value = keep[3] * here + near_sum
                    value = value + (1.0 / (scale[0] * scale[1] * scale[2])) * source[lead + j + 1, inner, :]
                    value = value * total_scale
                    sums[own_rows(lead + j), :] = sums[own_rows(lead + j), :] + value * moved[lead + j]
                    back.append(
                        jnp.where(inside(start_lead + lead + j), value * window[own_rows(lead + j), :], 0.0)
                    )
                turned = jnp.dot(
                    halves(jnp.concatenate(back, 0)), turn_out[...], preferred_element_type=jnp.float32
                )
                targets = [sums[far_rows(lead + j), :] for j in range(-1, chunk)]
                for j in range(-1, chunk):
                    total = targets[j + 1]
                    if j >= 0:
                        total = total + part(turned, j)[:, :LANES]
                    if j + 1 < chunk:
                        total = total + part(turned, j + 1)[:, LANES:]
                    targets[j + 1] = total
                for j in range(-1, chunk):
                    sums[far_rows(lead + j), :] = targets[j + 1]

            edge = jnp.zeros((rows, LANES), jnp.float32)
            for field in (source, even, odd):
                field[leads + 1, inner, :] = edge
            chunks = leads // chunk
            for_leads(chunks, build)
            for_leads(chunks, sweep(source, even, keep[1] + 1.0 / scale[0], None))
            for_leads(chunks, sweep(even, odd, keep[2], 1.0 / (scale[0] * scale[1])))
            for_leads(chunks, finish)

        for has_x, has_y, chunk in CHUNKS:
            narrow = side_x if has_x else jnp.logical_not(side_x)
            narrow = narrow & (side_y if has_y else jnp.logical_not(side_y))
            fields = (moved3, source3, even3, odd3) if has_x else (moved8, source8, even8, odd8)

            @pl.when(narrow)
            def _(has_x=has_x, has_y=has_y, chunk=chunk, fields=fields):
                run(
                    (RIM if has_x else SIDE) // 8,
                    RIM_LEADS if has_y else HALF,
                    chunk,
                    *fields,
                )

    def list_step(source, carry):
        return lax.fori_loop(0, lists[source, 2, 0], functools.partial(pair_step, source), carry)

    lax.fori_loop(0, 5, list_step, 0)

    own_copy = pltpu.make_async_copy(sums.at[pl.ds(PAD, BASE_X)], own_out, copies.at[0])
    own_copy.start()

    outgoing = []
    for step, out, target in zip([STEPS[index] for index in AHEAD], outs, targets_out):
        base, rows, leads = place_of(*step)

        def narrow(lead, base=base, rows=rows, leads=leads, out=out):
            lanes = pl.ds(pl.multiple_of(lead * LANES, LANES), LANES)
            values = []
            for k in range(2):
                start = pl.multiple_of(PAD + base + k * leads * rows + lead * rows, 8)
                values.append(sums[pl.ds(start, rows), :])
            if rows == RIM:
                out[:, lanes] = jnp.concatenate(values, 0).astype(out.dtype)
            else:
                for k in range(2):
                    out[k, :, lanes] = values[k].astype(out.dtype)

        for_leads(leads, narrow)
        copy = pltpu.make_async_copy(out, target, copies.at[11 + len(outgoing)])
        copy.start()
        outgoing.append(copy)

    slab = SIDE - 16

    def deposit(step_x, step_y, k, base, rows, leads):
        holder_x = lax.rem(here_x + step_x + mesh_x, mesh_x)
        holder_y = lax.rem(here_y + step_y + mesh_y, mesh_y)
        orbit = (holder_x * mesh_y + holder_y) * 2 + k
        at_x = anchors[0, orbit] - holder_x * slab
        at_y = anchors[1, orbit] - holder_y * slab
        at_z = anchors[2, orbit]
        row = at_x + step_x * slab + GRID_PAD + jnp.where(step_x < 0, LOW, 0)
        column = at_y + step_y * slab + GRID_PAD + jnp.where(step_y < 0, LOW, 0)
        start = column * GRID_ROWS + row
        from_lane = lax.broadcasted_iota(jnp.int32, (LANES, LANES), 0)
        apart = lax.broadcasted_iota(jnp.int32, (LANES, LANES), 1) - from_lane - at_z
        low = one_where((from_lane < SIDE) & (apart == 0))
        high = one_where((from_lane >= SIDE) & (apart == -SIDE))
        place[:, :LANES] = low
        place[:, LANES:] = high
        block = 16
        for first in range(0, leads, block):
            size = min(block, leads - first)
            value = window[pl.ds(pl.multiple_of(PAD + base + first * rows, 8), size * rows), :]
            placed = jnp.dot(value.astype(jnp.bfloat16), place[...], preferred_element_type=jnp.float32)
            for j in range(size):
                for odd_column in (0, 1):
                    at = pl.ds(start + (2 * (first + j) + odd_column) * GRID_ROWS, rows)
                    part = placed[j * rows : (j + 1) * rows, odd_column * LANES : (odd_column + 1) * LANES]
                    grid[at, :] = grid[at, :] + part * part

    for k in range(2):
        deposit(0, 0, k, k * HALF * SIDE, SIDE, HALF)

    def deposit_x(index, carry):
        deposit(2 * (index // 2) - 1, 0, lax.rem(index, 2), BASE_X + index * (HALF * RIM), RIM, HALF)
        return carry

    def deposit_y(index, carry):
        deposit(
            0, 2 * (index // 2) - 1, lax.rem(index, 2), BASE_Y + index * (RIM_LEADS * SIDE), SIDE, RIM_LEADS
        )
        return carry

    def deposit_corner(index, carry):
        deposit(
            2 * (index // 4) - 1,
            2 * lax.rem(index // 2, 2) - 1,
            lax.rem(index, 2),
            BASE_C + index * (RIM_LEADS * RIM),
            RIM,
            RIM_LEADS,
        )
        return carry

    lax.fori_loop(0, 4, deposit_x, 0)
    lax.fori_loop(0, 4, deposit_y, 0)
    lax.fori_loop(0, 8, deposit_corner, 0)
    grid_copy = pltpu.make_async_copy(grid.at[pl.ds(GRID_PAD * GRID_ROWS, EDGE_ROWS)], grid_out, copies.at[1])
    grid_copy.start()
    for copy in [own_copy, *outgoing, grid_copy]:
        copy.wait()


GRID_PAD = 8
GRID_ROWS = 88
EDGE = SIDE - 16 + RIM
EDGE_ROWS = (EDGE + 1) * GRID_ROWS
hbm = pl.BlockSpec(memory_space=pl.ANY)
MESH = pl.DeviceIdType.MESH

smem = pl.BlockSpec(memory_space=pltpu.SMEM)
vmem = pl.BlockSpec(memory_space=pltpu.VMEM)


def pairs_call(mesh_x, mesh_y, flat_anchors, lists, pieces):
    term_shapes = [
        jax.ShapeDtypeStruct((BASE_X, LANES), jnp.float32),
        jax.ShapeDtypeStruct((EDGE_ROWS, LANES), jnp.float32),
    ] + [jax.ShapeDtypeStruct(pieces[index].shape, jnp.bfloat16) for index in AHEAD]

    def field(rows):
        return pltpu.VMEM((HALF + 2, rows, LANES), jnp.float32)

    return pl.pallas_call(
        functools.partial(pair_kernel, mesh_x, mesh_y),
        out_shape=term_shapes,
        in_specs=[smem] * 2 + [hbm] * 9,
        out_specs=[hbm] * 6,
        scratch_shapes=[
            pltpu.VMEM((WINDOW_ROWS + 2 * PAD, LANES), jnp.float32),
            pltpu.VMEM((WINDOW_ROWS + 2 * PAD, LANES), jnp.float32),
            pltpu.VMEM((2 * LANES, 2 * LANES), jnp.bfloat16),
            pltpu.VMEM((2 * LANES, LANES), jnp.bfloat16),
            pltpu.VMEM((2 * LANES, 2 * LANES), jnp.bfloat16),
            pltpu.VMEM((HALF, RIM, LANES), jnp.float32),
            field(RIM + 16),
            field(RIM + 16),
            field(RIM + 16),
            pltpu.VMEM((HALF, SIDE, LANES), jnp.float32),
            field(SIDE + 16),
            field(SIDE + 16),
            field(SIDE + 16),
            pltpu.VMEM((GRID_ROWS * GRID_ROWS, LANES), jnp.float32),
            pltpu.VMEM((LANES, 2 * LANES), jnp.bfloat16),
            pltpu.SemaphoreType.DMA((19,)),
        ]
        + [pltpu.VMEM(piece.shape, jnp.bfloat16) for piece in pieces]
        + [pltpu.VMEM(pieces[index].shape, jnp.bfloat16) for index in AHEAD],
        compiler_params=pltpu.CompilerParams(vmem_limit_bytes=64 * 1024 * 1024),
        cost_estimate=pl.CostEstimate(flops=40_000_000, bytes_accessed=8_000_000, transcendentals=0),
        name="pair_terms",
    )(flat_anchors, lists, *pieces)


def cube_root(value):
    inverse = jnp.exp(jnp.log(value) * (-1.0 / 3.0))
    inverse = inverse * (4.0 - value * inverse * inverse * inverse) * (1.0 / 3.0)
    return value * inverse * inverse


def greet(mesh_x, mesh_y, diagonal=False):
    here_x = lax.axis_index("gx")
    here_y = lax.axis_index("gy")
    left = (lax.rem(here_x + mesh_x - 1, mesh_x), here_y)
    right = (lax.rem(here_x + 1, mesh_x), here_y)
    below = (here_x, lax.rem(here_y + mesh_y - 1, mesh_y))
    above = (here_x, lax.rem(here_y + 1, mesh_y))
    barrier = pltpu.get_barrier_semaphore()
    neighbours = [left, right, below, above]
    if diagonal:
        neighbours += [(side[0], end[1]) for side in (left, right) for end in (below, above)]
    for neighbour in neighbours:
        pl.semaphore_signal(barrier, inc=1, device_id=neighbour, device_id_type=MESH)
    pl.semaphore_wait(barrier, len(neighbours))
    return left, right, below, above


def gather_kernel(mesh_x, mesh_y, count, pairs, own, core_source, *refs):
    outs = refs[:8]
    narrow_outs = refs[8:11]
    lists = refs[11]
    send_low, send_high, core, narrow_x, narrow_y, list_source, sent, landed, copies = refs[12:]
    slots = pairs.shape[1]
    list_source[...] = jnp.full(list_source.shape, count[0], jnp.int32)
    list_source[0:2, 0:slots] = pairs[...]
    core_copy = pltpu.make_async_copy(core_source, core, copies.at[3])
    core_copy.start()
    list_copy = pltpu.make_async_copy(list_source, lists.at[0], copies.at[4])
    list_copy.start()
    left, right, below, above = greet(mesh_x, mesh_y, diagonal=True)
    started = []

    def send(source, slot, device, target=None):
        copy = pltpu.make_async_remote_copy(
            src_ref=source,
            dst_ref=outs[slot] if target is None else target,
            send_sem=sent.at[slot],
            recv_sem=landed.at[slot],
            device_id=device,
            device_id_type=MESH,
        )
        copy.start()
        started.append(copy)
        return copy

    def prepare(lead):
        lanes = pl.ds(pl.multiple_of(lead * LANES, LANES), LANES)
        values = [own[k, :, lanes].astype(jnp.float32) for k in range(2)]
        send_low[:, lanes] = jnp.concatenate([value[:RIM] for value in values], 0).astype(jnp.bfloat16)
        send_high[:, lanes] = jnp.concatenate([value[LOW:] for value in values], 0).astype(jnp.bfloat16)

    for_leads(HALF, prepare)
    from_left = send(send_high, 0, right)
    from_right = send(send_low, 1, left)
    high = pl.ds(LOW * SIDE, RIM * SIDE)
    low = pl.ds(0, RIM * SIDE)
    send(own.at[:, :, high], 2, above)
    send(own.at[:, :, low], 3, below)
    for index, device in enumerate(((left[0], above[1]), left, (left[0], below[1]), below)):
        send(list_source, 8 + index, device, target=lists.at[1 + index])
    core_copy.wait()

    def narrow(row):
        narrow_x[row] = core[row].astype(jnp.bfloat16)
        narrow_y[row] = jnp.concatenate([core[2 * row, :RIM], core[2 * row + 1, :RIM]], 0).astype(jnp.bfloat16)

    for_leads(RIM, narrow)
    narrow_copies = [
        pltpu.make_async_copy(source, target, copies.at[index])
        for index, (source, target) in enumerate(
            zip((narrow_x, narrow_y, narrow_y.at[pl.ds(0, RIM // 2)]), narrow_outs)
        )
    ]
    for copy in narrow_copies:
        copy.start()
    from_left.wait_recv()
    send(outs[0].at[:, high], 4, above)
    send(outs[0].at[:, low], 5, below)
    from_right.wait_recv()
    send(outs[1].at[:, high], 6, above)
    send(outs[1].at[:, low], 7, below)
    for copy in started:
        copy.wait_send()
    for copy in started[2:]:
        copy.wait_recv()
    for copy in narrow_copies:
        copy.wait()
    list_copy.wait()


def return_kernel(mesh_x, mesh_y, anchors, *refs):
    side_source, column_terms = refs[:2]
    corner_terms = refs[2:4]
    narrow_x, narrow_y, narrow_xy = refs[4:7]
    out_side, out_column, applied_out, potential_out = refs[11:15]
    landed_corners, send_right, right_terms = refs[15:18]
    loads = refs[18:22]
    density, core, own, applied = loads
    core_x, core_y, core_xy, potential, sent, landed, copies = refs[22:]
    here_x = lax.axis_index("gx")
    here_y = lax.axis_index("gy")
    incoming = [
        pltpu.make_async_copy(source, target, copies.at[index])
        for index, (source, target) in enumerate(zip(refs[7:11] + (side_source,), loads + (right_terms,)))
    ]
    left, right, below, above = greet(mesh_x, mesh_y, diagonal=True)

    def send(source, target, slot, device):
        copy = pltpu.make_async_remote_copy(
            src_ref=source,
            dst_ref=target,
            send_sem=sent.at[slot],
            recv_sem=landed.at[slot],
            device_id=device,
            device_id_type=MESH,
        )
        copy.start()
        return copy

    corners = [
        send(corner_terms[slot], landed_corners.at[slot], slot, device)
        for slot, device in enumerate((below, above))
    ]
    high = pl.ds(LOW * SIDE, RIM * SIDE)
    low = pl.ds(0, RIM * SIDE)
    middle = pl.ds(RIM * SIDE, (LOW - RIM) * SIDE)
    others = [send(side_source.at[:, middle], out_side.at[:, middle], 2, right)]
    from_right = send(narrow_x, core_x, 6, left)
    for copy in incoming:
        copy.start()
    for copy in incoming:
        copy.wait()
    slab = core.shape[0]

    def finish_at(row, column, core_part):
        at = pl.ds(column * GRID_ROWS + GRID_PAD + row, 8, stride=GRID_ROWS)
        value = -xc_factor * cube_root(density[at, :] + core_part)
        density[at, :] = value
        return value

    def own_rows(row):
        for column in range(0, slab, 8):
            potential[row, pl.ds(column, 8), :] = finish_at(row, column, core[row, pl.ds(column, 8), :])

    def right_rows(row):
        beside = core_x[row].astype(jnp.float32)
        for column in range(0, slab, 8):
            finish_at(slab + row, column, beside[column : column + 8])

    def above_rows(pair, source=core_y, beyond=0):
        part = source[pair].astype(jnp.float32)
        for j in range(2):
            for column in range(0, RIM, 8):
                start = j * RIM + column
                finish_at(beyond + 2 * pair + j, slab + column, part[start : start + 8])

    def corner_rows(pair):
        above_rows(pair, source=core_xy, beyond=slab)

    for_leads(slab, own_rows)
    from_above = send(narrow_y, core_y, 7, below)
    from_corner = send(narrow_xy, core_xy, 8, (left[0], below[1]))
    others.append(send(column_terms, out_column, 3, above))
    potential_copy = pltpu.make_async_copy(potential, potential_out, copies.at[7])
    potential_copy.start()
    for corner, (first, columns) in enumerate(((LOW_LEADS, high), (0, low))):
        corners[corner].wait_recv()

        def merge(index, first=first, corner=corner):
            lanes = pl.ds(pl.multiple_of((index + first) * LANES, LANES), LANES)
            at = pl.ds(pl.multiple_of(index * LANES, LANES), LANES)
            value = right_terms[:, lanes].astype(jnp.float32) + landed_corners[corner, :, at].astype(jnp.float32)
            send_right[:, lanes] = value.astype(jnp.bfloat16)

        for_leads(RIM_LEADS, merge)
        others.append(send(send_right.at[:, columns], out_side.at[:, columns], 4 + corner, right))
    from_right.wait()
    for_leads(RIM, right_rows)
    from_above.wait()
    for_leads(slab // 2, above_rows)
    from_corner.wait()
    for_leads(RIM // 2, corner_rows)

    lane = lane_index(SIDE)
    orbit = (here_x * mesh_y + here_y) * 2
    for k in range(2):
        at_x = jnp.clip(anchors[0, orbit + k] - here_x * slab, 0, GRID_PAD - 1)
        at_y = jnp.clip(anchors[1, orbit + k] - here_y * slab, 0, GRID_PAD - 1)
        at_z = anchors[2, orbit + k]
        start = at_y * GRID_ROWS + at_x + GRID_PAD
        turn_low = lax.rem(LANES - at_z, LANES)
        turn_high = lax.rem(LANES + SIDE - at_z, LANES)

        def sample(lead, k=k, start=start, turn_low=turn_low, turn_high=turn_high):
            lanes = pl.ds(pl.multiple_of(lead * LANES, LANES), LANES)
            low = density[pl.ds(start + 2 * lead * GRID_ROWS, SIDE), :]
            high = density[pl.ds(start + (2 * lead + 1) * GRID_ROWS, SIDE), :]
            sampled = jnp.where(lane < SIDE, pltpu.roll(low, turn_low, 1), pltpu.roll(high, turn_high, 1))
            at = pl.ds(pl.multiple_of((k * HALF + lead) * SIDE, SIDE), SIDE)
            applied[at, :] = sampled * own[k, :, lanes].astype(jnp.float32) - exx_share * applied[at, :]

        for_leads(HALF, sample)
    applied_copy = pltpu.make_async_copy(applied, applied_out, copies.at[8])
    applied_copy.start()
    for copy in corners:
        copy.wait_send()
    for copy in others:
        copy.wait()
    applied_copy.wait()
    potential_copy.wait()


STEP_LEADS = 4


def action_kernel(applied, from_left, from_below, potential_source, action, potential, staged, copied):
    step = pl.program_id(0)
    steps = HALF // STEP_LEADS
    load = pltpu.make_async_copy(potential_source, staged, copied.at[0])
    store = pltpu.make_async_copy(staged, potential, copied.at[1])

    @pl.when(step == 0)
    def _():
        load.start()

    @pl.when(step == 2)
    def _():
        load.wait()
        store.start()

    def apply(column):
        for lead in range(STEP_LEADS):
            lanes = slice(lead * LANES, (lead + 1) * LANES)
            low_rows = from_left[:, lanes].astype(jnp.float32)
            for k in range(2):
                value = applied[k, lead * SIDE : (lead + 1) * SIDE, :]
                terms = low_rows[k * RIM : (k + 1) * RIM]
                if column:
                    beside = from_below[k, :, lanes].astype(jnp.float32)
                    action[k, :RIM, lanes] = value[:RIM] - exx_share * (terms + beside[:RIM])
                    action[k, RIM:, lanes] = value[RIM:] - exx_share * beside[RIM:]
                else:
                    action[k, :RIM, lanes] = value[:RIM] - exx_share * terms
                    action[k, RIM:, lanes] = value[RIM:]

    @pl.when(step < RIM_LEADS // STEP_LEADS)
    def _():
        apply(True)

    @pl.when(step >= RIM_LEADS // STEP_LEADS)
    def _():
        apply(False)

    @pl.when(step == steps - 1)
    def _():
        store.wait()


def shape_of(dims, dtype=jnp.bfloat16):
    return jax.ShapeDtypeStruct(dims, dtype)


def local(orbitals, anchors, pair_list, pair_count, core_density):
    mesh_x = lax.axis_size("gx")
    mesh_y = lax.axis_size("gy")
    own = orbitals[0, 0]
    flat_anchors = anchors.T
    flat_pairs = pair_list[0, 0].T
    flat_count = pair_count.reshape(-1)
    list_shape = (8, LANES)
    side_shape = shape_of((2 * RIM, FLAT))
    column_shape = shape_of((2, SIDE, RIM * SIDE))
    corner_shape = shape_of((2 * RIM, RIM * SIDE))
    around = [side_shape] * 2 + [column_shape] * 2 + [corner_shape] * 4

    core_shape = core_density.shape
    narrow_shapes = [
        (RIM, core_shape[1], LANES),
        (core_shape[0] // 2, 2 * RIM, LANES),
        (RIM // 2, 2 * RIM, LANES),
    ]
    grant = 64 * 1024 * 1024

    gathered = pl.pallas_call(
        functools.partial(gather_kernel, mesh_x, mesh_y),
        out_shape=around
        + [shape_of(dims) for dims in narrow_shapes]
        + [shape_of((5,) + list_shape, jnp.int32)],
        in_specs=[smem, vmem, vmem, hbm],
        out_specs=[hbm] * 12,
        scratch_shapes=[
            pltpu.VMEM(side_shape.shape, jnp.bfloat16),
            pltpu.VMEM(side_shape.shape, jnp.bfloat16),
            pltpu.VMEM(core_shape, jnp.float32),
            pltpu.VMEM(narrow_shapes[0], jnp.bfloat16),
            pltpu.VMEM(narrow_shapes[1], jnp.bfloat16),
            pltpu.VMEM(list_shape, jnp.int32),
            pltpu.SemaphoreType.DMA((12,)),
            pltpu.SemaphoreType.DMA((12,)),
            pltpu.SemaphoreType.DMA((5,)),
        ],
        compiler_params=pltpu.CompilerParams(
            collective_id=0, has_side_effects=True, vmem_limit_bytes=grant
        ),
        name="gather_rims",
    )(flat_count, flat_pairs, own, core_density)
    pieces = gathered[:8]

    terms = pairs_call(mesh_x, mesh_y, flat_anchors, gathered[11], [own] + list(pieces))
    grid_shape = terms[1].shape
    *returned, applied, potential = pl.pallas_call(
        functools.partial(return_kernel, mesh_x, mesh_y),
        out_shape=[side_shape, column_shape]
        + [shape_of((BASE_X, LANES), jnp.float32), shape_of(core_shape, jnp.float32)],
        in_specs=[smem] + [hbm] * 11,
        out_specs=[hbm] * 4,
        scratch_shapes=[
            pltpu.VMEM((2,) + corner_shape.shape, jnp.bfloat16),
            pltpu.VMEM(side_shape.shape, jnp.bfloat16),
            pltpu.VMEM(side_shape.shape, jnp.bfloat16),
            pltpu.VMEM(grid_shape, jnp.float32),
            pltpu.VMEM(core_shape, jnp.float32),
            pltpu.VMEM(own.shape, jnp.bfloat16),
            pltpu.VMEM((BASE_X, LANES), jnp.float32),
            pltpu.VMEM(narrow_shapes[0], jnp.bfloat16),
            pltpu.VMEM(narrow_shapes[1], jnp.bfloat16),
            pltpu.VMEM(narrow_shapes[2], jnp.bfloat16),
            pltpu.VMEM(core_shape, jnp.float32),
            pltpu.SemaphoreType.DMA((12,)),
            pltpu.SemaphoreType.DMA((12,)),
            pltpu.SemaphoreType.DMA((10,)),
        ],
        compiler_params=pltpu.CompilerParams(
            collective_id=1, has_side_effects=True, vmem_limit_bytes=grant
        ),
        name="return_terms",
    )(flat_anchors, *terms[2:], *gathered[8:11], terms[1], core_density, own, terms[0])
    span = STEP_LEADS * LANES
    rim_steps = RIM_LEADS // STEP_LEADS
    action, potential = pl.pallas_call(
        action_kernel,
        grid=(HALF // STEP_LEADS,),
        out_shape=[shape_of(own.shape, jnp.float32), shape_of(core_shape, jnp.float32)],
        in_specs=[
            pl.BlockSpec((2, STEP_LEADS * SIDE, LANES), lambda step: (0, step, 0)),
            pl.BlockSpec((2 * RIM, span), lambda step: (0, step)),
            pl.BlockSpec((2, SIDE, span), lambda step: (0, 0, jnp.minimum(step, rim_steps - 1))),
            hbm,
        ],
        out_specs=[pl.BlockSpec((2, SIDE, span), lambda step: (0, 0, step)), hbm],
        scratch_shapes=[pltpu.VMEM(core_shape, jnp.float32), pltpu.SemaphoreType.DMA((2,))],
        compiler_params=pltpu.CompilerParams(vmem_limit_bytes=grant),
        name="action_terms",
    )(applied.reshape(2, HALF * SIDE, LANES), *returned, potential)
    return (action.reshape(orbitals.shape), potential)


def solution(mesh):
    placed = (
        P("gx", "gy", None, None, None),
        P(),
        P("gx", "gy", None, None),
        P("gx", "gy"),
        P("gx", "gy", None),
    )
    return jax.shard_map(
        local,
        mesh=mesh,
        in_specs=placed,
        out_specs=(P("gx", "gy", None, None, None), P("gx", "gy", None)),
        check_vma=False,
    )
```

```python
import functools
import math

import jax
import jax.numpy as jnp
from jax import lax
from jax.experimental import pallas as pl
from jax.experimental.pallas import tpu as pltpu
from jax.sharding import PartitionSpec as P

SWEEPS = 4
SIDE = 64
HALF = SIDE // 2
FLAT = SIDE * SIDE
RIM = 24
LOW = SIDE - RIM
RIM_LEADS = RIM // 2
LOW_LEADS = LOW // 2
LANES = 128
PAD = 512
CHUNKS = [(False, False, 32), (True, False, 32), (False, True, 12), (True, True, 12)]

screen_mass = 0.25
coupling = 2.0 * math.pi
exx_share = 0.25
xc_factor = (3.0 / math.pi) ** (1.0 / 3.0)

AHEAD = [2, 4, 7, 8]
BASE_X = 2 * HALF * SIDE
BASE_Y = BASE_X + 4 * HALF * RIM
BASE_C = BASE_Y + 4 * RIM_LEADS * SIDE
WINDOW_ROWS = BASE_C + 8 * RIM_LEADS * RIM
STEPS = [(0, 0), (-1, 0), (1, 0), (0, -1), (0, 1), (-1, -1), (-1, 1), (1, -1), (1, 1)]


def place_of(step_x, step_y):
    rows = SIDE if step_x == 0 else RIM
    leads = HALF if step_y == 0 else RIM_LEADS
    if step_x == 0 and step_y == 0:
        base = 0
    elif step_y == 0:
        base = BASE_X + (2 * HALF * RIM if step_x > 0 else 0)
    elif step_x == 0:
        base = BASE_Y + (2 * RIM_LEADS * SIDE if step_y > 0 else 0)
    else:
        base = BASE_C + ((2 if step_x > 0 else 0) + (1 if step_y > 0 else 0)) * 2 * RIM_LEADS * RIM
    return base, rows, leads


def sweep_weights(sweep_count):
    return [
        1.0 / (1.0 + 0.7 * math.cos(math.pi * (2 * order + 1) / (2 * sweep_count)))
        for order in range(sweep_count)
    ]


def lane_index(rows):
    return lax.broadcasted_iota(jnp.int32, (rows, LANES), 1)


def one_where(condition):
    return jnp.where(condition, 1.0, 0.0).astype(jnp.bfloat16)


def halves(value):
    upper = value.astype(jnp.bfloat16)
    lower = (value - upper.astype(jnp.float32)).astype(jnp.bfloat16)
    return jnp.concatenate([upper, lower], 1)


def for_leads(count, step):
    lax.fori_loop(0, count, lambda index, _: (step(index), 0)[1], 0)


def pair_kernel(mesh_x, mesh_y, anchors, lists, *refs):
    sources = refs[:9]
    own_out, grid_out = refs[9:11]
    targets_out = refs[11:15]
    (
        window,
        sums,
        near,
        turn_in,
        turn_out,
        moved3,
        source3,
        even3,
        odd3,
        moved8,
        source8,
        even8,
        odd8,
        grid,
        place,
        copies,
    ) = refs[15:31]
    pieces = refs[31:40]
    outs = refs[40:44]
    here_x = lax.axis_index("gx")
    here_y = lax.axis_index("gy")
    span_x = mesh_x * (SIDE - 16)
    span_y = mesh_y * (SIDE - 16)

    incoming = [
        pltpu.make_async_copy(source, piece, copies.at[2 + index])
        for index, (source, piece) in enumerate(zip(sources, pieces))
    ]
    for copy in incoming:
        copy.start()
    zeros64 = jnp.zeros((SIDE, LANES), jnp.float32)

    def clear_sums(lead):
        sums[pl.ds(pl.multiple_of(lead * SIDE, SIDE), SIDE), :] = zeros64

    for_leads((WINDOW_ROWS + 2 * PAD) // SIDE, clear_sums)

    def clear_ends(lead):
        for start in (0, PAD + WINDOW_ROWS):
            window[pl.ds(pl.multiple_of(start + lead * SIDE, SIDE), SIDE), :] = zeros64

    for_leads(PAD // SIDE, clear_ends)

    for field in (source3, even3, odd3, source8, even8, odd8):
        rows = field.shape[1]
        field[0] = jnp.zeros((rows, LANES), jnp.float32)

        def clear_edge(lead, field=field, rows=rows):
            edge = jnp.zeros((8, LANES), jnp.float32)
            field[lead, pl.ds(0, 8), :] = edge
            field[lead, pl.ds(rows - 8, 8), :] = edge

        for_leads(HALF + 2, clear_edge)

    from_lane = lax.broadcasted_iota(jnp.int32, (LANES, LANES), 0)
    to_lane = lax.broadcasted_iota(jnp.int32, (LANES, LANES), 1)
    swap = jnp.abs(to_lane - from_lane) == SIDE
    step = (jnp.abs(to_lane - from_lane) == 1) & ((to_lane < SIDE) == (from_lane < SIDE))
    for start in (0, LANES):
        near[start : start + LANES, :LANES] = one_where(step | swap)
        near[start : start + LANES, LANES:] = one_where(swap)

    def clear_grid(lead):
        start = pl.multiple_of(lead * GRID_ROWS, 8)
        grid[pl.ds(start, GRID_ROWS), :] = jnp.zeros((GRID_ROWS, LANES), jnp.float32)

    for_leads(GRID_ROWS, clear_grid)

    for (step_x, step_y), piece, copy in zip(STEPS, pieces, incoming):
        base, rows, leads = place_of(step_x, step_y)

        def widen(lead, base=base, rows=rows, leads=leads, piece=piece):
            lanes = pl.ds(pl.multiple_of(lead * LANES, LANES), LANES)
            if rows == RIM:
                both = piece[:, lanes].astype(jnp.float32)
            for k in range(2):
                start = pl.multiple_of(PAD + base + k * leads * rows + lead * rows, 8)
                if rows == RIM:
                    value = both[k * RIM : (k + 1) * RIM]
                else:
                    value = piece[k, :, lanes].astype(jnp.float32)
                window[pl.ds(start, rows), :] = value

        copy.wait()
        for_leads(leads, widen)

    weights = sweep_weights(SWEEPS)
    diagonal = 6.0 + screen_mass
    scale = [weight / diagonal for weight in weights]
    keep = [(1.0 - weight) / part for weight, part in zip(weights, scale)]
    total_scale = coupling * scale[0] * scale[1] * scale[2] * scale[3]

    def slot_of(offset_x, offset_y, k):
        plus_x = jnp.where(offset_x > 0, 1, 0)
        plus_y = jnp.where(offset_y > 0, 1, 0)
        rows = jnp.where(offset_x != 0, RIM, SIDE)
        leads = jnp.where(offset_y != 0, RIM_LEADS, HALF)
        base = jnp.where(
            offset_x != 0,
            jnp.where(
                offset_y != 0,
                BASE_C + (2 * plus_x + plus_y) * (2 * RIM_LEADS * RIM),
                BASE_X + plus_x * (2 * HALF * RIM),
            ),
            jnp.where(offset_y != 0, BASE_Y + plus_y * (2 * RIM_LEADS * SIDE), 0),
        )
        origin_x = jnp.where(offset_x < 0, LOW, 0)
        origin_lead = jnp.where(offset_y < 0, LOW_LEADS, 0)
        return PAD + base + k * leads * rows, rows, origin_x, origin_lead

    def pair_step(source, slot, carry):
        from_x = jnp.where((source >= 1) & (source <= 3), 1, 0)
        from_y = jnp.where(source == 1, -1, jnp.where(source >= 3, 1, 0))
        first = lists[source, 0, slot]
        second = lists[source, 1, slot]
        holder = lax.div(second, 2)
        to_x = lax.rem(lax.div(holder, mesh_y) - here_x + 1 + mesh_x, mesh_x) - 1
        to_y = lax.rem(lax.rem(holder, mesh_y) - here_y + 1 + mesh_y, mesh_y) - 1
        is_own = (to_x == 0) & (to_y == 0)
        ahead = (to_x == 1) | ((to_x == 0) & (to_y == 1))
        mine = is_own | (ahead & (source == 0))
        pl.when(mine)(functools.partial(pair_work, first, second, from_x, from_y, to_x, to_y))
        return carry

    def pair_work(first, second, from_x, from_y, to_x, to_y):
        step_x = to_x - from_x
        step_y = to_y - from_y
        shift_x = anchors[0, second] - anchors[0, first]
        shift_y = anchors[1, second] - anchors[1, first]
        shift_z = anchors[2, second] - anchors[2, first]
        shift_x = shift_x + jnp.where(shift_x < -(span_x // 2), span_x, 0) - jnp.where(
            shift_x >= span_x // 2, span_x, 0
        )
        shift_y = shift_y + jnp.where(shift_y < -(span_y // 2), span_y, 0) - jnp.where(
            shift_y >= span_y // 2, span_y, 0
        )
        half_y = lax.shift_right_arithmetic(shift_y, 1)
        odd_y = shift_y - 2 * half_y
        side_x = step_x != 0
        side_y = step_y != 0
        start_x = jnp.where(step_x > 0, LOW, 0)
        start_lead = jnp.where(step_y > 0, LOW_LEADS, 0)
        near_base, near_stride, near_x, near_lead = slot_of(from_x, from_y, lax.rem(first, 2))
        far_base, far_stride, far_x, far_lead = slot_of(to_x, to_y, lax.rem(second, 2))
        near_start = near_base + (start_lead - near_lead) * near_stride + start_x - near_x
        far_start = (
            far_base + (start_lead - half_y - far_lead) * far_stride + start_x - shift_x - far_x
        )
        from_lane = lax.broadcasted_iota(jnp.int32, (LANES, LANES), 0)
        to_lane = lax.broadcasted_iota(jnp.int32, (LANES, LANES), 1)
        apart = to_lane - from_lane - shift_z
        depth = lax.rem(to_lane, SIDE) - shift_z
        valid = (depth >= 0) & (depth < SIDE)
        same = valid & (apart == SIDE * odd_y)
        other = valid & (apart == -SIDE) & (odd_y == 1)
        turn_in[:LANES] = one_where(same)
        turn_in[LANES:] = one_where(other)
        from_lane, to_lane = to_lane, from_lane
        apart = to_lane - from_lane - shift_z
        depth = lax.rem(to_lane, SIDE) - shift_z
        valid = (depth >= 0) & (depth < SIDE)
        same = one_where(valid & (apart == SIDE * odd_y))
        other = one_where(valid & (apart == -SIDE) & (odd_y == 1))
        turn_out[:LANES, :LANES] = same
        turn_out[LANES:, :LANES] = same
        turn_out[:LANES, LANES:] = other
        turn_out[LANES:, LANES:] = other

        def run(tiles, leads, chunk, moved, source, even, odd):
            rows = tiles * 8
            inner = pl.ds(8, rows)
            lane = lane_index(rows)
            upper = lane >= SIDE
            row = lax.broadcasted_iota(jnp.int32, (rows, LANES), 0) + start_x
            column_part = jnp.where(upper, 1, 0) - shift_y
            inside_x = (row >= shift_x) & (row < SIDE + shift_x)

            def inside(lead):
                column = column_part + 2 * lead
                return inside_x & (column >= 0) & (column < SIDE)

            def far_rows(lead):
                return pl.ds(far_start + lead * far_stride, rows)

            def own_rows(lead):
                return pl.ds(pl.multiple_of(near_start + lead * near_stride, 8), rows)

            def part(value, index):
                return value[index * rows : (index + 1) * rows]

            def build(index):
                lead = index * chunk
                loads = [window[far_rows(lead + j), :] for j in range(-1, chunk)]
                now = jnp.concatenate(loads[1:], 0).astype(jnp.bfloat16)
                before = jnp.concatenate(loads[:-1], 0).astype(jnp.bfloat16)
                turned = jnp.dot(
                    jnp.concatenate([now, before], 1), turn_in[...], preferred_element_type=jnp.float32
                )
                for j in range(chunk):
                    piece = jnp.where(inside(start_lead + lead + j), part(turned, j), 0.0)
                    moved[lead + j] = piece
                    source[lead + j + 1, inner, :] = piece * window[own_rows(lead + j), :]

            def near_fields(field, lead):
                values = [field[lead + j, inner, :] for j in range(chunk + 2)]
                product = jnp.dot(
                    halves(jnp.concatenate(values, 0)), near[...], preferred_element_type=jnp.float32
                )
                for j in range(chunk):
                    across = jnp.where(
                        upper, part(product, j + 2)[:, LANES:], part(product, j)[:, LANES:]
                    )
                    beside = field[lead + j + 1, pl.ds(7, rows), :] + field[lead + j + 1, pl.ds(9, rows), :]
                    yield values[j + 1], (part(product, j + 1)[:, :LANES] + across) + beside

            def sweep(old, new, own_part, source_part):
                def body(index):
                    lead = index * chunk
                    for j, (here, near_sum) in enumerate(near_fields(old, lead)):
                        value = own_part * here + near_sum
                        if source_part is not None:
                            value = value + source_part * source[lead + j + 1, inner, :]
                        new[lead + j + 1, inner, :] = value

                return body

            def finish(index):
                lead = index * chunk
                back = []
                for j, (here, near_sum) in enumerate(near_fields(odd, lead)):
                    value = keep[3] * here + near_sum
                    value = value + (1.0 / (scale[0] * scale[1] * scale[2])) * source[lead + j + 1, inner, :]
                    value = value * total_scale
                    sums[own_rows(lead + j), :] = sums[own_rows(lead + j), :] + value * moved[lead + j]
                    back.append(
                        jnp.where(inside(start_lead + lead + j), value * window[own_rows(lead + j), :], 0.0)
                    )
                turned = jnp.dot(
                    halves(jnp.concatenate(back, 0)), turn_out[...], preferred_element_type=jnp.float32
                )
                targets = [sums[far_rows(lead + j), :] for j in range(-1, chunk)]
                for j in range(-1, chunk):
                    total = targets[j + 1]
                    if j >= 0:
                        total = total + part(turned, j)[:, :LANES]
                    if j + 1 < chunk:
                        total = total + part(turned, j + 1)[:, LANES:]
                    targets[j + 1] = total
                for j in range(-1, chunk):
                    sums[far_rows(lead + j), :] = targets[j + 1]

            edge = jnp.zeros((rows, LANES), jnp.float32)
            for field in (source, even, odd):
                field[leads + 1, inner, :] = edge
            chunks = leads // chunk
            for_leads(chunks, build)
            for_leads(chunks, sweep(source, even, keep[1] + 1.0 / scale[0], None))
            for_leads(chunks, sweep(even, odd, keep[2], 1.0 / (scale[0] * scale[1])))
            for_leads(chunks, finish)

        for has_x, has_y, chunk in CHUNKS:
            narrow = side_x if has_x else jnp.logical_not(side_x)
            narrow = narrow & (side_y if has_y else jnp.logical_not(side_y))
            fields = (moved3, source3, even3, odd3) if has_x else (moved8, source8, even8, odd8)

            @pl.when(narrow)
            def _(has_x=has_x, has_y=has_y, chunk=chunk, fields=fields):
                run(
                    (RIM if has_x else SIDE) // 8,
                    RIM_LEADS if has_y else HALF,
                    chunk,
                    *fields,
                )

    def list_step(source, carry):
        return lax.fori_loop(0, lists[source, 2, 0], functools.partial(pair_step, source), carry)

    lax.fori_loop(0, 5, list_step, 0)

    own_copy = pltpu.make_async_copy(sums.at[pl.ds(PAD, BASE_X)], own_out, copies.at[0])
    own_copy.start()

    outgoing = []
    for step, out, target in zip([STEPS[index] for index in AHEAD], outs, targets_out):
        base, rows, leads = place_of(*step)

        def narrow(lead, base=base, rows=rows, leads=leads, out=out):
            lanes = pl.ds(pl.multiple_of(lead * LANES, LANES), LANES)
            values = []
            for k in range(2):
                start = pl.multiple_of(PAD + base + k * leads * rows + lead * rows, 8)
                values.append(sums[pl.ds(start, rows), :])
            if rows == RIM:
                out[:, lanes] = jnp.concatenate(values, 0).astype(out.dtype)
            else:
                for k in range(2):
                    out[k, :, lanes] = values[k].astype(out.dtype)

        for_leads(leads, narrow)
        copy = pltpu.make_async_copy(out, target, copies.at[11 + len(outgoing)])
        copy.start()
        outgoing.append(copy)

    slab = SIDE - 16

    def deposit(step_x, step_y, k, base, rows, leads):
        holder_x = lax.rem(here_x + step_x + mesh_x, mesh_x)
        holder_y = lax.rem(here_y + step_y + mesh_y, mesh_y)
        orbit = (holder_x * mesh_y + holder_y) * 2 + k
        at_x = anchors[0, orbit] - holder_x * slab
        at_y = anchors[1, orbit] - holder_y * slab
        at_z = anchors[2, orbit]
        row = at_x + step_x * slab + GRID_PAD + jnp.where(step_x < 0, LOW, 0)
        column = at_y + step_y * slab + GRID_PAD + jnp.where(step_y < 0, LOW, 0)
        start = column * GRID_ROWS + row
        from_lane = lax.broadcasted_iota(jnp.int32, (LANES, LANES), 0)
        apart = lax.broadcasted_iota(jnp.int32, (LANES, LANES), 1) - from_lane - at_z
        low = one_where((from_lane < SIDE) & (apart == 0))
        high = one_where((from_lane >= SIDE) & (apart == -SIDE))
        place[:, :LANES] = low
        place[:, LANES:] = high
        block = 16
        for first in range(0, leads, block):
            size = min(block, leads - first)
            value = window[pl.ds(pl.multiple_of(PAD + base + first * rows, 8), size * rows), :]
            placed = jnp.dot(value.astype(jnp.bfloat16), place[...], preferred_element_type=jnp.float32)
            for j in range(size):
                for odd_column in (0, 1):
                    at = pl.ds(start + (2 * (first + j) + odd_column) * GRID_ROWS, rows)
                    part = placed[j * rows : (j + 1) * rows, odd_column * LANES : (odd_column + 1) * LANES]
                    grid[at, :] = grid[at, :] + part * part

    for k in range(2):
        deposit(0, 0, k, k * HALF * SIDE, SIDE, HALF)

    def deposit_x(index, carry):
        deposit(2 * (index // 2) - 1, 0, lax.rem(index, 2), BASE_X + index * (HALF * RIM), RIM, HALF)
        return carry

    def deposit_y(index, carry):
        deposit(
            0, 2 * (index // 2) - 1, lax.rem(index, 2), BASE_Y + index * (RIM_LEADS * SIDE), SIDE, RIM_LEADS
        )
        return carry

    def deposit_corner(index, carry):
        deposit(
            2 * (index // 4) - 1,
            2 * lax.rem(index // 2, 2) - 1,
            lax.rem(index, 2),
            BASE_C + index * (RIM_LEADS * RIM),
            RIM,
            RIM_LEADS,
        )
        return carry

    lax.fori_loop(0, 4, deposit_x, 0)
    lax.fori_loop(0, 4, deposit_y, 0)
    lax.fori_loop(0, 8, deposit_corner, 0)
    grid_copy = pltpu.make_async_copy(grid.at[pl.ds(GRID_PAD * GRID_ROWS, EDGE_ROWS)], grid_out, copies.at[1])
    grid_copy.start()
    for copy in [own_copy, *outgoing, grid_copy]:
        copy.wait()


GRID_PAD = 8
GRID_ROWS = 88
EDGE = SIDE - 16 + RIM
EDGE_ROWS = (EDGE + 1) * GRID_ROWS
hbm = pl.BlockSpec(memory_space=pl.ANY)
MESH = pl.DeviceIdType.MESH

smem = pl.BlockSpec(memory_space=pltpu.SMEM)
vmem = pl.BlockSpec(memory_space=pltpu.VMEM)


def pairs_call(mesh_x, mesh_y, flat_anchors, lists, pieces):
    term_shapes = [
        jax.ShapeDtypeStruct((BASE_X, LANES), jnp.float32),
        jax.ShapeDtypeStruct((EDGE_ROWS, LANES), jnp.float32),
    ] + [jax.ShapeDtypeStruct(pieces[index].shape, jnp.bfloat16) for index in AHEAD]

    def field(rows):
        return pltpu.VMEM((HALF + 2, rows, LANES), jnp.float32)

    return pl.pallas_call(
        functools.partial(pair_kernel, mesh_x, mesh_y),
        out_shape=term_shapes,
        in_specs=[smem] * 2 + [hbm] * 9,
        out_specs=[hbm] * 6,
        scratch_shapes=[
            pltpu.VMEM((WINDOW_ROWS + 2 * PAD, LANES), jnp.float32),
            pltpu.VMEM((WINDOW_ROWS + 2 * PAD, LANES), jnp.float32),
            pltpu.VMEM((2 * LANES, 2 * LANES), jnp.bfloat16),
            pltpu.VMEM((2 * LANES, LANES), jnp.bfloat16),
            pltpu.VMEM((2 * LANES, 2 * LANES), jnp.bfloat16),
            pltpu.VMEM((HALF, RIM, LANES), jnp.float32),
            field(RIM + 16),
            field(RIM + 16),
            field(RIM + 16),
            pltpu.VMEM((HALF, SIDE, LANES), jnp.float32),
            field(SIDE + 16),
            field(SIDE + 16),
            field(SIDE + 16),
            pltpu.VMEM((GRID_ROWS * GRID_ROWS, LANES), jnp.float32),
            pltpu.VMEM((LANES, 2 * LANES), jnp.bfloat16),
            pltpu.SemaphoreType.DMA((19,)),
        ]
        + [pltpu.VMEM(piece.shape, jnp.bfloat16) for piece in pieces]
        + [pltpu.VMEM(pieces[index].shape, jnp.bfloat16) for index in AHEAD],
        compiler_params=pltpu.CompilerParams(vmem_limit_bytes=64 * 1024 * 1024),
        cost_estimate=pl.CostEstimate(flops=40_000_000, bytes_accessed=8_000_000, transcendentals=0),
        name="pair_terms",
    )(flat_anchors, lists, *pieces)


def cube_root(value):
    inverse = jnp.exp(jnp.log(value) * (-1.0 / 3.0))
    inverse = inverse * (4.0 - value * inverse * inverse * inverse) * (1.0 / 3.0)
    return value * inverse * inverse


def greet(mesh_x, mesh_y, diagonal=False):
    here_x = lax.axis_index("gx")
    here_y = lax.axis_index("gy")
    left = (lax.rem(here_x + mesh_x - 1, mesh_x), here_y)
    right = (lax.rem(here_x + 1, mesh_x), here_y)
    below = (here_x, lax.rem(here_y + mesh_y - 1, mesh_y))
    above = (here_x, lax.rem(here_y + 1, mesh_y))
    barrier = pltpu.get_barrier_semaphore()
    neighbours = [left, right, below, above]
    if diagonal:
        neighbours += [(side[0], end[1]) for side in (left, right) for end in (below, above)]
    for neighbour in neighbours:
        pl.semaphore_signal(barrier, inc=1, device_id=neighbour, device_id_type=MESH)
    pl.semaphore_wait(barrier, len(neighbours))
    return left, right, below, above


def gather_kernel(mesh_x, mesh_y, count, pairs, own, core_source, *refs):
    outs = refs[:8]
    narrow_outs = refs[8:11]
    lists = refs[11]
    send_low, send_high, core, narrow_x, narrow_y, list_source, sent, landed, copies = refs[12:]
    slots = pairs.shape[1]
    list_source[...] = jnp.full(list_source.shape, count[0], jnp.int32)
    list_source[0:2, 0:slots] = pairs[...]
    core_copy = pltpu.make_async_copy(core_source, core, copies.at[3])
    core_copy.start()
    list_copy = pltpu.make_async_copy(list_source, lists.at[0], copies.at[4])
    list_copy.start()
    left, right, below, above = greet(mesh_x, mesh_y, diagonal=True)
    started = []

    def send(source, slot, device, target=None):
        copy = pltpu.make_async_remote_copy(
            src_ref=source,
            dst_ref=outs[slot] if target is None else target,
            send_sem=sent.at[slot],
            recv_sem=landed.at[slot],
            device_id=device,
            device_id_type=MESH,
        )
        copy.start()
        started.append(copy)
        return copy

    def prepare(lead):
        lanes = pl.ds(pl.multiple_of(lead * LANES, LANES), LANES)
        values = [own[k, :, lanes].astype(jnp.float32) for k in range(2)]
        send_low[:, lanes] = jnp.concatenate([value[:RIM] for value in values], 0).astype(jnp.bfloat16)
        send_high[:, lanes] = jnp.concatenate([value[LOW:] for value in values], 0).astype(jnp.bfloat16)

    for_leads(HALF, prepare)
    from_left = send(send_high, 0, right)
    from_right = send(send_low, 1, left)
    high = pl.ds(LOW * SIDE, RIM * SIDE)
    low = pl.ds(0, RIM * SIDE)
    send(own.at[:, :, high], 2, above)
    send(own.at[:, :, low], 3, below)
    for index, device in enumerate(((left[0], above[1]), left, (left[0], below[1]), below)):
        send(list_source, 8 + index, device, target=lists.at[1 + index])
    core_copy.wait()

    def narrow(row):
        narrow_x[row] = core[row].astype(jnp.bfloat16)
        narrow_y[row] = jnp.concatenate([core[2 * row, :RIM], core[2 * row + 1, :RIM]], 0).astype(jnp.bfloat16)

    for_leads(RIM, narrow)
    narrow_copies = [
        pltpu.make_async_copy(source, target, copies.at[index])
        for index, (source, target) in enumerate(
            zip((narrow_x, narrow_y, narrow_y.at[pl.ds(0, RIM // 2)]), narrow_outs)
        )
    ]
    for copy in narrow_copies:
        copy.start()
    from_left.wait_recv()
    send(outs[0].at[:, high], 4, above)
    send(outs[0].at[:, low], 5, below)
    from_right.wait_recv()
    send(outs[1].at[:, high], 6, above)
    send(outs[1].at[:, low], 7, below)
    for copy in started:
        copy.wait_send()
    for copy in started[2:]:
        copy.wait_recv()
    for copy in narrow_copies:
        copy.wait()
    list_copy.wait()


def return_kernel(mesh_x, mesh_y, anchors, *refs):
    side_source, column_terms = refs[:2]
    corner_terms = refs[2:4]
    action_out, potential_out = refs[11:13]
    landed_corners, out_side, send_right, out_column, right_terms = refs[13:18]
    loads = refs[18:25]
    density, core, core_x, core_y, core_xy, own, own_terms = loads
    potential, action, sent, landed, copies = refs[25:]
    here_x = lax.axis_index("gx")
    here_y = lax.axis_index("gy")
    incoming = [
        pltpu.make_async_copy(source, target, copies.at[index])
        for index, (source, target) in enumerate(zip(refs[4:11] + (side_source,), loads + (right_terms,)))
    ]
    for copy in incoming:
        copy.start()
    left, right, below, above = greet(mesh_x, mesh_y)

    def send(source, target, slot, device):
        copy = pltpu.make_async_remote_copy(
            src_ref=source,
            dst_ref=target,
            send_sem=sent.at[slot],
            recv_sem=landed.at[slot],
            device_id=device,
            device_id_type=MESH,
        )
        copy.start()
        return copy

    corners = [
        send(corner_terms[slot], landed_corners.at[slot], slot, device)
        for slot, device in enumerate((below, above))
    ]
    high = pl.ds(LOW * SIDE, RIM * SIDE)
    low = pl.ds(0, RIM * SIDE)
    middle = pl.ds(RIM * SIDE, (LOW - RIM) * SIDE)
    others = [send(side_source.at[:, middle], out_side.at[:, middle], 2, right)]
    for copy in incoming:
        copy.wait()
    slab = core.shape[0]

    def finish_at(row, column, core_part):
        at = pl.ds(column * GRID_ROWS + GRID_PAD + row, 8, stride=GRID_ROWS)
        value = -xc_factor * cube_root(density[at, :] + core_part)
        density[at, :] = value
        return value

    def own_rows(row):
        for column in range(0, slab, 8):
            potential[row, pl.ds(column, 8), :] = finish_at(row, column, core[row, pl.ds(column, 8), :])

    def right_rows(row):
        beside = core_x[row].astype(jnp.float32)
        for column in range(0, slab, 8):
            finish_at(slab + row, column, beside[column : column + 8])

    def above_rows(pair, source=core_y, beyond=0):
        part = source[pair].astype(jnp.float32)
        for j in range(2):
            for column in range(0, RIM, 8):
                start = j * RIM + column
                finish_at(beyond + 2 * pair + j, slab + column, part[start : start + 8])

    def corner_rows(pair):
        above_rows(pair, source=core_xy, beyond=slab)

    for_leads(slab, own_rows)
    others.append(send(column_terms, out_column, 3, above))
    potential_copy = pltpu.make_async_copy(potential, potential_out, copies.at[8])
    potential_copy.start()
    for_leads(RIM, right_rows)
    for corner, (first, columns) in enumerate(((LOW_LEADS, high), (0, low))):
        corners[corner].wait_recv()

        def merge(index, first=first, corner=corner):
            lanes = pl.ds(pl.multiple_of((index + first) * LANES, LANES), LANES)
            at = pl.ds(pl.multiple_of(index * LANES, LANES), LANES)
            value = right_terms[:, lanes].astype(jnp.float32) + landed_corners[corner, :, at].astype(jnp.float32)
            send_right[:, lanes] = value.astype(jnp.bfloat16)

        for_leads(RIM_LEADS, merge)
        others.append(send(send_right.at[:, columns], out_side.at[:, columns], 4 + corner, right))
    for_leads(slab // 2, above_rows)
    for_leads(RIM // 2, corner_rows)

    lane = lane_index(SIDE)
    orbit = (here_x * mesh_y + here_y) * 2
    for k in range(2):
        at_x = jnp.clip(anchors[0, orbit + k] - here_x * slab, 0, GRID_PAD - 1)
        at_y = jnp.clip(anchors[1, orbit + k] - here_y * slab, 0, GRID_PAD - 1)
        at_z = anchors[2, orbit + k]
        start = at_y * GRID_ROWS + at_x + GRID_PAD
        turn_low = lax.rem(LANES - at_z, LANES)
        turn_high = lax.rem(LANES + SIDE - at_z, LANES)

        def sample(lead, k=k, start=start, turn_low=turn_low, turn_high=turn_high):
            lanes = pl.ds(pl.multiple_of(lead * LANES, LANES), LANES)
            low = density[pl.ds(start + 2 * lead * GRID_ROWS, SIDE), :]
            high = density[pl.ds(start + (2 * lead + 1) * GRID_ROWS, SIDE), :]
            sampled = jnp.where(lane < SIDE, pltpu.roll(low, turn_low, 1), pltpu.roll(high, turn_high, 1))
            at = pl.ds(pl.multiple_of((k * HALF + lead) * SIDE, SIDE), SIDE)
            action[k, :, lanes] = sampled * own[k, :, lanes].astype(jnp.float32) - exx_share * own_terms[at, :]

        for_leads(HALF, sample)
    for copy in others:
        copy.wait_recv()

    def add_side(lead, column=False):
        lanes = pl.ds(pl.multiple_of(lead * LANES, LANES), LANES)
        rows = out_side[:, lanes].astype(jnp.float32)
        for k in range(2):
            terms = rows[k * RIM : (k + 1) * RIM]
            if column:
                beside = out_column[k, :, lanes].astype(jnp.float32)
                terms = terms + beside[:RIM]
                action[k, RIM:, lanes] = action[k, RIM:, lanes] - exx_share * beside[RIM:]
            action[k, :RIM, lanes] = action[k, :RIM, lanes] - exx_share * terms

    action_copies = []
    for first, last in ((0, RIM_LEADS), (RIM_LEADS, LOW_LEADS), (LOW_LEADS, HALF)):

        def part_step(index, first=first):
            add_side(index + first, column=first == 0)

        for_leads(last - first, part_step)
        columns = pl.ds(first * LANES, (last - first) * LANES)
        copy = pltpu.make_async_copy(
            action.at[:, :, columns], action_out.at[:, :, columns], copies.at[9 + len(action_copies)]
        )
        copy.start()
        action_copies.append(copy)
    for copy in corners + others:
        copy.wait_send()
    for copy in [*action_copies, potential_copy]:
        copy.wait()


def shape_of(dims, dtype=jnp.bfloat16):
    return jax.ShapeDtypeStruct(dims, dtype)


def local(orbitals, anchors, pair_list, pair_count, core_density):
    mesh_x = lax.axis_size("gx")
    mesh_y = lax.axis_size("gy")
    own = orbitals[0, 0]
    flat_anchors = anchors.T
    flat_pairs = pair_list[0, 0].T
    flat_count = pair_count.reshape(-1)
    list_shape = (8, LANES)
    side_shape = shape_of((2 * RIM, FLAT))
    column_shape = shape_of((2, SIDE, RIM * SIDE))
    corner_shape = shape_of((2 * RIM, RIM * SIDE))
    around = [side_shape] * 2 + [column_shape] * 2 + [corner_shape] * 4

    core_shape = core_density.shape
    narrow_shapes = [
        (RIM, core_shape[1], LANES),
        (core_shape[0] // 2, 2 * RIM, LANES),
        (RIM // 2, 2 * RIM, LANES),
    ]
    grant = 64 * 1024 * 1024

    gathered = pl.pallas_call(
        functools.partial(gather_kernel, mesh_x, mesh_y),
        out_shape=around
        + [shape_of(dims) for dims in narrow_shapes]
        + [shape_of((5,) + list_shape, jnp.int32)],
        in_specs=[smem, vmem, vmem, hbm],
        out_specs=[hbm] * 12,
        scratch_shapes=[
            pltpu.VMEM(side_shape.shape, jnp.bfloat16),
            pltpu.VMEM(side_shape.shape, jnp.bfloat16),
            pltpu.VMEM(core_shape, jnp.float32),
            pltpu.VMEM(narrow_shapes[0], jnp.bfloat16),
            pltpu.VMEM(narrow_shapes[1], jnp.bfloat16),
            pltpu.VMEM(list_shape, jnp.int32),
            pltpu.SemaphoreType.DMA((12,)),
            pltpu.SemaphoreType.DMA((12,)),
            pltpu.SemaphoreType.DMA((5,)),
        ],
        compiler_params=pltpu.CompilerParams(
            collective_id=0, has_side_effects=True, vmem_limit_bytes=grant
        ),
        name="gather_rims",
    )(flat_count, flat_pairs, own, core_density)
    pieces = gathered[:8]

    back_x = [((i + 1) % mesh_x, i) for i in range(mesh_x)]
    back_y = [((i + 1) % mesh_y, i) for i in range(mesh_y)]
    back_xy = [
        ((i + 1) % mesh_x * mesh_y + (j + 1) % mesh_y, i * mesh_y + j)
        for i in range(mesh_x)
        for j in range(mesh_y)
    ]
    core_rims = [
        lax.ppermute(gathered[8], "gx", back_x),
        lax.ppermute(gathered[9], "gy", back_y),
        lax.ppermute(gathered[10], ("gx", "gy"), back_xy),
    ]

    terms = pairs_call(mesh_x, mesh_y, flat_anchors, gathered[11], [own] + list(pieces))
    grid_shape = terms[1].shape
    action, potential = pl.pallas_call(
        functools.partial(return_kernel, mesh_x, mesh_y),
        out_shape=[shape_of(own.shape, jnp.float32), shape_of(core_shape, jnp.float32)],
        in_specs=[smem] + [hbm] * 11,
        out_specs=[hbm] * 2,
        scratch_shapes=[
            pltpu.VMEM((2,) + corner_shape.shape, jnp.bfloat16),
            pltpu.VMEM(side_shape.shape, jnp.bfloat16),
            pltpu.VMEM(side_shape.shape, jnp.bfloat16),
            pltpu.VMEM(column_shape.shape, jnp.bfloat16),
            pltpu.VMEM(side_shape.shape, jnp.bfloat16),
            pltpu.VMEM(grid_shape, jnp.float32),
            pltpu.VMEM(core_shape, jnp.float32),
            pltpu.VMEM(narrow_shapes[0], jnp.bfloat16),
            pltpu.VMEM(narrow_shapes[1], jnp.bfloat16),
            pltpu.VMEM(narrow_shapes[2], jnp.bfloat16),
            pltpu.VMEM(own.shape, jnp.bfloat16),
            pltpu.VMEM((BASE_X, LANES), jnp.float32),
            pltpu.VMEM(core_shape, jnp.float32),
            pltpu.VMEM(own.shape, jnp.float32),
            pltpu.SemaphoreType.DMA((6,)),
            pltpu.SemaphoreType.DMA((6,)),
            pltpu.SemaphoreType.DMA((13,)),
        ],
        compiler_params=pltpu.CompilerParams(
            collective_id=1, has_side_effects=True, vmem_limit_bytes=grant
        ),
        name="return_terms",
    )(flat_anchors, *terms[2:], terms[1], core_density, *core_rims, own, terms[0])
    return (action.reshape(orbitals.shape), potential)


def solution(mesh):
    placed = (
        P("gx", "gy", None, None, None),
        P(),
        P("gx", "gy", None, None),
        P("gx", "gy"),
        P("gx", "gy", None),
    )
    return jax.shard_map(
        local,
        mesh=mesh,
        in_specs=placed,
        out_specs=(P("gx", "gy", None, None, None), P("gx", "gy", None)),
        check_vma=False,
    )
```

```python
import functools
import math

import jax
import jax.numpy as jnp
from jax import lax
from jax.experimental import pallas as pl
from jax.experimental.pallas import tpu as pltpu
from jax.sharding import PartitionSpec as P

SWEEPS = 4
SIDE = 64
HALF = SIDE // 2
FLAT = SIDE * SIDE
RIM = 24
LOW = SIDE - RIM
RIM_LEADS = RIM // 2
LOW_LEADS = LOW // 2
LANES = 128
PAD = 512
CHUNKS = [(False, False, 32), (True, False, 32), (False, True, 12), (True, True, 12)]

screen_mass = 0.25
coupling = 2.0 * math.pi
exx_share = 0.25
xc_factor = (3.0 / math.pi) ** (1.0 / 3.0)

AHEAD = [2, 4, 7, 8]
BASE_X = 2 * HALF * SIDE
BASE_Y = BASE_X + 4 * HALF * RIM
BASE_C = BASE_Y + 4 * RIM_LEADS * SIDE
WINDOW_ROWS = BASE_C + 8 * RIM_LEADS * RIM
STEPS = [(0, 0), (-1, 0), (1, 0), (0, -1), (0, 1), (-1, -1), (-1, 1), (1, -1), (1, 1)]


def place_of(step_x, step_y):
    rows = SIDE if step_x == 0 else RIM
    leads = HALF if step_y == 0 else RIM_LEADS
    if step_x == 0 and step_y == 0:
        base = 0
    elif step_y == 0:
        base = BASE_X + (2 * HALF * RIM if step_x > 0 else 0)
    elif step_x == 0:
        base = BASE_Y + (2 * RIM_LEADS * SIDE if step_y > 0 else 0)
    else:
        base = BASE_C + ((2 if step_x > 0 else 0) + (1 if step_y > 0 else 0)) * 2 * RIM_LEADS * RIM
    return base, rows, leads


def sweep_weights(sweep_count):
    return [
        1.0 / (1.0 + 0.7 * math.cos(math.pi * (2 * order + 1) / (2 * sweep_count)))
        for order in range(sweep_count)
    ]


def lane_index(rows):
    return lax.broadcasted_iota(jnp.int32, (rows, LANES), 1)


def one_where(condition):
    return jnp.where(condition, 1.0, 0.0).astype(jnp.bfloat16)


def halves(value):
    upper = value.astype(jnp.bfloat16)
    lower = (value - upper.astype(jnp.float32)).astype(jnp.bfloat16)
    return jnp.concatenate([upper, lower], 1)


def for_leads(count, step):
    lax.fori_loop(0, count, lambda index, _: (step(index), 0)[1], 0)


def pair_kernel(mesh_x, mesh_y, anchors, lists, *refs):
    sources = refs[:9]
    own_out, grid_out = refs[9:11]
    targets_out = refs[11:15]
    (
        window,
        sums,
        near,
        turn_in,
        turn_out,
        moved3,
        source3,
        even3,
        odd3,
        moved8,
        source8,
        even8,
        odd8,
        grid,
        place,
        copies,
    ) = refs[15:31]
    pieces = refs[31:40]
    outs = refs[40:44]
    here_x = lax.axis_index("gx")
    here_y = lax.axis_index("gy")
    span_x = mesh_x * (SIDE - 16)
    span_y = mesh_y * (SIDE - 16)

    incoming = [
        pltpu.make_async_copy(source, piece, copies.at[2 + index])
        for index, (source, piece) in enumerate(zip(sources, pieces))
    ]
    for copy in incoming:
        copy.start()
    zeros64 = jnp.zeros((SIDE, LANES), jnp.float32)

    def clear_sums(lead):
        sums[pl.ds(pl.multiple_of(lead * SIDE, SIDE), SIDE), :] = zeros64

    for_leads((WINDOW_ROWS + 2 * PAD) // SIDE, clear_sums)

    def clear_ends(lead):
        for start in (0, PAD + WINDOW_ROWS):
            window[pl.ds(pl.multiple_of(start + lead * SIDE, SIDE), SIDE), :] = zeros64

    for_leads(PAD // SIDE, clear_ends)

    for field in (source3, even3, odd3, source8, even8, odd8):
        rows = field.shape[1]
        field[0] = jnp.zeros((rows, LANES), jnp.float32)

        def clear_edge(lead, field=field, rows=rows):
            edge = jnp.zeros((8, LANES), jnp.float32)
            field[lead, pl.ds(0, 8), :] = edge
            field[lead, pl.ds(rows - 8, 8), :] = edge

        for_leads(HALF + 2, clear_edge)

    from_lane = lax.broadcasted_iota(jnp.int32, (LANES, LANES), 0)
    to_lane = lax.broadcasted_iota(jnp.int32, (LANES, LANES), 1)
    swap = jnp.abs(to_lane - from_lane) == SIDE
    step = (jnp.abs(to_lane - from_lane) == 1) & ((to_lane < SIDE) == (from_lane < SIDE))
    for start in (0, LANES):
        near[start : start + LANES, :LANES] = one_where(step | swap)
        near[start : start + LANES, LANES:] = one_where(swap)

    def clear_grid(lead):
        start = pl.multiple_of(lead * GRID_ROWS, 8)
        grid[pl.ds(start, GRID_ROWS), :] = jnp.zeros((GRID_ROWS, LANES), jnp.float32)

    for_leads(GRID_ROWS, clear_grid)

    for (step_x, step_y), piece, copy in zip(STEPS, pieces, incoming):
        base, rows, leads = place_of(step_x, step_y)

        def widen(lead, base=base, rows=rows, leads=leads, piece=piece):
            lanes = pl.ds(pl.multiple_of(lead * LANES, LANES), LANES)
            if rows == RIM:
                both = piece[:, lanes].astype(jnp.float32)
            for k in range(2):
                start = pl.multiple_of(PAD + base + k * leads * rows + lead * rows, 8)
                if rows == RIM:
                    value = both[k * RIM : (k + 1) * RIM]
                else:
                    value = piece[k, :, lanes].astype(jnp.float32)
                window[pl.ds(start, rows), :] = value

        copy.wait()
        for_leads(leads, widen)

    weights = sweep_weights(SWEEPS)
    diagonal = 6.0 + screen_mass
    scale = [weight / diagonal for weight in weights]
    keep = [(1.0 - weight) / part for weight, part in zip(weights, scale)]
    total_scale = coupling * scale[0] * scale[1] * scale[2] * scale[3]

    def slot_of(offset_x, offset_y, k):
        plus_x = jnp.where(offset_x > 0, 1, 0)
        plus_y = jnp.where(offset_y > 0, 1, 0)
        rows = jnp.where(offset_x != 0, RIM, SIDE)
        leads = jnp.where(offset_y != 0, RIM_LEADS, HALF)
        base = jnp.where(
            offset_x != 0,
            jnp.where(
                offset_y != 0,
                BASE_C + (2 * plus_x + plus_y) * (2 * RIM_LEADS * RIM),
                BASE_X + plus_x * (2 * HALF * RIM),
            ),
            jnp.where(offset_y != 0, BASE_Y + plus_y * (2 * RIM_LEADS * SIDE), 0),
        )
        origin_x = jnp.where(offset_x < 0, LOW, 0)
        origin_lead = jnp.where(offset_y < 0, LOW_LEADS, 0)
        return PAD + base + k * leads * rows, rows, origin_x, origin_lead

    def pair_step(source, slot, carry):
        from_x = jnp.where((source >= 1) & (source <= 3), 1, 0)
        from_y = jnp.where(source == 1, -1, jnp.where(source >= 3, 1, 0))
        first = lists[source, 0, slot]
        second = lists[source, 1, slot]
        holder = lax.div(second, 2)
        to_x = lax.rem(lax.div(holder, mesh_y) - here_x + 1 + mesh_x, mesh_x) - 1
        to_y = lax.rem(lax.rem(holder, mesh_y) - here_y + 1 + mesh_y, mesh_y) - 1
        is_own = (to_x == 0) & (to_y == 0)
        ahead = (to_x == 1) | ((to_x == 0) & (to_y == 1))
        mine = is_own | (ahead & (source == 0))
        pl.when(mine)(functools.partial(pair_work, first, second, from_x, from_y, to_x, to_y))
        return carry

    def pair_work(first, second, from_x, from_y, to_x, to_y):
        step_x = to_x - from_x
        step_y = to_y - from_y
        shift_x = anchors[0, second] - anchors[0, first]
        shift_y = anchors[1, second] - anchors[1, first]
        shift_z = anchors[2, second] - anchors[2, first]
        shift_x = shift_x + jnp.where(shift_x < -(span_x // 2), span_x, 0) - jnp.where(
            shift_x >= span_x // 2, span_x, 0
        )
        shift_y = shift_y + jnp.where(shift_y < -(span_y // 2), span_y, 0) - jnp.where(
            shift_y >= span_y // 2, span_y, 0
        )
        half_y = lax.shift_right_arithmetic(shift_y, 1)
        odd_y = shift_y - 2 * half_y
        side_x = step_x != 0
        side_y = step_y != 0
        start_x = jnp.where(step_x > 0, LOW, 0)
        start_lead = jnp.where(step_y > 0, LOW_LEADS, 0)
        near_base, near_stride, near_x, near_lead = slot_of(from_x, from_y, lax.rem(first, 2))
        far_base, far_stride, far_x, far_lead = slot_of(to_x, to_y, lax.rem(second, 2))
        near_start = near_base + (start_lead - near_lead) * near_stride + start_x - near_x
        far_start = (
            far_base + (start_lead - half_y - far_lead) * far_stride + start_x - shift_x - far_x
        )
        from_lane = lax.broadcasted_iota(jnp.int32, (LANES, LANES), 0)
        to_lane = lax.broadcasted_iota(jnp.int32, (LANES, LANES), 1)
        apart = to_lane - from_lane - shift_z
        depth = lax.rem(to_lane, SIDE) - shift_z
        valid = (depth >= 0) & (depth < SIDE)
        same = valid & (apart == SIDE * odd_y)
        other = valid & (apart == -SIDE) & (odd_y == 1)
        turn_in[:LANES] = one_where(same)
        turn_in[LANES:] = one_where(other)
        from_lane, to_lane = to_lane, from_lane
        apart = to_lane - from_lane - shift_z
        depth = lax.rem(to_lane, SIDE) - shift_z
        valid = (depth >= 0) & (depth < SIDE)
        same = one_where(valid & (apart == SIDE * odd_y))
        other = one_where(valid & (apart == -SIDE) & (odd_y == 1))
        turn_out[:LANES, :LANES] = same
        turn_out[LANES:, :LANES] = same
        turn_out[:LANES, LANES:] = other
        turn_out[LANES:, LANES:] = other

        def run(tiles, leads, chunk, moved, source, even, odd):
            rows = tiles * 8
            inner = pl.ds(8, rows)
            lane = lane_index(rows)
            upper = lane >= SIDE
            row = lax.broadcasted_iota(jnp.int32, (rows, LANES), 0) + start_x
            column_part = jnp.where(upper, 1, 0) - shift_y
            inside_x = (row >= shift_x) & (row < SIDE + shift_x)

            def inside(lead):
                column = column_part + 2 * lead
                return inside_x & (column >= 0) & (column < SIDE)

            def far_rows(lead):
                return pl.ds(far_start + lead * far_stride, rows)

            def own_rows(lead):
                return pl.ds(pl.multiple_of(near_start + lead * near_stride, 8), rows)

            def part(value, index):
                return value[index * rows : (index + 1) * rows]

            def build(index):
                lead = index * chunk
                loads = [window[far_rows(lead + j), :] for j in range(-1, chunk)]
                now = jnp.concatenate(loads[1:], 0).astype(jnp.bfloat16)
                before = jnp.concatenate(loads[:-1], 0).astype(jnp.bfloat16)
                turned = jnp.dot(
                    jnp.concatenate([now, before], 1), turn_in[...], preferred_element_type=jnp.float32
                )
                for j in range(chunk):
                    piece = jnp.where(inside(start_lead + lead + j), part(turned, j), 0.0)
                    moved[lead + j] = piece
                    source[lead + j + 1, inner, :] = piece * window[own_rows(lead + j), :]

            def near_fields(field, lead):
                values = [field[lead + j, inner, :] for j in range(chunk + 2)]
                product = jnp.dot(
                    halves(jnp.concatenate(values, 0)), near[...], preferred_element_type=jnp.float32
                )
                for j in range(chunk):
                    across = jnp.where(
                        upper, part(product, j + 2)[:, LANES:], part(product, j)[:, LANES:]
                    )
                    beside = field[lead + j + 1, pl.ds(7, rows), :] + field[lead + j + 1, pl.ds(9, rows), :]
                    yield values[j + 1], (part(product, j + 1)[:, :LANES] + across) + beside

            def sweep(old, new, own_part, source_part):
                def body(index):
                    lead = index * chunk
                    for j, (here, near_sum) in enumerate(near_fields(old, lead)):
                        value = own_part * here + near_sum
                        if source_part is not None:
                            value = value + source_part * source[lead + j + 1, inner, :]
                        new[lead + j + 1, inner, :] = value

                return body

            def finish(index):
                lead = index * chunk
                back = []
                for j, (here, near_sum) in enumerate(near_fields(odd, lead)):
                    value = keep[3] * here + near_sum
                    value = value + (1.0 / (scale[0] * scale[1] * scale[2])) * source[lead + j + 1, inner, :]
                    value = value * total_scale
                    sums[own_rows(lead + j), :] = sums[own_rows(lead + j), :] + value * moved[lead + j]
                    back.append(
                        jnp.where(inside(start_lead + lead + j), value * window[own_rows(lead + j), :], 0.0)
                    )
                turned = jnp.dot(
                    halves(jnp.concatenate(back, 0)), turn_out[...], preferred_element_type=jnp.float32
                )
                targets = [sums[far_rows(lead + j), :] for j in range(-1, chunk)]
                for j in range(-1, chunk):
                    total = targets[j + 1]
                    if j >= 0:
                        total = total + part(turned, j)[:, :LANES]
                    if j + 1 < chunk:
                        total = total + part(turned, j + 1)[:, LANES:]
                    targets[j + 1] = total
                for j in range(-1, chunk):
                    sums[far_rows(lead + j), :] = targets[j + 1]

            edge = jnp.zeros((rows, LANES), jnp.float32)
            for field in (source, even, odd):
                field[leads + 1, inner, :] = edge
            chunks = leads // chunk
            for_leads(chunks, build)
            for_leads(chunks, sweep(source, even, keep[1] + 1.0 / scale[0], None))
            for_leads(chunks, sweep(even, odd, keep[2], 1.0 / (scale[0] * scale[1])))
            for_leads(chunks, finish)

        for has_x, has_y, chunk in CHUNKS:
            narrow = side_x if has_x else jnp.logical_not(side_x)
            narrow = narrow & (side_y if has_y else jnp.logical_not(side_y))
            fields = (moved3, source3, even3, odd3) if has_x else (moved8, source8, even8, odd8)

            @pl.when(narrow)
            def _(has_x=has_x, has_y=has_y, chunk=chunk, fields=fields):
                run(
                    (RIM if has_x else SIDE) // 8,
                    RIM_LEADS if has_y else HALF,
                    chunk,
                    *fields,
                )

    def list_step(source, carry):
        return lax.fori_loop(0, lists[source, 2, 0], functools.partial(pair_step, source), carry)

    lax.fori_loop(0, 5, list_step, 0)

    own_copy = pltpu.make_async_copy(sums.at[pl.ds(PAD, BASE_X)], own_out, copies.at[0])
    own_copy.start()

    outgoing = []
    for step, out, target in zip([STEPS[index] for index in AHEAD], outs, targets_out):
        base, rows, leads = place_of(*step)

        def narrow(lead, base=base, rows=rows, leads=leads, out=out):
            lanes = pl.ds(pl.multiple_of(lead * LANES, LANES), LANES)
            values = []
            for k in range(2):
                start = pl.multiple_of(PAD + base + k * leads * rows + lead * rows, 8)
                values.append(sums[pl.ds(start, rows), :])
            if rows == RIM:
                out[:, lanes] = jnp.concatenate(values, 0).astype(out.dtype)
            else:
                for k in range(2):
                    out[k, :, lanes] = values[k].astype(out.dtype)

        for_leads(leads, narrow)
        copy = pltpu.make_async_copy(out, target, copies.at[11 + len(outgoing)])
        copy.start()
        outgoing.append(copy)

    slab = SIDE - 16

    def deposit(step_x, step_y, k, base, rows, leads):
        holder_x = lax.rem(here_x + step_x + mesh_x, mesh_x)
        holder_y = lax.rem(here_y + step_y + mesh_y, mesh_y)
        orbit = (holder_x * mesh_y + holder_y) * 2 + k
        at_x = anchors[0, orbit] - holder_x * slab
        at_y = anchors[1, orbit] - holder_y * slab
        at_z = anchors[2, orbit]
        row = at_x + step_x * slab + GRID_PAD + jnp.where(step_x < 0, LOW, 0)
        column = at_y + step_y * slab + GRID_PAD + jnp.where(step_y < 0, LOW, 0)
        start = column * GRID_ROWS + row
        from_lane = lax.broadcasted_iota(jnp.int32, (LANES, LANES), 0)
        apart = lax.broadcasted_iota(jnp.int32, (LANES, LANES), 1) - from_lane - at_z
        low = one_where((from_lane < SIDE) & (apart == 0))
        high = one_where((from_lane >= SIDE) & (apart == -SIDE))
        place[:, :LANES] = low
        place[:, LANES:] = high
        block = 16
        for first in range(0, leads, block):
            size = min(block, leads - first)
            value = window[pl.ds(pl.multiple_of(PAD + base + first * rows, 8), size * rows), :]
            placed = jnp.dot(value.astype(jnp.bfloat16), place[...], preferred_element_type=jnp.float32)
            for j in range(size):
                for odd_column in (0, 1):
                    at = pl.ds(start + (2 * (first + j) + odd_column) * GRID_ROWS, rows)
                    part = placed[j * rows : (j + 1) * rows, odd_column * LANES : (odd_column + 1) * LANES]
                    grid[at, :] = grid[at, :] + part * part

    for k in range(2):
        deposit(0, 0, k, k * HALF * SIDE, SIDE, HALF)

    def deposit_x(index, carry):
        deposit(2 * (index // 2) - 1, 0, lax.rem(index, 2), BASE_X + index * (HALF * RIM), RIM, HALF)
        return carry

    def deposit_y(index, carry):
        deposit(
            0, 2 * (index // 2) - 1, lax.rem(index, 2), BASE_Y + index * (RIM_LEADS * SIDE), SIDE, RIM_LEADS
        )
        return carry

    def deposit_corner(index, carry):
        deposit(
            2 * (index // 4) - 1,
            2 * lax.rem(index // 2, 2) - 1,
            lax.rem(index, 2),
            BASE_C + index * (RIM_LEADS * RIM),
            RIM,
            RIM_LEADS,
        )
        return carry

    lax.fori_loop(0, 4, deposit_x, 0)
    lax.fori_loop(0, 4, deposit_y, 0)
    lax.fori_loop(0, 8, deposit_corner, 0)
    grid_copy = pltpu.make_async_copy(grid.at[pl.ds(GRID_PAD * GRID_ROWS, EDGE_ROWS)], grid_out, copies.at[1])
    grid_copy.start()
    for copy in [own_copy, *outgoing, grid_copy]:
        copy.wait()


GRID_PAD = 8
GRID_ROWS = 88
EDGE = SIDE - 16 + RIM
EDGE_ROWS = (EDGE + 1) * GRID_ROWS
hbm = pl.BlockSpec(memory_space=pl.ANY)
MESH = pl.DeviceIdType.MESH

smem = pl.BlockSpec(memory_space=pltpu.SMEM)
vmem = pl.BlockSpec(memory_space=pltpu.VMEM)


def pairs_call(mesh_x, mesh_y, flat_anchors, lists, pieces):
    term_shapes = [
        jax.ShapeDtypeStruct((BASE_X, LANES), jnp.float32),
        jax.ShapeDtypeStruct((EDGE_ROWS, LANES), jnp.float32),
    ] + [jax.ShapeDtypeStruct(pieces[index].shape, jnp.bfloat16) for index in AHEAD]

    def field(rows):
        return pltpu.VMEM((HALF + 2, rows, LANES), jnp.float32)

    return pl.pallas_call(
        functools.partial(pair_kernel, mesh_x, mesh_y),
        out_shape=term_shapes,
        in_specs=[smem] * 2 + [hbm] * 9,
        out_specs=[hbm] * 6,
        scratch_shapes=[
            pltpu.VMEM((WINDOW_ROWS + 2 * PAD, LANES), jnp.float32),
            pltpu.VMEM((WINDOW_ROWS + 2 * PAD, LANES), jnp.float32),
            pltpu.VMEM((2 * LANES, 2 * LANES), jnp.bfloat16),
            pltpu.VMEM((2 * LANES, LANES), jnp.bfloat16),
            pltpu.VMEM((2 * LANES, 2 * LANES), jnp.bfloat16),
            pltpu.VMEM((HALF, RIM, LANES), jnp.float32),
            field(RIM + 16),
            field(RIM + 16),
            field(RIM + 16),
            pltpu.VMEM((HALF, SIDE, LANES), jnp.float32),
            field(SIDE + 16),
            field(SIDE + 16),
            field(SIDE + 16),
            pltpu.VMEM((GRID_ROWS * GRID_ROWS, LANES), jnp.float32),
            pltpu.VMEM((LANES, 2 * LANES), jnp.bfloat16),
            pltpu.SemaphoreType.DMA((19,)),
        ]
        + [pltpu.VMEM(piece.shape, jnp.bfloat16) for piece in pieces]
        + [pltpu.VMEM(pieces[index].shape, jnp.bfloat16) for index in AHEAD],
        compiler_params=pltpu.CompilerParams(vmem_limit_bytes=64 * 1024 * 1024),
        cost_estimate=pl.CostEstimate(flops=40_000_000, bytes_accessed=8_000_000, transcendentals=0),
        name="pair_terms",
    )(flat_anchors, lists, *pieces)


def cube_root(value):
    inverse = jnp.exp(jnp.log(value) * (-1.0 / 3.0))
    inverse = inverse * (4.0 - value * inverse * inverse * inverse) * (1.0 / 3.0)
    return value * inverse * inverse


def greet(mesh_x, mesh_y, diagonal=False):
    here_x = lax.axis_index("gx")
    here_y = lax.axis_index("gy")
    left = (lax.rem(here_x + mesh_x - 1, mesh_x), here_y)
    right = (lax.rem(here_x + 1, mesh_x), here_y)
    below = (here_x, lax.rem(here_y + mesh_y - 1, mesh_y))
    above = (here_x, lax.rem(here_y + 1, mesh_y))
    barrier = pltpu.get_barrier_semaphore()
    neighbours = [left, right, below, above]
    if diagonal:
        neighbours += [(side[0], end[1]) for side in (left, right) for end in (below, above)]
    for neighbour in neighbours:
        pl.semaphore_signal(barrier, inc=1, device_id=neighbour, device_id_type=MESH)
    pl.semaphore_wait(barrier, len(neighbours))
    return left, right, below, above


def gather_kernel(mesh_x, mesh_y, count, pairs, own, core_source, *refs):
    outs = refs[:8]
    narrow_outs = refs[8:11]
    lists = refs[11]
    send_low, send_high, core, narrow_x, narrow_y, list_source, sent, landed, copies = refs[12:]
    slots = pairs.shape[1]
    list_source[...] = jnp.full(list_source.shape, count[0], jnp.int32)
    list_source[0:2, 0:slots] = pairs[...]
    core_copy = pltpu.make_async_copy(core_source, core, copies.at[3])
    core_copy.start()
    list_copy = pltpu.make_async_copy(list_source, lists.at[0], copies.at[4])
    list_copy.start()
    left, right, below, above = greet(mesh_x, mesh_y, diagonal=True)
    started = []

    def send(source, slot, device, target=None):
        copy = pltpu.make_async_remote_copy(
            src_ref=source,
            dst_ref=outs[slot] if target is None else target,
            send_sem=sent.at[slot],
            recv_sem=landed.at[slot],
            device_id=device,
            device_id_type=MESH,
        )
        copy.start()
        started.append(copy)
        return copy

    def prepare(lead):
        lanes = pl.ds(pl.multiple_of(lead * LANES, LANES), LANES)
        values = [own[k, :, lanes].astype(jnp.float32) for k in range(2)]
        send_low[:, lanes] = jnp.concatenate([value[:RIM] for value in values], 0).astype(jnp.bfloat16)
        send_high[:, lanes] = jnp.concatenate([value[LOW:] for value in values], 0).astype(jnp.bfloat16)

    for_leads(HALF, prepare)
    from_left = send(send_high, 0, right)
    from_right = send(send_low, 1, left)
    high = pl.ds(LOW * SIDE, RIM * SIDE)
    low = pl.ds(0, RIM * SIDE)
    send(own.at[:, :, high], 2, above)
    send(own.at[:, :, low], 3, below)
    for index, device in enumerate(((left[0], above[1]), left, (left[0], below[1]), below)):
        send(list_source, 8 + index, device, target=lists.at[1 + index])
    core_copy.wait()

    def narrow(row):
        narrow_x[row] = core[row].astype(jnp.bfloat16)
        narrow_y[row] = jnp.concatenate([core[2 * row, :RIM], core[2 * row + 1, :RIM]], 0).astype(jnp.bfloat16)

    for_leads(RIM, narrow)
    narrow_copies = [
        pltpu.make_async_copy(source, target, copies.at[index])
        for index, (source, target) in enumerate(
            zip((narrow_x, narrow_y, narrow_y.at[pl.ds(0, RIM // 2)]), narrow_outs)
        )
    ]
    for copy in narrow_copies:
        copy.start()
    from_left.wait_recv()
    send(outs[0].at[:, high], 4, above)
    send(outs[0].at[:, low], 5, below)
    from_right.wait_recv()
    send(outs[1].at[:, high], 6, above)
    send(outs[1].at[:, low], 7, below)
    for copy in started:
        copy.wait_send()
    for copy in started[2:]:
        copy.wait_recv()
    for copy in narrow_copies:
        copy.wait()
    list_copy.wait()


def return_kernel(mesh_x, mesh_y, anchors, *refs):
    side_source, column_terms = refs[:2]
    corner_terms = refs[2:4]
    action_out, potential_out = refs[11:13]
    landed_corners, out_side, send_right, out_column, right_terms = refs[13:18]
    loads = refs[18:25]
    density, core, core_x, core_y, core_xy, own, own_terms = loads
    potential, action, sent, landed, copies = refs[25:]
    here_x = lax.axis_index("gx")
    here_y = lax.axis_index("gy")
    incoming = [
        pltpu.make_async_copy(source, target, copies.at[index])
        for index, (source, target) in enumerate(zip((side_source,) + refs[4:11], (right_terms,) + loads))
    ]
    for copy in incoming:
        copy.start()
    left, right, below, above = greet(mesh_x, mesh_y)

    def send(source, target, slot, device):
        copy = pltpu.make_async_remote_copy(
            src_ref=source,
            dst_ref=target,
            send_sem=sent.at[slot],
            recv_sem=landed.at[slot],
            device_id=device,
            device_id_type=MESH,
        )
        copy.start()
        return copy

    corners = [
        send(corner_terms[slot], landed_corners.at[slot], slot, device)
        for slot, device in enumerate((below, above))
    ]
    high = pl.ds(LOW * SIDE, RIM * SIDE)
    low = pl.ds(0, RIM * SIDE)
    middle = pl.ds(RIM * SIDE, (LOW - RIM) * SIDE)
    others = [
        send(side_source.at[:, middle], out_side.at[:, middle], 2, right),
        send(column_terms, out_column, 3, above),
    ]
    for copy in incoming[:3]:
        copy.wait()
    slab = core.shape[0]

    def finish_at(row, column, core_part):
        at = pl.ds(column * GRID_ROWS + GRID_PAD + row, 8, stride=GRID_ROWS)
        value = -xc_factor * cube_root(density[at, :] + core_part)
        density[at, :] = value
        return value

    def own_rows(row):
        for column in range(0, slab, 8):
            potential[row, pl.ds(column, 8), :] = finish_at(row, column, core[row, pl.ds(column, 8), :])

    def right_rows(row):
        beside = core_x[row].astype(jnp.float32)
        for column in range(0, slab, 8):
            finish_at(slab + row, column, beside[column : column + 8])

    def above_rows(pair, source=core_y, beyond=0):
        part = source[pair].astype(jnp.float32)
        for j in range(2):
            for column in range(0, RIM, 8):
                start = j * RIM + column
                finish_at(beyond + 2 * pair + j, slab + column, part[start : start + 8])

    def corner_rows(pair):
        above_rows(pair, source=core_xy, beyond=slab)

    for_leads(RIM // 2, own_rows)
    for corner, (first, columns) in enumerate(((LOW_LEADS, high), (0, low))):
        corners[corner].wait_recv()

        def merge(index, first=first, corner=corner):
            lanes = pl.ds(pl.multiple_of((index + first) * LANES, LANES), LANES)
            at = pl.ds(pl.multiple_of(index * LANES, LANES), LANES)
            value = right_terms[:, lanes].astype(jnp.float32) + landed_corners[corner, :, at].astype(jnp.float32)
            send_right[:, lanes] = value.astype(jnp.bfloat16)

        for_leads(RIM_LEADS, merge)
        others.append(send(send_right.at[:, columns], out_side.at[:, columns], 4 + corner, right))

    def later_rows(row):
        own_rows(row + RIM // 2)

    for_leads(slab - RIM // 2, later_rows)
    potential_copy = pltpu.make_async_copy(potential, potential_out, copies.at[8])
    potential_copy.start()
    for copy in incoming[3:]:
        copy.wait()
    for_leads(RIM, right_rows)
    for_leads(slab // 2, above_rows)
    for_leads(RIM // 2, corner_rows)

    lane = lane_index(SIDE)
    orbit = (here_x * mesh_y + here_y) * 2
    for k in range(2):
        at_x = jnp.clip(anchors[0, orbit + k] - here_x * slab, 0, GRID_PAD - 1)
        at_y = jnp.clip(anchors[1, orbit + k] - here_y * slab, 0, GRID_PAD - 1)
        at_z = anchors[2, orbit + k]
        start = at_y * GRID_ROWS + at_x + GRID_PAD
        turn_low = lax.rem(LANES - at_z, LANES)
        turn_high = lax.rem(LANES + SIDE - at_z, LANES)

        def sample(lead, k=k, start=start, turn_low=turn_low, turn_high=turn_high):
            lanes = pl.ds(pl.multiple_of(lead * LANES, LANES), LANES)
            low = density[pl.ds(start + 2 * lead * GRID_ROWS, SIDE), :]
            high = density[pl.ds(start + (2 * lead + 1) * GRID_ROWS, SIDE), :]
            sampled = jnp.where(lane < SIDE, pltpu.roll(low, turn_low, 1), pltpu.roll(high, turn_high, 1))
            at = pl.ds(pl.multiple_of((k * HALF + lead) * SIDE, SIDE), SIDE)
            action[k, :, lanes] = sampled * own[k, :, lanes].astype(jnp.float32) - exx_share * own_terms[at, :]

        for_leads(HALF, sample)
    for copy in others:
        copy.wait_recv()

    def add_side(lead, column=False):
        lanes = pl.ds(pl.multiple_of(lead * LANES, LANES), LANES)
        rows = out_side[:, lanes].astype(jnp.float32)
        for k in range(2):
            terms = rows[k * RIM : (k + 1) * RIM]
            if column:
                beside = out_column[k, :, lanes].astype(jnp.float32)
                terms = terms + beside[:RIM]
                action[k, RIM:, lanes] = action[k, RIM:, lanes] - exx_share * beside[RIM:]
            action[k, :RIM, lanes] = action[k, :RIM, lanes] - exx_share * terms

    action_copies = []
    for first, last in ((0, RIM_LEADS), (RIM_LEADS, LOW_LEADS), (LOW_LEADS, HALF)):

        def part_step(index, first=first):
            add_side(index + first, column=first == 0)

        for_leads(last - first, part_step)
        columns = pl.ds(first * LANES, (last - first) * LANES)
        copy = pltpu.make_async_copy(
            action.at[:, :, columns], action_out.at[:, :, columns], copies.at[9 + len(action_copies)]
        )
        copy.start()
        action_copies.append(copy)
    for copy in corners + others:
        copy.wait_send()
    for copy in [*action_copies, potential_copy]:
        copy.wait()


def shape_of(dims, dtype=jnp.bfloat16):
    return jax.ShapeDtypeStruct(dims, dtype)


def local(orbitals, anchors, pair_list, pair_count, core_density):
    mesh_x = lax.axis_size("gx")
    mesh_y = lax.axis_size("gy")
    own = orbitals[0, 0]
    flat_anchors = anchors.T
    flat_pairs = pair_list[0, 0].T
    flat_count = pair_count.reshape(-1)
    list_shape = (8, LANES)
    side_shape = shape_of((2 * RIM, FLAT))
    column_shape = shape_of((2, SIDE, RIM * SIDE))
    corner_shape = shape_of((2 * RIM, RIM * SIDE))
    around = [side_shape] * 2 + [column_shape] * 2 + [corner_shape] * 4

    core_shape = core_density.shape
    narrow_shapes = [
        (RIM, core_shape[1], LANES),
        (core_shape[0] // 2, 2 * RIM, LANES),
        (RIM // 2, 2 * RIM, LANES),
    ]
    grant = 64 * 1024 * 1024

    gathered = pl.pallas_call(
        functools.partial(gather_kernel, mesh_x, mesh_y),
        out_shape=around
        + [shape_of(dims) for dims in narrow_shapes]
        + [shape_of((5,) + list_shape, jnp.int32)],
        in_specs=[smem, vmem, vmem, hbm],
        out_specs=[hbm] * 12,
        scratch_shapes=[
            pltpu.VMEM(side_shape.shape, jnp.bfloat16),
            pltpu.VMEM(side_shape.shape, jnp.bfloat16),
            pltpu.VMEM(core_shape, jnp.float32),
            pltpu.VMEM(narrow_shapes[0], jnp.bfloat16),
            pltpu.VMEM(narrow_shapes[1], jnp.bfloat16),
            pltpu.VMEM(list_shape, jnp.int32),
            pltpu.SemaphoreType.DMA((12,)),
            pltpu.SemaphoreType.DMA((12,)),
            pltpu.SemaphoreType.DMA((5,)),
        ],
        compiler_params=pltpu.CompilerParams(
            collective_id=0, has_side_effects=True, vmem_limit_bytes=grant
        ),
        name="gather_rims",
    )(flat_count, flat_pairs, own, core_density)
    pieces = gathered[:8]

    back_x = [((i + 1) % mesh_x, i) for i in range(mesh_x)]
    back_y = [((i + 1) % mesh_y, i) for i in range(mesh_y)]
    back_xy = [
        ((i + 1) % mesh_x * mesh_y + (j + 1) % mesh_y, i * mesh_y + j)
        for i in range(mesh_x)
        for j in range(mesh_y)
    ]
    core_rims = [
        lax.ppermute(gathered[8], "gx", back_x),
        lax.ppermute(gathered[9], "gy", back_y),
        lax.ppermute(gathered[10], ("gx", "gy"), back_xy),
    ]

    terms = pairs_call(mesh_x, mesh_y, flat_anchors, gathered[11], [own] + list(pieces))
    grid_shape = terms[1].shape
    action, potential = pl.pallas_call(
        functools.partial(return_kernel, mesh_x, mesh_y),
        out_shape=[shape_of(own.shape, jnp.float32), shape_of(core_shape, jnp.float32)],
        in_specs=[smem] + [hbm] * 11,
        out_specs=[hbm] * 2,
        scratch_shapes=[
            pltpu.VMEM((2,) + corner_shape.shape, jnp.bfloat16),
            pltpu.VMEM(side_shape.shape, jnp.bfloat16),
            pltpu.VMEM(side_shape.shape, jnp.bfloat16),
            pltpu.VMEM(column_shape.shape, jnp.bfloat16),
            pltpu.VMEM(side_shape.shape, jnp.bfloat16),
            pltpu.VMEM(grid_shape, jnp.float32),
            pltpu.VMEM(core_shape, jnp.float32),
            pltpu.VMEM(narrow_shapes[0], jnp.bfloat16),
            pltpu.VMEM(narrow_shapes[1], jnp.bfloat16),
            pltpu.VMEM(narrow_shapes[2], jnp.bfloat16),
            pltpu.VMEM(own.shape, jnp.bfloat16),
            pltpu.VMEM((BASE_X, LANES), jnp.float32),
            pltpu.VMEM(core_shape, jnp.float32),
            pltpu.VMEM(own.shape, jnp.float32),
            pltpu.SemaphoreType.DMA((6,)),
            pltpu.SemaphoreType.DMA((6,)),
            pltpu.SemaphoreType.DMA((13,)),
        ],
        compiler_params=pltpu.CompilerParams(
            collective_id=1, has_side_effects=True, vmem_limit_bytes=grant
        ),
        name="return_terms",
    )(flat_anchors, *terms[2:], terms[1], core_density, *core_rims, own, terms[0])
    return (action.reshape(orbitals.shape), potential)


def solution(mesh):
    placed = (
        P("gx", "gy", None, None, None),
        P(),
        P("gx", "gy", None, None),
        P("gx", "gy"),
        P("gx", "gy", None),
    )
    return jax.shard_map(
        local,
        mesh=mesh,
        in_specs=placed,
        out_specs=(P("gx", "gy", None, None, None), P("gx", "gy", None)),
        check_vma=False,
    )
```
